32 devices in a mesh: dp: 8 (over z, x), seq: 4 (over y, core).
Axes of the slice: x: 2, y: 2, z: 4, core: 2. Of those that a mesh axis runs over, the one named last changes fastest.
Arguments:
- inputs: bfloat16 [8, 1024, 1280], P('dp', 'seq'), may hold values from -6 to 6
- lengths: int32 [8], P('dp'), may hold values from 256 to 1024, as said below
- cotangent: bfloat16 [8, 1024, 1280], P('dp', 'seq'), may hold values from -6 to 6
- gain_attn: bfloat16 [1280], P(('dp', 'seq')), may hold values from 0.099609375 to 1.8984375
- w_query: bfloat16 [1280, 1280], P(('dp', 'seq')), may hold values from -0.15625 to 0.15625
- bias_query: bfloat16 [1280], P(('dp', 'seq')), may hold values from -3 to 3
- query_scale: bfloat16 [1280], P(('dp', 'seq')), may hold values from -3 to 3
- w_key: bfloat16 [1280, 1280], P(('dp', 'seq')), may hold values from -0.15625 to 0.15625
- w_value: bfloat16 [1280, 1280], P(('dp', 'seq')), may hold values from -0.15625 to 0.15625
- bias_value: bfloat16 [1280], P(('dp', 'seq')), may hold values from -3 to 3
- w_out: bfloat16 [1280, 1280], P(('dp', 'seq')), may hold values from -1.25 to 1.25
- gain_mlp: bfloat16 [1280], P(('dp', 'seq')), may hold values from 0.099609375 to 1.8984375
- w_hidden: bfloat16 [1280, 1280], P(('dp', 'seq')), may hold values from -0.15625 to 0.15625
- w_back: bfloat16 [1280, 1280], P(('dp', 'seq')), may hold values from -0.15625 to 0.15625
Outputs:
- outputs: bfloat16 [8, 1024, 1280], P('dp', 'seq')
- input_grad: float32 [8, 1024, 1280], P('dp', 'seq')
- grad_gain_attn: float32 [1280], P(('dp', 'seq'))
- grad_w_query: float32 [1280, 1280], P(('dp', 'seq'))
- grad_bias_query: float32 [1280], P(('dp', 'seq'))
- grad_query_scale: float32 [1280], P(('dp', 'seq'))
- grad_w_key: float32 [1280, 1280], P(('dp', 'seq'))
- grad_w_value: float32 [1280, 1280], P(('dp', 'seq'))
- grad_bias_value: float32 [1280], P(('dp', 'seq'))
- grad_w_out: float32 [1280, 1280], P(('dp', 'seq'))
- grad_gain_mlp: float32 [1280], P(('dp', 'seq'))
- grad_w_hidden: float32 [1280, 1280], P(('dp', 'seq'))
- grad_w_back: float32 [1280, 1280], P(('dp', 'seq'))
The draws below stay inside these ranges and needn't reach their ends.
Inputs may be any that keep to these rules, and one draw needn't show every extreme that they name: Slots from lengths[b] on are padding; some sequence has exactly 1024 valid slots and some exactly 256.
All inputs are finite; a program needn't handle non-finite values.
Results may differ from the reference program's by a relative error of at most 0.015.
Values may be sent and summed in bfloat16 or wider, within the bound.
A program may use at most 192 MiB of HBM per device.

```python
import math
import jax
import jax.numpy as jnp
from jax import lax

D = 1280
FF = 1280
HEADS = 16
HEAD_DIM = 80
SEQS = 8
SEQ_LEN = 1024


def draw_lengths(key, part):
    first = jax.random.fold_in(key, 11)
    second = jax.random.fold_in(key, 12)
    drawn = jax.random.randint(first, (SEQS,), SEQ_LEN // 4, SEQ_LEN + 1, dtype=jnp.int32)
    order = jax.random.permutation(second, SEQS)
    drawn = drawn.at[order[0]].set(SEQ_LEN)
    drawn = drawn.at[order[1]].set(SEQ_LEN // 4)
    return drawn.astype(jnp.int32)


def block_scale(key, extent, split, smallest, top_value):
    gain = 1.0
    for position, blocks in split:
        steps = jax.random.uniform(jax.random.fold_in(jax.random.fold_in(key, 6), position), (blocks,), jnp.float32, smallest / len(split), top_value / len(split))
        gain = gain * jnp.repeat(jnp.exp(steps), extent[position] // blocks).reshape((-1,) + (1,) * (len(extent) - 1 - position))
    return gain


def bell_draw(key, shape, spread, most, split=(), kind=jnp.bfloat16):
    factor_of = block_scale(key, shape, split, -0.22, 0.18) if split else 1.0
    entries = jax.random.normal(key, shape, jnp.float32) * spread * factor_of
    return jnp.minimum(jnp.maximum(entries, -most), most).astype(kind)


def setup_inputs(seed: int = 0) -> dict:
    key_list = jax.random.split(jax.random.key(seed), 15)
    inputs = bell_draw(key_list[0], (SEQS, SEQ_LEN, D), 1.0, 6.0, ((0, 8), (1, 4)))
    lengths = draw_lengths(jax.random.fold_in(key_list[14], 71), 0)
    cotangent = bell_draw(key_list[2], (SEQS, SEQ_LEN, D), 1.0, 6.0, ((0, 8), (1, 4)))
    gain_attn = jnp.clip(1.0 + 0.18 * jax.random.normal(key_list[3], (D,), jnp.float32), 0.099609375, 1.8984375).astype(jnp.bfloat16)
    w_query = bell_draw(key_list[4], (D, D), D ** -0.5, 0.15625, ((0, 32),))
    bias_query = bell_draw(key_list[5], (D,), 0.5, 3.0, ((0, 32),))
    query_scale = bell_draw(key_list[6], (D,), 0.5, 3.0, ((0, 32),))
    w_key = bell_draw(key_list[7], (D, D), D ** -0.5, 0.15625, ((0, 32),))
    w_value = bell_draw(key_list[8], (D, D), D ** -0.5, 0.15625, ((0, 32),))
    bias_value = bell_draw(key_list[9], (D,), 0.5, 3.0, ((0, 32),))
    w_out = bell_draw(key_list[10], (D, D), (max(1, D * 16 // SEQ_LEN)) ** -0.5, 1.25, ((0, 32),))
    gain_mlp = jnp.clip(1.0 + 0.18 * jax.random.normal(key_list[11], (D,), jnp.float32), 0.099609375, 1.8984375).astype(jnp.bfloat16)
    w_hidden = bell_draw(key_list[12], (D, FF), D ** -0.5, 0.15625, ((0, 32),))
    w_back = bell_draw(key_list[13], (FF, D), FF ** -0.5, 0.15625, ((0, 32),))
    return dict(inputs=inputs, lengths=lengths, cotangent=cotangent, gain_attn=gain_attn, w_query=w_query, bias_query=bias_query, query_scale=query_scale, w_key=w_key, w_value=w_value, bias_value=bias_value, w_out=w_out, gain_mlp=gain_mlp, w_hidden=w_hidden, w_back=w_back)


query_gain = 1.442695041
masked_score = -1e+30

@jax.custom_vjp
def low(v):
    return lax.optimization_barrier(v.astype(jnp.bfloat16)).astype(jnp.float32)

@jax.custom_vjp
def low_back(v):
    return v

def low_keep(v):
    return (low(v), None)

def low_pass(kept, grad):
    return (grad,)

def back_keep(v):
    return (v, None)

def back_low(kept, grad):
    return (low(grad),)
low.defvjp(low_keep, low_pass)
low_back.defvjp(back_keep, back_low)

def matmul(left, right):
    return jnp.dot(left, right, precision=lax.Precision.HIGHEST, preferred_element_type=jnp.float32)

def rms_unit(values):
    return values * lax.rsqrt(lax.optimization_barrier(jnp.mean(values * values, axis=-1, keepdims=True)) + 1e-06)

def layer(params, inputs_row, valid):
    norm_one, query_mat, query_bias, query_log, key_mat, value_mat, value_bias, output_mat, norm_two, hidden_mat, back_mat = params
    block = min(512, SEQ_LEN)
    blocks = SEQ_LEN // block
    positions = jnp.arange(SEQ_LEN, dtype=jnp.int32)
    normed1 = low(rms_unit(inputs_row) * norm_one)
    query_raw = low_back(matmul(normed1, query_mat) + query_bias)
    scale_vec = jax.nn.softplus(query_log) * query_gain / math.sqrt(HEAD_DIM)
    queries = low(query_raw * scale_vec)
    keys = low_back(low(matmul(normed1, key_mat)))
    values = low_back(low(matmul(normed1, value_mat) + value_bias))
    key_heads = keys.reshape(SEQ_LEN, HEADS, HEAD_DIM)
    value_heads = values.reshape(SEQ_LEN, HEADS, HEAD_DIM)
    query_blocks = queries.reshape(blocks, block, HEADS, HEAD_DIM)
    place_blocks = positions.reshape(blocks, block)

    @jax.checkpoint
    def attend(pieces):
        query_block, place_block = pieces
        scores = jnp.einsum('qhd,khd->hqk', query_block, key_heads, precision=lax.Precision.HIGHEST)
        scores = low_back(scores)
        allowed = positions[None, :] <= place_block[:, None]
        scores = jnp.where(allowed[None], scores, masked_score)
        weights_soft = jax.nn.softmax(scores, axis=-1)
        mixed = jnp.einsum('hqk,khd->qhd', low(weights_soft), value_heads, precision=lax.Precision.HIGHEST)
        return mixed.reshape(block, D)
    mixed = lax.map(attend, (query_blocks, place_blocks)).reshape(SEQ_LEN, D)
    mixed = low_back(low(mixed))
    branch = low_back(matmul(mixed, output_mat))
    middle = inputs_row + branch
    normed2 = low(rms_unit(middle) * norm_two)
    hidden = low_back(matmul(normed2, hidden_mat))
    active = low(jax.nn.silu(hidden))
    result = middle + matmul(active, back_mat)
    return jnp.where(valid[:, None], result, 0.0)

def reference(inputs, lengths, cotangent, gain_attn, w_query, bias_query, query_scale, w_key, w_value, bias_value, w_out, gain_mlp, w_hidden, w_back):
    params = tuple((entry.astype(jnp.float32) for entry in (gain_attn, w_query, bias_query, query_scale, w_key, w_value, bias_value, w_out, gain_mlp, w_hidden, w_back)))
    positions = jnp.arange(SEQ_LEN, dtype=jnp.int32)

    def one_seq(totals, pieces):
        inputs_row, grad_row, length_one = pieces
        valid = positions < length_one
        inputs_float = inputs_row.astype(jnp.float32)

        def local(param_set, values_in):
            return layer(param_set, values_in, valid)
        result, pull = jax.vjp(local, params, inputs_float)
        param_grads, input_grads = pull(grad_row.astype(jnp.float32))
        totals = jax.tree.map(lambda left, right: left + right, totals, param_grads)
        return (totals, (result.astype(jnp.bfloat16), input_grads))
    zeros = tuple((jnp.zeros(entry.shape, jnp.float32) for entry in params))
    totals, (outputs, input_grad) = lax.scan(one_seq, zeros, (inputs, cotangent, lengths))
    return (outputs, input_grad, totals[0], totals[1], totals[2], totals[3], totals[4], totals[5], totals[6], totals[7], totals[8], totals[9], totals[10])
```

```python
import math

import jax
import jax.numpy as jnp
from jax import lax
from jax.experimental import pallas as pl
from jax.experimental.pallas import tpu as pltpu
from jax.sharding import PartitionSpec as P

HEADS = 16
HEAD_DIM = 80


query_gain = 1.442695041
masked_score = -1e30


def normed(values):
    squares = jnp.mean(values * values, axis=-1, keepdims=True)
    inverse = lax.rsqrt(squares + 1e-06)
    return (values * inverse, inverse)


def norm_back(grad_in, unit, inverse, gain):
    scaled = grad_in * gain
    return inverse * (scaled - unit * jnp.mean(scaled * unit, axis=-1, keepdims=True))


def row_product(left, right):
    return lax.dot_general(
        left, right, (((0,), (0,)), ((), ())), preferred_element_type=jnp.float32
    )


def back_product(left, right):
    return lax.dot_general(
        left, right, (((1,), (1,)), ((), ())), preferred_element_type=jnp.float32
    )


def shards(
    inputs,
    lengths,
    cotangent,
    gain_attn,
    w_query,
    bias_query,
    query_scale,
    w_key,
    w_value,
    bias_value,
    w_out,
    gain_mlp,
    w_hidden,
    w_back,
):
    seq_dev, group_rows, width = inputs.shape
    tok_rows = seq_dev * group_rows
    head_count = HEADS
    head_width = HEAD_DIM
    gathered = (
        lax.all_gather(gain_attn, ("dp", "seq"), axis=0, tiled=True),
        lax.all_gather(w_query, ("dp", "seq"), axis=0, tiled=True),
        lax.all_gather(bias_query, ("dp", "seq"), axis=0, tiled=True),
        lax.all_gather(query_scale, ("dp", "seq"), axis=0, tiled=True),
        lax.all_gather(w_key, ("dp", "seq"), axis=0, tiled=True),
        lax.all_gather(w_value, ("dp", "seq"), axis=0, tiled=True),
        lax.all_gather(bias_value, ("dp", "seq"), axis=0, tiled=True),
        lax.all_gather(w_out, ("dp", "seq"), axis=0, tiled=True),
        lax.all_gather(gain_mlp, ("dp", "seq"), axis=0, tiled=True),
        lax.all_gather(w_hidden, ("dp", "seq"), axis=0, tiled=True),
        lax.all_gather(w_back, ("dp", "seq"), axis=0, tiled=True),
    )
    (
        norm_one,
        query_mat,
        query_bias,
        query_log,
        key_mat,
        value_mat,
        value_bias,
        output_mat,
        norm_two,
        hidden_mat,
        back_mat,
    ) = gathered
    ff_width = hidden_mat.shape[1]
    offset = lax.axis_index("seq") * group_rows
    place = offset + jnp.arange(group_rows, dtype=jnp.int32)
    valid = place[None, :] < lengths[:, None]
    row_valid = valid.reshape(tok_rows, 1)
    inputs_rows = inputs.reshape(tok_rows, width).astype(jnp.float32)
    unit_one, inverse_one = normed(inputs_rows)
    gain_one = norm_one.astype(jnp.float32)
    normed_one = (unit_one * gain_one).astype(jnp.bfloat16)
    query_raw = jnp.dot(
        normed_one, query_mat, preferred_element_type=jnp.float32
    ) + query_bias.astype(jnp.float32)
    query_logf = query_log.astype(jnp.float32)
    scale_vec = jax.nn.softplus(query_logf) * (query_gain / math.sqrt(head_width))
    queries = (query_raw * scale_vec).astype(jnp.bfloat16)
    keys_local = jnp.dot(normed_one, key_mat, preferred_element_type=jnp.float32).astype(
        jnp.bfloat16
    )
    values_local = (
        jnp.dot(normed_one, value_mat, preferred_element_type=jnp.float32)
        + value_bias.astype(jnp.float32)
    ).astype(jnp.bfloat16)
    keys_three = keys_local.reshape(seq_dev, group_rows, width)
    values_three = values_local.reshape(seq_dev, group_rows, width)
    queries_three = queries.reshape(seq_dev, group_rows, width)
    keys_all, values_all = (
        lax.all_gather(keys_three, "seq", axis=1, tiled=True),
        lax.all_gather(values_three, "seq", axis=1, tiled=True),
    )
    seq_slots = keys_all.shape[1]
    key_place = jnp.arange(seq_slots, dtype=jnp.int32)
    allowed = key_place[None, :] <= place[:, None]

    def attend(pieces):
        query_block, key_block, value_block = pieces
        query_heads = query_block.reshape(group_rows, head_count, head_width)
        key_heads = key_block.reshape(seq_slots, head_count, head_width)
        value_heads = value_block.reshape(seq_slots, head_count, head_width)
        scores = jnp.einsum(
            "qhd,khd->hqk", query_heads, key_heads, preferred_element_type=jnp.float32
        )
        scores = jnp.where(allowed[None], scores, masked_score)
        largest = jnp.max(scores, axis=-1, keepdims=True)
        raised = jnp.exp(scores - largest)
        totals = jnp.sum(raised, axis=-1, keepdims=True)
        weights_soft = (raised / totals).astype(jnp.bfloat16)
        mixed = jnp.einsum(
            "hqk,khd->qhd", weights_soft, value_heads, preferred_element_type=jnp.float32
        )
        log_total = largest[..., 0] + jnp.log(totals[..., 0])
        return (mixed.reshape(group_rows, width).astype(jnp.bfloat16), log_total)

    mixed_three, log_totals = lax.map(attend, (queries_three, keys_all, values_all))
    mixed = mixed_three.reshape(tok_rows, width)
    middle = inputs_rows + jnp.dot(mixed, output_mat, preferred_element_type=jnp.float32)
    unit_two, inverse_two = normed(middle)
    gain_two = norm_two.astype(jnp.float32)
    normed_two = (unit_two * gain_two).astype(jnp.bfloat16)
    hidden = jnp.dot(normed_two, hidden_mat, preferred_element_type=jnp.float32)
    active = jax.nn.silu(hidden).astype(jnp.bfloat16)
    result = middle + jnp.dot(active, back_mat, preferred_element_type=jnp.float32)
    outputs = (
        jnp.where(row_valid, result, 0.0).astype(jnp.bfloat16).reshape(seq_dev, group_rows, width)
    )
    again = (
        lax.all_gather(gain_attn, ("dp", "seq"), axis=0, tiled=True),
        lax.all_gather(w_query, ("dp", "seq"), axis=0, tiled=True),
        lax.all_gather(w_key, ("dp", "seq"), axis=0, tiled=True),
        lax.all_gather(w_value, ("dp", "seq"), axis=0, tiled=True),
        lax.all_gather(w_out, ("dp", "seq"), axis=0, tiled=True),
        lax.all_gather(gain_mlp, ("dp", "seq"), axis=0, tiled=True),
        lax.all_gather(w_hidden, ("dp", "seq"), axis=0, tiled=True),
        lax.all_gather(w_back, ("dp", "seq"), axis=0, tiled=True),
    )
    norm_one, query_mat, key_mat, value_mat, output_mat, norm_two, hidden_mat, back_mat = again
    gain_one = norm_one.astype(jnp.float32)
    gain_two = norm_two.astype(jnp.float32)
    keys_back, values_back = (
        lax.all_gather(keys_three, "seq", axis=1, tiled=True),
        lax.all_gather(values_three, "seq", axis=1, tiled=True),
    )
    cot_rows = cotangent.reshape(tok_rows, width)
    grad_out = jnp.where(row_valid, cot_rows, jnp.zeros_like(cot_rows))
    grad_active = back_product(grad_out, back_mat)
    sigma = jax.nn.sigmoid(hidden)
    grad_hidden = (grad_active * sigma * (1.0 + hidden * (1.0 - sigma))).astype(jnp.bfloat16)
    grad_normed_two = back_product(grad_hidden, hidden_mat)
    grad_gain_two = jnp.sum(grad_normed_two * unit_two, axis=0)
    grad_middle = grad_out.astype(jnp.float32) + norm_back(
        grad_normed_two, unit_two, inverse_two, gain_two
    )
    grad_middle_low = grad_middle.astype(jnp.bfloat16)
    grad_mixed = back_product(grad_middle_low, output_mat).astype(jnp.bfloat16)
    grad_mixed_three = grad_mixed.reshape(seq_dev, group_rows, width)

    def attend_query(pieces):
        query_block, key_block, value_block, grad_block, log_total = pieces
        query_heads = query_block.reshape(group_rows, head_count, head_width)
        key_heads = key_block.reshape(seq_slots, head_count, head_width)
        value_heads = value_block.reshape(seq_slots, head_count, head_width)
        grad_heads = grad_block.reshape(group_rows, head_count, head_width)
        scores = jnp.einsum(
            "qhd,khd->hqk", query_heads, key_heads, preferred_element_type=jnp.float32
        )
        scores = jnp.where(allowed[None], scores, masked_score)
        weights_soft = jnp.exp(scores - log_total[..., None])
        grad_soft = jnp.einsum(
            "qhd,khd->hqk", grad_heads, value_heads, preferred_element_type=jnp.float32
        )
        inner = jnp.sum(weights_soft * grad_soft, axis=-1, keepdims=True)
        grad_scores = (weights_soft * (grad_soft - inner)).astype(jnp.bfloat16)
        grad_queries = jnp.einsum(
            "hqk,khd->qhd", grad_scores, key_heads, preferred_element_type=jnp.float32
        )
        return (grad_queries.reshape(group_rows, width), inner[..., 0])

    grad_queries, inner_rows = lax.map(
        attend_query, (queries_three, keys_back, values_back, grad_mixed_three, log_totals)
    )
    queries_every, grad_every = (
        lax.all_gather(queries_three, "seq", axis=1, tiled=True),
        lax.all_gather(grad_mixed_three, "seq", axis=1, tiled=True),
    )
    lse_every, inner_every = (
        lax.all_gather(log_totals, "seq", axis=2, tiled=True),
        lax.all_gather(inner_rows, "seq", axis=2, tiled=True),
    )
    later = key_place[:, None] >= place[None, :]

    def key_side(pieces):
        query_block, grad_block, key_block, value_block, lse_block, inner_block = pieces
        query_heads = query_block.reshape(seq_slots, head_count, head_width)
        grad_heads = grad_block.reshape(seq_slots, head_count, head_width)
        key_heads = key_block.reshape(group_rows, head_count, head_width)
        value_heads = value_block.reshape(group_rows, head_count, head_width)
        scores = jnp.einsum(
            "qhd,khd->hqk", query_heads, key_heads, preferred_element_type=jnp.float32
        )
        scores = jnp.where(later[None], scores, masked_score)
        weights_soft = jnp.exp(scores - lse_block[..., None])
        weights_low = weights_soft.astype(jnp.bfloat16)
        grad_soft = jnp.einsum(
            "qhd,khd->hqk", grad_heads, value_heads, preferred_element_type=jnp.float32
        )
        grad_scores = (weights_soft * (grad_soft - inner_block[..., None])).astype(jnp.bfloat16)
        grad_keys = jnp.einsum(
            "hqk,qhd->khd", grad_scores, query_heads, preferred_element_type=jnp.float32
        )
        grad_values = jnp.einsum(
            "hqk,qhd->khd", weights_low, grad_heads, preferred_element_type=jnp.float32
        )
        return (grad_keys.reshape(group_rows, width), grad_values.reshape(group_rows, width))

    grad_keys_sum, grad_values_sum = lax.map(
        key_side, (queries_every, grad_every, keys_three, values_three, lse_every, inner_every)
    )
    grad_keys = grad_keys_sum.reshape(tok_rows, width).astype(jnp.bfloat16)
    grad_values = grad_values_sum.reshape(tok_rows, width).astype(jnp.bfloat16)
    grad_queries = grad_queries.reshape(tok_rows, width)
    grad_query_raw = (grad_queries * scale_vec).astype(jnp.bfloat16)
    grad_scale = jnp.sum(grad_queries * query_raw, axis=0)
    grad_query_log = grad_scale * jax.nn.sigmoid(query_logf) * (query_gain / math.sqrt(head_width))
    grad_query_bias = jnp.sum(grad_query_raw.astype(jnp.float32), axis=0)
    grad_value_bias = jnp.sum(grad_values.astype(jnp.float32), axis=0)
    grad_normed_one = (
        back_product(grad_query_raw, query_mat)
        + back_product(grad_keys, key_mat)
        + back_product(grad_values, value_mat)
    )
    grad_gain_one = jnp.sum(grad_normed_one * unit_one, axis=0)
    input_grad = grad_middle + norm_back(grad_normed_one, unit_one, inverse_one, gain_one)
    dp_count = lax.axis_size("dp")
    seq_count = lax.axis_size("seq")
    share = width // (dp_count * seq_count)
    share_ff = ff_width // (dp_count * seq_count)
    left_parts = (
        lax.all_to_all(
            normed_one.reshape(tok_rows, dp_count, seq_count, share),
            "seq",
            split_axis=2,
            concat_axis=0,
            tiled=True,
        ),
        lax.all_to_all(
            mixed.reshape(tok_rows, dp_count, seq_count, share),
            "seq",
            split_axis=2,
            concat_axis=0,
            tiled=True,
        ),
        lax.all_to_all(
            normed_two.reshape(tok_rows, dp_count, seq_count, share),
            "seq",
            split_axis=2,
            concat_axis=0,
            tiled=True,
        ),
        lax.all_to_all(
            active.reshape(tok_rows, dp_count, seq_count, share_ff),
            "seq",
            split_axis=2,
            concat_axis=0,
            tiled=True,
        ),
    )
    left_normed_one = left_parts[0].reshape(-1, dp_count * share)
    left_mixed = left_parts[1].reshape(-1, dp_count * share)
    left_normed_two = left_parts[2].reshape(-1, dp_count * share)
    left_active = left_parts[3].reshape(-1, dp_count * share_ff)
    right_parts = (
        lax.all_gather(grad_query_raw, "seq", axis=0, tiled=True),
        lax.all_gather(grad_keys, "seq", axis=0, tiled=True),
        lax.all_gather(grad_values, "seq", axis=0, tiled=True),
        lax.all_gather(grad_middle_low, "seq", axis=0, tiled=True),
        lax.all_gather(grad_hidden, "seq", axis=0, tiled=True),
        lax.all_gather(grad_out, "seq", axis=0, tiled=True),
    )
    right_query, right_keys, right_values, right_middle, right_hidden, right_out = right_parts
    part_query_mat = row_product(left_normed_one, right_query)
    part_key_mat = row_product(left_normed_one, right_keys)
    part_value_mat = row_product(left_normed_one, right_values)
    part_output_mat = row_product(left_mixed, right_middle)
    part_hidden_mat = row_product(left_normed_two, right_hidden)
    part_back_mat = row_product(left_active, right_out)
    matrices = (
        lax.psum_scatter(
            part_query_mat.astype(jnp.bfloat16), "dp", scatter_dimension=0, tiled=True
        ).astype(jnp.float32),
        lax.psum_scatter(
            part_key_mat.astype(jnp.bfloat16), "dp", scatter_dimension=0, tiled=True
        ).astype(jnp.float32),
        lax.psum_scatter(
            part_value_mat.astype(jnp.bfloat16), "dp", scatter_dimension=0, tiled=True
        ).astype(jnp.float32),
        lax.psum_scatter(
            part_output_mat.astype(jnp.bfloat16), "dp", scatter_dimension=0, tiled=True
        ).astype(jnp.float32),
        lax.psum_scatter(
            part_hidden_mat.astype(jnp.bfloat16), "dp", scatter_dimension=0, tiled=True
        ).astype(jnp.float32),
        lax.psum_scatter(
            part_back_mat.astype(jnp.bfloat16), "dp", scatter_dimension=0, tiled=True
        ).astype(jnp.float32),
    )
    vectors = (
        lax.psum_scatter(grad_gain_one, ("dp", "seq"), scatter_dimension=0, tiled=True),
        lax.psum_scatter(grad_query_bias, ("dp", "seq"), scatter_dimension=0, tiled=True),
        lax.psum_scatter(grad_query_log, ("dp", "seq"), scatter_dimension=0, tiled=True),
        lax.psum_scatter(grad_value_bias, ("dp", "seq"), scatter_dimension=0, tiled=True),
        lax.psum_scatter(grad_gain_two, ("dp", "seq"), scatter_dimension=0, tiled=True),
    )
    return (
        outputs,
        input_grad.reshape(seq_dev, group_rows, width),
        vectors[0],
        matrices[0],
        vectors[1],
        vectors[2],
        matrices[1],
        matrices[2],
        vectors[3],
        matrices[3],
        vectors[4],
        matrices[4],
        matrices[5],
    )


F32 = jnp.float32
BF16 = jnp.bfloat16
MESH_ID = pl.DeviceIdType.MESH
ROWS = 256
WIDTH = 1280
SHARE = 40
MINE = 320
GROUP_HEADS = 4
SLOTS = 1024
PACK = 1024


def fits(mesh):
    return mesh.shape["dp"] == 8 and mesh.shape["seq"] == 4


def dot_nn(left, right):
    return jnp.dot(left, right, preferred_element_type=F32)


def dot_nt(left, right):
    return lax.dot_general(left, right, (((1,), (1,)), ((), ())), preferred_element_type=F32)


def dot_tn(left, right):
    return lax.dot_general(left, right, (((0,), (0,)), ((), ())), preferred_element_type=F32)


def tile(index, size):
    return pl.ds(pl.multiple_of(index * size, size), size)


def strip(xx, yy):
    return pl.ds(pl.multiple_of((xx * 2 + yy) * 2 * SHARE, 16), 2 * SHARE)


def half(cc):
    return pl.ds(pl.multiple_of(cc * (WIDTH // 2), 128), WIDTH // 2)


class Links:
    def __init__(self, send_sems, recv_sems):
        self.send_sems, self.recv_sems = send_sems, recv_sems
        self.count = 0
        self.open = {}

    def send(self, key, src, dst, device):
        index = self.count
        self.count += 1
        copy = pltpu.make_async_remote_copy(
            src_ref=src,
            dst_ref=dst,
            send_sem=self.send_sems.at[index],
            recv_sem=self.recv_sems.at[index],
            device_id=device,
            device_id_type=MESH_ID,
        )
        copy.start()
        self.open[key] = copy

    def recv(self, *keys):
        for key in keys:
            self.open[key].wait_recv()

    def sent(self, *keys):
        for key in keys:
            self.open.pop(key).wait_send()

    def sent_all(self):
        for key in list(self.open):
            self.open.pop(key).wait_send()


def layer_kernel(
    x_ref,
    len_ref,
    cot_ref,
    vec_ref,
    wq_ref,
    wk_ref,
    wv_ref,
    wo_ref,
    wh_ref,
    wb_ref,
    out_ref,
    ig_ref,
    gvec_ref,
    gq_ref,
    gk_ref,
    gv_ref,
    go_ref,
    gh_ref,
    gb_ref,
    full_o,
    full_h,
    full_b,
    part_b,
    core_in,
    far_in,
    near_in,
    last_in,
    qkv_w,
    stage,
    tokens,
    keys,
    vals,
    queries_t,
    keys_t,
    vals_t,
    queries_n,
    lse,
    mix_out,
    mix_in,
    mix,
    middle,
    hidden,
    norm2,
    active,
    gmix_out,
    gmix_in,
    grad_low,
    dk_acc,
    dv_acc,
    dq_t,
    grads,
    unit_core,
    unit_far,
    qkv_part,
    qkv_near,
    qkv_last,
    qkv_home,
    qkv_sum,
    vec_slots,
    vec_row,
    vec_part,
    vec_in,
    qkv_own,
    pair_in,
    give_out,
    give_in,
    mix_send,
    mix_recv,
    send_sems,
    recv_sems,
):
    d = lax.axis_index("dp")
    s = lax.axis_index("seq")
    z, x = d // 2, d % 2
    y, c = s // 2, s % 2
    links = Links(send_sems, recv_sems)
    send, recv = links.send, links.recv
    core_dev = (d, y * 2 + (1 - c))
    y_dev = (d, (1 - y) * 2 + c)
    yc_dev = (d, (1 - y) * 2 + (1 - c))
    x_dev = (z * 2 + (1 - x), s)
    zs = [None] + [(z + k) % 4 for k in range(1, 4)]
    from_z = [None] + [(z + 4 - k) % 4 for k in range(1, 4)]
    z_devs = [None] + [(zs[k] * 2 + x, s) for k in range(1, 4)]

    barrier = pltpu.get_barrier_semaphore()
    for device in (core_dev, y_dev, yc_dev, x_dev, z_devs[1], z_devs[2], z_devs[3]):
        pl.semaphore_signal(barrier, inc=1, device_id=device, device_id_type=MESH_ID)

    for member in range(4):
        cols = slice(MINE * member, MINE * (member + 1))
        stage[member] = jnp.concatenate(
            [wq_ref[:, cols], wk_ref[:, cols], wv_ref[:, cols], jnp.zeros((SHARE, 64), BF16)], axis=1
        )
    qkv_own[s] = stage[s]
    tokens[s] = x_ref[...]
    vec_slots[z, x, y, c] = vec_ref[...]
    shards = {"o": wo_ref, "h": wh_ref, "b": wb_ref}
    slot_of = {"o": 0, "h": 1, "b": 2}
    for m in "ohb":
        pair_in[slot_of[m], c] = shards[m][:, half(c)]
    pl.semaphore_wait(barrier, 7)

    group = ((1, core_dev), (2, y_dev), (3, yc_dev))
    peers = (None, y * 2 + (1 - c), (1 - y) * 2 + c, (1 - y) * 2 + (1 - c))
    for k, device in ((2, y_dev), (3, yc_dev), (1, core_dev)):
        send(("a2a", k), stage.at[peers[k]], qkv_own.at[s], device)
    for m in "ohb":
        send(("pair", m), shards[m].at[:, half(1 - c)], pair_in.at[slot_of[m], c], core_dev)
    for k in (1, 2, 3):
        send(("vz", k), vec_ref, vec_slots.at[z, x, y, c], z_devs[k])
    send("xy", x_ref, tokens.at[s], y_dev)
    send("xc", x_ref, tokens.at[s], core_dev)

    fulls = {"o": full_o, "h": full_h, "b": full_b}
    near_axis = {"o": "x", "h": "x", "b": "y"}

    def strip_of(axis, near, far):
        if axis == "x":
            return strip(x if near == 0 else 1 - x, y if far == 0 else 1 - y)
        return strip(x if far == 0 else 1 - x, y if near == 0 else 1 - y)

    def devs(m):
        return (x_dev, y_dev) if near_axis[m] == "x" else (y_dev, x_dev)

    def gather_z(m):
        for k in (1, 2, 3):
            piece = fulls[m].at[z, strip(x, y), half(c)]
            send((m, "z", k), piece, piece, z_devs[k])

    def gather_own(m):
        near_dev, far_dev = devs(m)
        piece = fulls[m].at[z, strip(x, y), half(c)]
        send((m, "n", 0), piece, piece, near_dev)
        send((m, "f", 0), piece, piece, far_dev)

    def gather_near(m, k):
        near_dev, far_dev = devs(m)
        recv((m, "z", k))
        piece = fulls[m].at[from_z[k], strip(x, y), half(c)]
        send((m, "n", k), piece, piece, near_dev)
        send((m, "f", k), piece, piece, far_dev)

    def all_z(m, near, far):
        return fulls[m].at[:, strip_of(near_axis[m], near, far), half(c)]

    def gather_far(m):
        near_dev, far_dev = devs(m)
        piece = all_z(m, 0, 0)
        send((m, "c", 0), piece, piece, core_dev)
        recv(*[(m, "n", k) for k in range(4)])
        piece = all_z(m, 1, 0)
        send((m, "f", 4), piece, piece, far_dev)
        send((m, "c", 1), piece, piece, core_dev)

    def gather_core(m, part):
        if part == 0:
            recv(*[(m, "f", k) for k in range(4)])
            piece = all_z(m, 0, 1)
            send((m, "c", 2), piece, piece, core_dev)
        else:
            recv((m, "f", 4))
            piece = all_z(m, 1, 1)
            send((m, "c", 3), piece, piece, core_dev)

    def gather_done(m):
        recv(*[(m, "c", k) for k in range(4)])

    for m in "ohb":
        recv(("pair", m))
        fulls[m][z, strip(x, y), half(c)] = jnp.concatenate(
            [pair_in[slot_of[m], 0], pair_in[slot_of[m], 1]], axis=0
        )
    gather_z("o")
    gather_own("o")
    gather_own("h")
    gather_own("b")
    recv(("a2a", 1), ("a2a", 2), ("a2a", 3))
    qkv_w[d] = jnp.concatenate([qkv_own[member] for member in range(4)], axis=0)
    for k in (1, 2, 3):
        send(("wz", k), qkv_w.at[d], qkv_w.at[d], z_devs[k])
    send(("wx", 0), qkv_w.at[d], qkv_w.at[d], x_dev)
    gather_z("h")
    gather_z("b")
    recv(("vz", 1), ("vz", 2), ("vz", 3))
    piece = vec_slots.at[:, x, y, c]
    send("vx", piece, piece, x_dev)
    gather_near("o", 1)
    gather_near("o", 2)
    gather_near("o", 3)
    recv("vx")
    piece = vec_slots.at[:, :, y, c]
    send("vy", piece, piece, y_dev)
    recv("xy")
    piece = tokens.at[peers[2]]
    send("xyc", piece, piece, core_dev)
    recv("vy")
    piece = vec_slots.at[:, :, :, c]
    send("vc", piece, piece, core_dev)

    def qkv_near_step(k):
        recv(("wz", k))
        row = from_z[k] * 2 + x
        send(("wx", k), qkv_w.at[row], qkv_w.at[row], x_dev)

    gather_far("o")
    qkv_near_step(1)
    recv("vc")
    vec_row[...] = jnp.zeros_like(vec_row)
    for slot in range(32):
        start = slot * SHARE
        low = start // 128 * 128
        piece = jnp.concatenate(
            [vec_slots[slot // 8, slot // 4 % 2, slot // 2 % 2, slot % 2], jnp.zeros((8, 128), F32)], axis=1
        )
        if start > low:
            piece = pltpu.roll(piece, start - low, 1)
        vec_row[:, low : low + 256] += piece
    recv("xc", "xyc")
    links.sent("xyc")

    def norm_rows(step, carry):
        for member in range(4):
            rows = tile(step, 64)
            value = tokens[member, rows, :].astype(F32)
            unit = value * lax.rsqrt(jnp.mean(value * value, axis=-1, keepdims=True) + 1e-06)
            tokens[member, rows, :] = (unit * vec_row[0:1, :WIDTH]).astype(BF16)
        return carry

    lax.fori_loop(0, ROWS // 64, norm_rows, 0)
    qkv_near_step(2)
    gather_core("o", 0)
    gather_core("o", 1)
    qkv_near_step(3)

    def own(row):
        value = vec_row[row : row + 1, 0:MINE]
        for member in range(1, 4):
            value = jnp.where(s == member, vec_row[row : row + 1, MINE * member : MINE * (member + 1)], value)
        return value

    query_log = own(2)
    factor = query_gain / math.sqrt(HEAD_DIM)
    scale = (jnp.maximum(query_log, 0.0) + jnp.log1p(jnp.exp(-jnp.abs(query_log)))) * factor
    query_bias, value_bias = own(1), own(3)

    recv(*[("wx", k) for k in range(4)])
    weights = qkv_w.reshape(WIDTH, PACK)

    def project(i, carry):
        rows = tile(i, ROWS)
        raw = dot_nn(tokens[i], weights[...])
        query = ((raw[:, :MINE] + query_bias) * scale).astype(BF16)
        key = raw[:, MINE : 2 * MINE].astype(BF16)
        val = (raw[:, 2 * MINE : 3 * MINE] + value_bias).astype(BF16)
        queries_n[i] = query
        queries_t[:, rows] = query.T
        keys_t[:, rows] = key.T
        vals_t[:, rows] = val.T
        for h in range(GROUP_HEADS):
            keys[h, rows, :] = key[:, HEAD_DIM * h : HEAD_DIM * (h + 1)]
            vals[h, rows, :] = val[:, HEAD_DIM * h : HEAD_DIM * (h + 1)]
        return carry

    lax.fori_loop(0, 4, project, 0)
    for k in (1, 2, 3):
        gather_near("h", k)

    key_place = lax.broadcasted_iota(jnp.int32, (ROWS, ROWS), 0)
    query_place = lax.broadcasted_iota(jnp.int32, (ROWS, ROWS), 1)
    allowed = key_place <= query_place

    def attend(i):
        low, high = i * ROWS, (i + 1) * ROWS

        def head(h, carry):
            rows = tile(h, HEAD_DIM)
            query = queries_t[rows, low:high]
            near = jnp.where(allowed, dot_nn(keys[h, low:high, :], query), masked_score)
            largest = jnp.max(near, axis=0, keepdims=True)
            if i:
                before = dot_nn(keys[h, 0:low, :], query)
                largest = jnp.maximum(largest, jnp.max(before, axis=0, keepdims=True))
            near = jnp.exp(near - largest)
            total = jnp.sum(near, axis=0, keepdims=True)
            mixed = dot_nn(vals_t[rows, low:high], near.astype(BF16))
            if i:
                before = jnp.exp(before - largest)
                total += jnp.sum(before, axis=0, keepdims=True)
                mixed += dot_nn(vals_t[rows, 0:low], before.astype(BF16))
            lse[h, :, low:high] = largest + jnp.log(total)
            mix_out[i, rows, :] = (mixed / total).astype(BF16)
            return carry

        lax.fori_loop(0, GROUP_HEADS, head, 0)

    def mix_copy(dest, source):
        return pltpu.make_async_remote_copy(
            src_ref=mix_out.at[dest],
            dst_ref=mix_in.at[source],
            send_sem=mix_send.at[dest],
            recv_sem=mix_recv.at[source],
            device_id=(d, dest),
            device_id_type=MESH_ID,
        )

    for i in (3, 2, 1, 0):
        attend(i)

        @pl.when(s != i)
        def _():
            mix_copy(i, s).start()

        @pl.when(s == i)
        def _():
            mix_in[i] = mix_out[i]

        if i == 3:
            gather_far("h")
        if i == 2:
            gather_near("b", 1)
            gather_near("b", 2)
        if i == 1:
            gather_near("b", 3)

    gather_done("o")
    for k in (1, 2, 3):
        mix_copy(peers[k], peers[k]).wait_recv()

    mix[...] = mix_in[...].reshape(WIDTH, ROWS).T
    mats = {m: fulls[m].reshape(WIDTH, WIDTH) for m in "ohb"}

    def middle_step(j, carry):
        cols = tile(j, 256)
        middle[:, cols] = x_ref[:, cols].astype(F32) + dot_nn(mix[...], mats["o"][:, cols])
        return carry

    lax.fori_loop(0, 5, middle_step, 0)

    def rms_inverse(value):
        return lax.rsqrt(jnp.mean(value * value, axis=-1, keepdims=True) + 1e-06)

    def norm_two(step, carry):
        rows = tile(step, 64)
        value = middle[rows, :]
        norm2[rows, :] = (value * rms_inverse(value) * vec_row[4:5, :WIDTH]).astype(BF16)
        return carry

    lax.fori_loop(0, ROWS // 64, norm_two, 0)
    gather_far("b")
    gather_core("h", 0)
    gather_core("h", 1)
    gather_done("h")

    def hidden_step(j, carry):
        cols = tile(j, 256)
        value = dot_nn(norm2[...], mats["h"][:, cols])
        hidden[:, cols] = value
        active[:, cols] = (value * jax.nn.sigmoid(value)).astype(BF16)
        return carry

    lax.fori_loop(0, 5, hidden_step, 0)

    place = s * ROWS + lax.broadcasted_iota(jnp.int32, (ROWS, 1), 0)
    valid = place < len_ref[0]

    def grad_y():
        return jnp.where(valid, cot_ref[...], jnp.zeros((ROWS, WIDTH), BF16))

    parts = {"b": part_b, "h": full_b, "o": full_h}
    far_axis = {"b": "x", "h": "x", "o": "y"}
    outs = {"b": gb_ref, "h": gh_ref, "o": go_ref}
    order = {"b": 0, "h": 1, "o": 2}

    def weight_grad(m, left):
        flat = parts[m].reshape(WIDTH, WIDTH)
        right = grad_y() if m == "b" else grad_low[...]

        def step(j, carry):
            flat[tile(j, 256), :] = left(j, right).astype(BF16)
            return carry

        lax.fori_loop(0, 5, step, 0)

    def part_at(m, far, near, cc):
        return parts[m].at[:, strip_of(far_axis[m], far, near), half(cc)]

    def core_at(m, far, near):
        ref = core_in.at[order[m]]
        if far_axis[m] == "x":
            return ref.at[:, x if far == 0 else 1 - x, y if near == 0 else 1 - y]
        return ref.at[:, x if near == 0 else 1 - x, y if far == 0 else 1 - y]

    def add_into(target, other):
        def step(zz, carry):
            target[zz] = (target[zz].astype(F32) + other[zz].astype(F32)).astype(BF16)
            return carry

        lax.fori_loop(0, 4, step, 0)

    def grad_devs(m):
        return (x_dev, y_dev) if far_axis[m] == "x" else (y_dev, x_dev)

    def scatter_core(m):
        for far in (1, 0):
            for near in (1, 0):
                send((m, "gc", far, near), part_at(m, far, near, 1 - c), core_at(m, far, near), core_dev)

    def scatter_far(m):
        far_dev, near_dev = grad_devs(m)
        for near in (1, 0):
            recv((m, "gc", 1, near))
            add_into(part_at(m, 1, near, c), core_at(m, 1, near))
            send((m, "gf", near), part_at(m, 1, near, c), far_in.at[order[m], near], far_dev)
        for near in (1, 0):
            recv((m, "gc", 0, near))
            add_into(part_at(m, 0, near, c), core_at(m, 0, near))

    def scatter_near(m):
        far_dev, near_dev = grad_devs(m)
        recv((m, "gf", 1))
        add_into(part_at(m, 0, 1, c), far_in.at[order[m], 1])
        send((m, "gn"), part_at(m, 0, 1, c), near_in.at[order[m]], near_dev)
        recv((m, "gf", 0))
        add_into(part_at(m, 0, 0, c), far_in.at[order[m], 0])

    def scatter_z(m):
        recv((m, "gn"))
        add_into(part_at(m, 0, 0, c), near_in.at[order[m]])
        for k in (1, 2, 3):
            send((m, "gz", k), part_at(m, 0, 0, c).at[zs[k]], last_in.at[order[m], k - 1], z_devs[k])

    def scatter_sum(m):
        total = part_at(m, 0, 0, c)[z].astype(F32)
        for k in (1, 2, 3):
            recv((m, "gz", k))
            total += last_in[order[m], k - 1].astype(F32)
        outs[m][:, half(c)] = jnp.where(c == 0, total[:SHARE], total[SHARE:])
        give_out[order[m]] = jnp.where(c == 0, total[SHARE:], total[:SHARE])
        send((m, "give"), give_out.at[order[m]], give_in.at[order[m]], core_dev)

    def scatter_done(m):
        recv((m, "give"))
        outs[m][:, half(1 - c)] = give_in[order[m]]

    weight_grad("b", lambda j, right: dot_tn(active[:, tile(j, 256)], right))
    scatter_core("b")
    gather_core("b", 0)
    gather_core("b", 1)
    gather_done("b")
    scatter_far("b")

    def back_step(j, carry):
        cols = tile(j, 256)
        value = hidden[:, cols]
        sigma = jax.nn.sigmoid(value)
        grad = dot_nt(grad_y(), mats["b"][cols, :])
        grad_low[:, cols] = (grad * sigma * (1.0 + value * (1.0 - sigma))).astype(BF16)
        out_ref[:, cols] = jnp.where(
            valid, middle[:, cols] + dot_nn(active[...], mats["b"][:, cols]), 0.0
        ).astype(BF16)
        return carry

    lax.fori_loop(0, 5, back_step, 0)
    links.sent(*[("b", "c", k) for k in range(4)], *[("b", "z", k) for k in (1, 2, 3)])
    links.sent(*[("b", kind, k) for kind in "nf" for k in range(4)], ("b", "f", 4))
    weight_grad("h", lambda j, right: dot_tn(norm2[:, tile(j, 256)], right))
    scatter_core("h")

    def normed_step(j, carry):
        hidden[:, tile(j, 256)] = dot_nt(grad_low[...], mats["h"][tile(j, 256), :])
        return carry

    lax.fori_loop(0, 5, normed_step, 0)
    vec_part[...] = jnp.zeros_like(vec_part)

    def middle_back(step, carry):
        rows = tile(step, 64)
        value = middle[rows, :]
        inverse = rms_inverse(value)
        unit = value * inverse
        grad = hidden[rows, :]
        vec_part[4:5, :] += jnp.sum(grad * unit, axis=0, keepdims=True)
        scaled = grad * vec_row[4:5, :WIDTH]
        inside = (s * ROWS + step * 64 + lax.broadcasted_iota(jnp.int32, (64, 1), 0)) < len_ref[0]
        base = jnp.where(inside, cot_ref[rows, :].astype(F32), 0.0)
        total = base + inverse * (scaled - unit * jnp.mean(scaled * unit, axis=-1, keepdims=True))
        ig_ref[rows, :] = total
        grad_low[rows, :] = total.astype(BF16)
        return carry

    lax.fori_loop(0, ROWS // 64, middle_back, 0)

    def mixed_back(member, carry):
        gmix_out[member] = dot_nt(mats["o"][tile(member, MINE), :], grad_low[...]).astype(BF16)
        return carry

    lax.fori_loop(0, 4, mixed_back, 0)
    for k, device in ((2, y_dev), (3, yc_dev), (1, core_dev)):
        send(("gm", k), gmix_out.at[peers[k]], gmix_in.at[s], device)
    gmix_in[s] = gmix_out[s]
    scatter_far("h")
    links.sent(*[("h", "c", k) for k in range(4)], *[("h", "z", k) for k in (1, 2, 3)])
    links.sent(*[("h", kind, k) for kind in "nf" for k in range(4)], ("h", "f", 4))
    mixed_flat = mix_in.reshape(WIDTH, ROWS)
    weight_grad("o", lambda j, right: dot_nn(mixed_flat[tile(j, 256), :], right))
    scatter_core("o")
    scatter_near("b")
    recv(("gm", 1), ("gm", 2), ("gm", 3))
    scatter_far("o")

    def attend_back(h):
        rows = slice(HEAD_DIM * h, HEAD_DIM * (h + 1))
        dk_acc[...] = jnp.zeros_like(dk_acc)
        dv_acc[...] = jnp.zeros_like(dv_acc)
        for i in range(4):
            low, high = i * ROWS, (i + 1) * ROWS
            query = queries_t[rows, low:high]
            grad = gmix_in[i, rows, :]
            log_total = lse[h, :, low:high]
            spans = [(0, low), (low, high)] if i else [(low, high)]
            held = []
            inner = jnp.zeros((1, ROWS), F32)
            for first, last in spans:
                scores = dot_nn(keys[h, first:last, :], query)
                if first == low:
                    scores = jnp.where(allowed, scores, masked_score)
                probs = jnp.exp(scores - log_total)
                grad_probs = dot_nn(vals[h, first:last, :], grad)
                inner += jnp.sum(probs * grad_probs, axis=0, keepdims=True)
                held.append((first, last, probs, grad_probs))
            grad_query = jnp.zeros((HEAD_DIM, ROWS), F32)
            for first, last, probs, grad_probs in held:
                grad_scores = (probs * (grad_probs - inner)).astype(BF16)
                grad_query += dot_nn(keys_t[rows, first:last], grad_scores)
                dk_acc[first:last, :] += dot_nt(grad_scores, query)
                dv_acc[first:last, :] += dot_nt(probs.astype(BF16), grad)
            dq_t[rows, low:high] = grad_query
        grads[:, MINE + HEAD_DIM * h : MINE + HEAD_DIM * (h + 1)] = dk_acc[...].astype(BF16)
        grads[:, 2 * MINE + HEAD_DIM * h : 2 * MINE + HEAD_DIM * (h + 1)] = dv_acc[...].astype(BF16)

    attend_back(0)
    scatter_near("h")
    attend_back(1)
    scatter_z("b")
    attend_back(2)
    scatter_near("o")
    attend_back(3)
    scatter_z("h")
    grads[:, 3 * MINE :] = jnp.zeros((SLOTS, PACK - 3 * MINE), BF16)
    bias_grad = jnp.zeros((1, MINE), F32)
    scale_grad = jnp.zeros((1, MINE), F32)
    value_grad = jnp.zeros((1, MINE), F32)
    for i in range(4):
        rows = slice(i * ROWS, (i + 1) * ROWS)
        grad = dq_t[:, rows].T
        low_grad = (grad * scale).astype(BF16)
        grads[rows, 0:MINE] = low_grad
        bias_grad += jnp.sum(low_grad.astype(F32), axis=0, keepdims=True)
        scale_grad += jnp.sum(grad * queries_n[i].astype(F32), axis=0, keepdims=True)
        value_grad += jnp.sum(grads[rows, 2 * MINE : 3 * MINE].astype(F32), axis=0, keepdims=True)
    scale_grad = scale_grad / scale * jax.nn.sigmoid(query_log) * factor
    for row, value in ((1, bias_grad), (2, scale_grad), (3, value_grad)):
        vec_part[row : row + 1, :] = jnp.concatenate(
            [jnp.where(s == member, value, 0.0) for member in range(4)], axis=1
        )

    flat = qkv_part.reshape(WIDTH, PACK)

    def qkv_grad(j, carry):
        total = jnp.zeros((256, PACK), F32)
        for i in range(4):
            total += dot_tn(tokens[i, :, tile(j, 256)], grads[i * ROWS : (i + 1) * ROWS, :])
        flat[tile(j, 256), :] = total.astype(BF16)
        return carry

    lax.fori_loop(0, 5, qkv_grad, 0)
    for k in (1, 2, 3):
        send(("px", k), qkv_part.at[zs[k], 1 - x], qkv_near.at[k], x_dev)
    send(("px", 0), qkv_part.at[z, 1 - x], qkv_near.at[0], x_dev)

    def unit_grad(j, carry):
        cols = tile(j, 256)
        for i in range(4):
            tokens[i, :, cols] = dot_nt(grads[i * ROWS : (i + 1) * ROWS, :], weights[cols, :]).astype(BF16)
        return carry

    links.sent("xy", "xc")
    lax.fori_loop(0, 5, unit_grad, 0)
    for far in (1, 0):
        member = (y if far == 0 else 1 - y) * 2 + (1 - c)
        send(("uc", far), tokens.at[member], unit_core.at[far], core_dev)
    recv(("uc", 1))
    far_member = (1 - y) * 2 + c
    tokens[far_member] = (tokens[far_member].astype(F32) + unit_core[1].astype(F32)).astype(BF16)
    send("uy", tokens.at[far_member], unit_far, y_dev)
    recv(("uc", 0))
    scatter_z("o")
    for k in (1, 2, 3):
        recv(("px", k))
        qkv_part[zs[k], x] = (qkv_part[zs[k], x].astype(F32) + qkv_near[k].astype(F32)).astype(BF16)
        send(("pz", k), qkv_part.at[zs[k], x], qkv_last.at[k - 1], z_devs[k])
    scatter_sum("b")
    scatter_sum("h")
    recv("uy")

    def input_back(step, carry):
        rows = tile(step, 64)
        value = x_ref[rows, :].astype(F32)
        inverse = rms_inverse(value)
        unit = value * inverse
        grad = (
            tokens[s, rows, :].astype(F32) + unit_core[0, rows, :].astype(F32) + unit_far[rows, :].astype(F32)
        )
        vec_part[0:1, :] += jnp.sum(grad * unit, axis=0, keepdims=True)
        scaled = grad * vec_row[0:1, :WIDTH]
        ig_ref[rows, :] += inverse * (scaled - unit * jnp.mean(scaled * unit, axis=-1, keepdims=True))
        return carry

    lax.fori_loop(0, ROWS // 64, input_back, 0)
    send("sc", vec_part, vec_in.at[0], core_dev)
    recv("sc")
    links.sent("sc")
    vec_part[...] += vec_in[0]
    send("sy", vec_part, vec_in.at[1], y_dev)
    scatter_sum("o")
    recv("sy")
    links.sent("sy")
    vec_part[...] += vec_in[1]
    send("sx", vec_part, vec_in.at[2], x_dev)
    recv("sx")
    links.sent("sx")
    vec_part[...] += vec_in[2]
    for k in (1, 2, 3):
        send(("sz", k), vec_part, vec_in.at[2 + k], z_devs[k])
    recv(("px", 0))
    qkv_part[z, x] = (qkv_part[z, x].astype(F32) + qkv_near[0].astype(F32)).astype(BF16)
    recv(("pz", 1), ("pz", 2), ("pz", 3))
    total = qkv_part[z, x].astype(F32)
    for k in (1, 2, 3):
        total += qkv_last[k - 1].astype(F32)
    for member in range(4):
        qkv_sum[member] = total[SHARE * member : SHARE * (member + 1), :].astype(BF16)
    for k, device in ((2, y_dev), (3, yc_dev), (1, core_dev)):
        send(("ph", k), qkv_sum.at[peers[k]], qkv_home.at[s], device)
    qkv_home[s] = qkv_sum[s]
    recv(("sz", 1), ("sz", 2), ("sz", 3))
    total = vec_part[...] + vec_in[3] + vec_in[4] + vec_in[5]
    gvec_ref[...] = pltpu.roll(total, WIDTH - (d * 4 + s) * SHARE, 1)[:, :128]
    for m in "bho":
        scatter_done(m)
    recv(("ph", 1), ("ph", 2), ("ph", 3))
    for index, ref in enumerate((gq_ref, gk_ref, gv_ref)):
        for member in range(4):
            ref[:, MINE * member : MINE * (member + 1)] = qkv_home[
                member, :, MINE * index : MINE * (index + 1)
            ].astype(F32)
    links.sent_all()
    for i in range(4):

        @pl.when(s != i)
        def _():
            mix_copy(i, s).wait_send()


def fused_shards(
    inputs,
    lengths,
    cotangent,
    gain_attn,
    w_query,
    bias_query,
    query_scale,
    w_key,
    w_value,
    bias_value,
    w_out,
    gain_mlp,
    w_hidden,
    w_back,
):
    rows = jnp.stack([gain_attn, bias_query, query_scale, bias_value, gain_mlp]).astype(F32)
    vectors = jnp.pad(rows, ((0, 3), (0, 128 - SHARE)))
    vmem = pl.BlockSpec(memory_space=pltpu.VMEM)
    whole = (4, 8 * SHARE, WIDTH)
    buffers = [
        (whole, BF16),
        (whole, BF16),
        (whole, BF16),
        (whole, BF16),
        ((3, 4, 2, 2, 2 * SHARE, WIDTH // 2), BF16),
        ((3, 2, 4, 2 * SHARE, WIDTH // 2), BF16),
        ((3, 4, 2 * SHARE, WIDTH // 2), BF16),
        ((3, 3, 2 * SHARE, WIDTH // 2), BF16),
        ((8, 4 * SHARE, PACK), BF16),
        ((4, SHARE, PACK), BF16),
        ((4, ROWS, WIDTH), BF16),
        ((GROUP_HEADS, SLOTS, HEAD_DIM), BF16),
        ((GROUP_HEADS, SLOTS, HEAD_DIM), BF16),
        ((MINE, SLOTS), BF16),
        ((MINE, SLOTS), BF16),
        ((MINE, SLOTS), BF16),
        ((4, ROWS, MINE), BF16),
        ((GROUP_HEADS, 1, SLOTS), F32),
        ((4, MINE, ROWS), BF16),
        ((4, MINE, ROWS), BF16),
        ((ROWS, WIDTH), BF16),
        ((ROWS, WIDTH), F32),
        ((ROWS, WIDTH), F32),
        ((ROWS, WIDTH), BF16),
        ((ROWS, WIDTH), BF16),
        ((4, MINE, ROWS), BF16),
        ((4, MINE, ROWS), BF16),
        ((ROWS, WIDTH), BF16),
        ((SLOTS, HEAD_DIM), F32),
        ((SLOTS, HEAD_DIM), F32),
        ((MINE, SLOTS), F32),
        ((SLOTS, PACK), BF16),
        ((2, ROWS, WIDTH), BF16),
        ((ROWS, WIDTH), BF16),
        ((4, 2, 4 * SHARE, PACK), BF16),
        ((4, 4 * SHARE, PACK), BF16),
        ((3, 4 * SHARE, PACK), BF16),
        ((4, SHARE, PACK), BF16),
        ((4, SHARE, PACK), BF16),
        ((4, 2, 2, 2, 8, 128), F32),
        ((8, WIDTH + 128), F32),
        ((8, WIDTH), F32),
        ((6, 8, WIDTH), F32),
        ((4, SHARE, PACK), BF16),
        ((3, 2, SHARE, WIDTH // 2), BF16),
        ((3, SHARE, WIDTH // 2), F32),
        ((3, SHARE, WIDTH // 2), F32),
    ]
    scratch = [pltpu.VMEM(shape, kind) for shape, kind in buffers]
    scratch += [pltpu.SemaphoreType.DMA((4,)), pltpu.SemaphoreType.DMA((4,))]
    scratch += [pltpu.SemaphoreType.DMA((128,)), pltpu.SemaphoreType.DMA((128,))]
    square = jax.ShapeDtypeStruct((SHARE, WIDTH), F32)
    results = pl.pallas_call(
        layer_kernel,
        out_shape=(
            jax.ShapeDtypeStruct((ROWS, WIDTH), BF16),
            jax.ShapeDtypeStruct((ROWS, WIDTH), F32),
            jax.ShapeDtypeStruct((8, 128), F32),
            square,
            square,
            square,
            square,
            square,
            square,
        ),
        in_specs=[vmem, pl.BlockSpec(memory_space=pltpu.SMEM)] + [vmem] * 8,
        out_specs=tuple([vmem] * 9),
        scratch_shapes=scratch,
        compiler_params=pltpu.CompilerParams(
            collective_id=0, has_side_effects=True, vmem_limit_bytes=66 * 1000 * 1000
        ),
        cost_estimate=pl.CostEstimate(flops=25_000_000_000, bytes_accessed=10_000_000, transcendentals=10_000_000),
    )(
        inputs.reshape(ROWS, WIDTH),
        lengths,
        cotangent.reshape(ROWS, WIDTH),
        vectors,
        w_query,
        w_key,
        w_value,
        w_out,
        w_hidden,
        w_back,
    )
    out, input_grad, gvec, gq, gk, gv, go, gh, gb = results
    return (
        out.reshape(inputs.shape),
        input_grad.reshape(inputs.shape),
        gvec[0, :SHARE],
        gq,
        gvec[1, :SHARE],
        gvec[2, :SHARE],
        gk,
        gv,
        gvec[3, :SHARE],
        go,
        gvec[4, :SHARE],
        gh,
        gb,
    )


def solution(mesh):
    placed = (
        P("dp", "seq", None),
        P("dp"),
        P("dp", "seq", None),
        P(("dp", "seq")),
        P(("dp", "seq"), None),
        P(("dp", "seq")),
        P(("dp", "seq")),
        P(("dp", "seq"), None),
        P(("dp", "seq"), None),
        P(("dp", "seq")),
        P(("dp", "seq"), None),
        P(("dp", "seq")),
        P(("dp", "seq"), None),
        P(("dp", "seq"), None),
    )
    return jax.shard_map(
        fused_shards if fits(mesh) else shards,
        mesh=mesh,
        in_specs=placed,
        out_specs=(
            P("dp", "seq", None),
            P("dp", "seq", None),
            P(("dp", "seq")),
            P(("dp", "seq"), None),
            P(("dp", "seq")),
            P(("dp", "seq")),
            P(("dp", "seq"), None),
            P(("dp", "seq"), None),
            P(("dp", "seq")),
            P(("dp", "seq"), None),
            P(("dp", "seq")),
            P(("dp", "seq"), None),
            P(("dp", "seq"), None),
        ),
        check_vma=False,
    )
```

```python
import math

import jax
import jax.numpy as jnp
from jax import lax
from jax.experimental import pallas as pl
from jax.experimental.pallas import tpu as pltpu
from jax.sharding import PartitionSpec as P

HEADS = 16
HEAD_DIM = 80


query_gain = 1.442695041
masked_score = -1e30


def normed(values):
    squares = jnp.mean(values * values, axis=-1, keepdims=True)
    inverse = lax.rsqrt(squares + 1e-06)
    return (values * inverse, inverse)


def norm_back(grad_in, unit, inverse, gain):
    scaled = grad_in * gain
    return inverse * (scaled - unit * jnp.mean(scaled * unit, axis=-1, keepdims=True))


def row_product(left, right):
    return lax.dot_general(
        left, right, (((0,), (0,)), ((), ())), preferred_element_type=jnp.float32
    )


def back_product(left, right):
    return lax.dot_general(
        left, right, (((1,), (1,)), ((), ())), preferred_element_type=jnp.float32
    )


def shards(
    inputs,
    lengths,
    cotangent,
    gain_attn,
    w_query,
    bias_query,
    query_scale,
    w_key,
    w_value,
    bias_value,
    w_out,
    gain_mlp,
    w_hidden,
    w_back,
):
    seq_dev, group_rows, width = inputs.shape
    tok_rows = seq_dev * group_rows
    head_count = HEADS
    head_width = HEAD_DIM
    gathered = (
        lax.all_gather(gain_attn, ("dp", "seq"), axis=0, tiled=True),
        lax.all_gather(w_query, ("dp", "seq"), axis=0, tiled=True),
        lax.all_gather(bias_query, ("dp", "seq"), axis=0, tiled=True),
        lax.all_gather(query_scale, ("dp", "seq"), axis=0, tiled=True),
        lax.all_gather(w_key, ("dp", "seq"), axis=0, tiled=True),
        lax.all_gather(w_value, ("dp", "seq"), axis=0, tiled=True),
        lax.all_gather(bias_value, ("dp", "seq"), axis=0, tiled=True),
        lax.all_gather(w_out, ("dp", "seq"), axis=0, tiled=True),
        lax.all_gather(gain_mlp, ("dp", "seq"), axis=0, tiled=True),
        lax.all_gather(w_hidden, ("dp", "seq"), axis=0, tiled=True),
        lax.all_gather(w_back, ("dp", "seq"), axis=0, tiled=True),
    )
    (
        norm_one,
        query_mat,
        query_bias,
        query_log,
        key_mat,
        value_mat,
        value_bias,
        output_mat,
        norm_two,
        hidden_mat,
        back_mat,
    ) = gathered
    ff_width = hidden_mat.shape[1]
    offset = lax.axis_index("seq") * group_rows
    place = offset + jnp.arange(group_rows, dtype=jnp.int32)
    valid = place[None, :] < lengths[:, None]
    row_valid = valid.reshape(tok_rows, 1)
    inputs_rows = inputs.reshape(tok_rows, width).astype(jnp.float32)
    unit_one, inverse_one = normed(inputs_rows)
    gain_one = norm_one.astype(jnp.float32)
    normed_one = (unit_one * gain_one).astype(jnp.bfloat16)
    query_raw = jnp.dot(
        normed_one, query_mat, preferred_element_type=jnp.float32
    ) + query_bias.astype(jnp.float32)
    query_logf = query_log.astype(jnp.float32)
    scale_vec = jax.nn.softplus(query_logf) * (query_gain / math.sqrt(head_width))
    queries = (query_raw * scale_vec).astype(jnp.bfloat16)
    keys_local = jnp.dot(normed_one, key_mat, preferred_element_type=jnp.float32).astype(
        jnp.bfloat16
    )
    values_local = (
        jnp.dot(normed_one, value_mat, preferred_element_type=jnp.float32)
        + value_bias.astype(jnp.float32)
    ).astype(jnp.bfloat16)
    keys_three = keys_local.reshape(seq_dev, group_rows, width)
    values_three = values_local.reshape(seq_dev, group_rows, width)
    queries_three = queries.reshape(seq_dev, group_rows, width)
    keys_all, values_all = (
        lax.all_gather(keys_three, "seq", axis=1, tiled=True),
        lax.all_gather(values_three, "seq", axis=1, tiled=True),
    )
    seq_slots = keys_all.shape[1]
    key_place = jnp.arange(seq_slots, dtype=jnp.int32)
    allowed = key_place[None, :] <= place[:, None]

    def attend(pieces):
        query_block, key_block, value_block = pieces
        query_heads = query_block.reshape(group_rows, head_count, head_width)
        key_heads = key_block.reshape(seq_slots, head_count, head_width)
        value_heads = value_block.reshape(seq_slots, head_count, head_width)
        scores = jnp.einsum(
            "qhd,khd->hqk", query_heads, key_heads, preferred_element_type=jnp.float32
        )
        scores = jnp.where(allowed[None], scores, masked_score)
        largest = jnp.max(scores, axis=-1, keepdims=True)
        raised = jnp.exp(scores - largest)
        totals = jnp.sum(raised, axis=-1, keepdims=True)
        weights_soft = (raised / totals).astype(jnp.bfloat16)
        mixed = jnp.einsum(
            "hqk,khd->qhd", weights_soft, value_heads, preferred_element_type=jnp.float32
        )
        log_total = largest[..., 0] + jnp.log(totals[..., 0])
        return (mixed.reshape(group_rows, width).astype(jnp.bfloat16), log_total)

    mixed_three, log_totals = lax.map(attend, (queries_three, keys_all, values_all))
    mixed = mixed_three.reshape(tok_rows, width)
    middle = inputs_rows + jnp.dot(mixed, output_mat, preferred_element_type=jnp.float32)
    unit_two, inverse_two = normed(middle)
    gain_two = norm_two.astype(jnp.float32)
    normed_two = (unit_two * gain_two).astype(jnp.bfloat16)
    hidden = jnp.dot(normed_two, hidden_mat, preferred_element_type=jnp.float32)
    active = jax.nn.silu(hidden).astype(jnp.bfloat16)
    result = middle + jnp.dot(active, back_mat, preferred_element_type=jnp.float32)
    outputs = (
        jnp.where(row_valid, result, 0.0).astype(jnp.bfloat16).reshape(seq_dev, group_rows, width)
    )
    again = (
        lax.all_gather(gain_attn, ("dp", "seq"), axis=0, tiled=True),
        lax.all_gather(w_query, ("dp", "seq"), axis=0, tiled=True),
        lax.all_gather(w_key, ("dp", "seq"), axis=0, tiled=True),
        lax.all_gather(w_value, ("dp", "seq"), axis=0, tiled=True),
        lax.all_gather(w_out, ("dp", "seq"), axis=0, tiled=True),
        lax.all_gather(gain_mlp, ("dp", "seq"), axis=0, tiled=True),
        lax.all_gather(w_hidden, ("dp", "seq"), axis=0, tiled=True),
        lax.all_gather(w_back, ("dp", "seq"), axis=0, tiled=True),
    )
    norm_one, query_mat, key_mat, value_mat, output_mat, norm_two, hidden_mat, back_mat = again
    gain_one = norm_one.astype(jnp.float32)
    gain_two = norm_two.astype(jnp.float32)
    keys_back, values_back = (
        lax.all_gather(keys_three, "seq", axis=1, tiled=True),
        lax.all_gather(values_three, "seq", axis=1, tiled=True),
    )
    cot_rows = cotangent.reshape(tok_rows, width)
    grad_out = jnp.where(row_valid, cot_rows, jnp.zeros_like(cot_rows))
    grad_active = back_product(grad_out, back_mat)
    sigma = jax.nn.sigmoid(hidden)
    grad_hidden = (grad_active * sigma * (1.0 + hidden * (1.0 - sigma))).astype(jnp.bfloat16)
    grad_normed_two = back_product(grad_hidden, hidden_mat)
    grad_gain_two = jnp.sum(grad_normed_two * unit_two, axis=0)
    grad_middle = grad_out.astype(jnp.float32) + norm_back(
        grad_normed_two, unit_two, inverse_two, gain_two
    )
    grad_middle_low = grad_middle.astype(jnp.bfloat16)
    grad_mixed = back_product(grad_middle_low, output_mat).astype(jnp.bfloat16)
    grad_mixed_three = grad_mixed.reshape(seq_dev, group_rows, width)

    def attend_query(pieces):
        query_block, key_block, value_block, grad_block, log_total = pieces
        query_heads = query_block.reshape(group_rows, head_count, head_width)
        key_heads = key_block.reshape(seq_slots, head_count, head_width)
        value_heads = value_block.reshape(seq_slots, head_count, head_width)
        grad_heads = grad_block.reshape(group_rows, head_count, head_width)
        scores = jnp.einsum(
            "qhd,khd->hqk", query_heads, key_heads, preferred_element_type=jnp.float32
        )
        scores = jnp.where(allowed[None], scores, masked_score)
        weights_soft = jnp.exp(scores - log_total[..., None])
        grad_soft = jnp.einsum(
            "qhd,khd->hqk", grad_heads, value_heads, preferred_element_type=jnp.float32
        )
        inner = jnp.sum(weights_soft * grad_soft, axis=-1, keepdims=True)
        grad_scores = (weights_soft * (grad_soft - inner)).astype(jnp.bfloat16)
        grad_queries = jnp.einsum(
            "hqk,khd->qhd", grad_scores, key_heads, preferred_element_type=jnp.float32
        )
        return (grad_queries.reshape(group_rows, width), inner[..., 0])

    grad_queries, inner_rows = lax.map(
        attend_query, (queries_three, keys_back, values_back, grad_mixed_three, log_totals)
    )
    queries_every, grad_every = (
        lax.all_gather(queries_three, "seq", axis=1, tiled=True),
        lax.all_gather(grad_mixed_three, "seq", axis=1, tiled=True),
    )
    lse_every, inner_every = (
        lax.all_gather(log_totals, "seq", axis=2, tiled=True),
        lax.all_gather(inner_rows, "seq", axis=2, tiled=True),
    )
    later = key_place[:, None] >= place[None, :]

    def key_side(pieces):
        query_block, grad_block, key_block, value_block, lse_block, inner_block = pieces
        query_heads = query_block.reshape(seq_slots, head_count, head_width)
        grad_heads = grad_block.reshape(seq_slots, head_count, head_width)
        key_heads = key_block.reshape(group_rows, head_count, head_width)
        value_heads = value_block.reshape(group_rows, head_count, head_width)
        scores = jnp.einsum(
            "qhd,khd->hqk", query_heads, key_heads, preferred_element_type=jnp.float32
        )
        scores = jnp.where(later[None], scores, masked_score)
        weights_soft = jnp.exp(scores - lse_block[..., None])
        weights_low = weights_soft.astype(jnp.bfloat16)
        grad_soft = jnp.einsum(
            "qhd,khd->hqk", grad_heads, value_heads, preferred_element_type=jnp.float32
        )
        grad_scores = (weights_soft * (grad_soft - inner_block[..., None])).astype(jnp.bfloat16)
        grad_keys = jnp.einsum(
            "hqk,qhd->khd", grad_scores, query_heads, preferred_element_type=jnp.float32
        )
        grad_values = jnp.einsum(
            "hqk,qhd->khd", weights_low, grad_heads, preferred_element_type=jnp.float32
        )
        return (grad_keys.reshape(group_rows, width), grad_values.reshape(group_rows, width))

    grad_keys_sum, grad_values_sum = lax.map(
        key_side, (queries_every, grad_every, keys_three, values_three, lse_every, inner_every)
    )
    grad_keys = grad_keys_sum.reshape(tok_rows, width).astype(jnp.bfloat16)
    grad_values = grad_values_sum.reshape(tok_rows, width).astype(jnp.bfloat16)
    grad_queries = grad_queries.reshape(tok_rows, width)
    grad_query_raw = (grad_queries * scale_vec).astype(jnp.bfloat16)
    grad_scale = jnp.sum(grad_queries * query_raw, axis=0)
    grad_query_log = grad_scale * jax.nn.sigmoid(query_logf) * (query_gain / math.sqrt(head_width))
    grad_query_bias = jnp.sum(grad_query_raw.astype(jnp.float32), axis=0)
    grad_value_bias = jnp.sum(grad_values.astype(jnp.float32), axis=0)
    grad_normed_one = (
        back_product(grad_query_raw, query_mat)
        + back_product(grad_keys, key_mat)
        + back_product(grad_values, value_mat)
    )
    grad_gain_one = jnp.sum(grad_normed_one * unit_one, axis=0)
    input_grad = grad_middle + norm_back(grad_normed_one, unit_one, inverse_one, gain_one)
    dp_count = lax.axis_size("dp")
    seq_count = lax.axis_size("seq")
    share = width // (dp_count * seq_count)
    share_ff = ff_width // (dp_count * seq_count)
    left_parts = (
        lax.all_to_all(
            normed_one.reshape(tok_rows, dp_count, seq_count, share),
            "seq",
            split_axis=2,
            concat_axis=0,
            tiled=True,
        ),
        lax.all_to_all(
            mixed.reshape(tok_rows, dp_count, seq_count, share),
            "seq",
            split_axis=2,
            concat_axis=0,
            tiled=True,
        ),
        lax.all_to_all(
            normed_two.reshape(tok_rows, dp_count, seq_count, share),
            "seq",
            split_axis=2,
            concat_axis=0,
            tiled=True,
        ),
        lax.all_to_all(
            active.reshape(tok_rows, dp_count, seq_count, share_ff),
            "seq",
            split_axis=2,
            concat_axis=0,
            tiled=True,
        ),
    )
    left_normed_one = left_parts[0].reshape(-1, dp_count * share)
    left_mixed = left_parts[1].reshape(-1, dp_count * share)
    left_normed_two = left_parts[2].reshape(-1, dp_count * share)
    left_active = left_parts[3].reshape(-1, dp_count * share_ff)
    right_parts = (
        lax.all_gather(grad_query_raw, "seq", axis=0, tiled=True),
        lax.all_gather(grad_keys, "seq", axis=0, tiled=True),
        lax.all_gather(grad_values, "seq", axis=0, tiled=True),
        lax.all_gather(grad_middle_low, "seq", axis=0, tiled=True),
        lax.all_gather(grad_hidden, "seq", axis=0, tiled=True),
        lax.all_gather(grad_out, "seq", axis=0, tiled=True),
    )
    right_query, right_keys, right_values, right_middle, right_hidden, right_out = right_parts
    part_query_mat = row_product(left_normed_one, right_query)
    part_key_mat = row_product(left_normed_one, right_keys)
    part_value_mat = row_product(left_normed_one, right_values)
    part_output_mat = row_product(left_mixed, right_middle)
    part_hidden_mat = row_product(left_normed_two, right_hidden)
    part_back_mat = row_product(left_active, right_out)
    matrices = (
        lax.psum_scatter(
            part_query_mat.astype(jnp.bfloat16), "dp", scatter_dimension=0, tiled=True
        ).astype(jnp.float32),
        lax.psum_scatter(
            part_key_mat.astype(jnp.bfloat16), "dp", scatter_dimension=0, tiled=True
        ).astype(jnp.float32),
        lax.psum_scatter(
            part_value_mat.astype(jnp.bfloat16), "dp", scatter_dimension=0, tiled=True
        ).astype(jnp.float32),
        lax.psum_scatter(
            part_output_mat.astype(jnp.bfloat16), "dp", scatter_dimension=0, tiled=True
        ).astype(jnp.float32),
        lax.psum_scatter(
            part_hidden_mat.astype(jnp.bfloat16), "dp", scatter_dimension=0, tiled=True
        ).astype(jnp.float32),
        lax.psum_scatter(
            part_back_mat.astype(jnp.bfloat16), "dp", scatter_dimension=0, tiled=True
        ).astype(jnp.float32),
    )
    vectors = (
        lax.psum_scatter(grad_gain_one, ("dp", "seq"), scatter_dimension=0, tiled=True),
        lax.psum_scatter(grad_query_bias, ("dp", "seq"), scatter_dimension=0, tiled=True),
        lax.psum_scatter(grad_query_log, ("dp", "seq"), scatter_dimension=0, tiled=True),
        lax.psum_scatter(grad_value_bias, ("dp", "seq"), scatter_dimension=0, tiled=True),
        lax.psum_scatter(grad_gain_two, ("dp", "seq"), scatter_dimension=0, tiled=True),
    )
    return (
        outputs,
        input_grad.reshape(seq_dev, group_rows, width),
        vectors[0],
        matrices[0],
        vectors[1],
        vectors[2],
        matrices[1],
        matrices[2],
        vectors[3],
        matrices[3],
        vectors[4],
        matrices[4],
        matrices[5],
    )


F32 = jnp.float32
BF16 = jnp.bfloat16
MESH_ID = pl.DeviceIdType.MESH
ROWS = 256
WIDTH = 1280
SHARE = 40
MINE = 320
SLOTS = 1024
PACK = 512
PAIR = 160
COPIES = 144


def fits(mesh):
    return mesh.shape["dp"] == 8 and mesh.shape["seq"] == 4


def dot_nn(left, right):
    return jnp.dot(left, right, preferred_element_type=F32)


def dot_nt(left, right):
    return lax.dot_general(left, right, (((1,), (1,)), ((), ())), preferred_element_type=F32)


def dot_tn(left, right):
    return lax.dot_general(left, right, (((0,), (0,)), ((), ())), preferred_element_type=F32)


def tile(index, size):
    return pl.ds(pl.multiple_of(index * size, size), size)


def strip(yy):
    return pl.ds(pl.multiple_of(yy * 2 * SHARE, 16), 2 * SHARE)


def half(cc):
    return pl.ds(pl.multiple_of(cc * (WIDTH // 2), 128), WIDTH // 2)


class Links:
    def __init__(self, send_sems, recv_sems):
        self.send_sems, self.recv_sems = send_sems, recv_sems
        self.count = 0
        self.open = {}

    def send(self, key, src, dst, device):
        index = self.count
        assert index < COPIES
        self.count += 1
        copy = pltpu.make_async_remote_copy(
            src_ref=src,
            dst_ref=dst,
            send_sem=self.send_sems.at[index],
            recv_sem=self.recv_sems.at[index],
            device_id=device,
            device_id_type=MESH_ID,
        )
        copy.start()
        self.open[key] = copy

    def recv(self, *keys):
        for key in keys:
            self.open[key].wait_recv()

    def sent(self, *keys):
        for key in keys:
            self.open.pop(key).wait_send()

    def sent_of(self, name):
        for key in list(self.open):
            if key[0] == name:
                self.open.pop(key).wait_send()

    def sent_all(self):
        for key in list(self.open):
            self.open.pop(key).wait_send()


def layer_kernel(
    x_ref,
    len_ref,
    cot_ref,
    vec_ref,
    wq_ref,
    wk_ref,
    wv_ref,
    wo_ref,
    wh_ref,
    wb_ref,
    out_ref,
    ig_ref,
    gvec_ref,
    gq_ref,
    gk_ref,
    gv_ref,
    go_ref,
    gh_ref,
    gb_ref,
    full_o,
    full_h,
    full_b,
    part_b,
    core_in,
    far_in,
    near_in,
    last_in,
    qkv_w,
    stage,
    tokens,
    keys,
    vals,
    queries_t,
    keys_t,
    vals_t,
    queries_n,
    lse,
    mix_out,
    mix_in,
    mix,
    middle,
    hidden,
    norm2,
    active,
    gmix_out,
    gmix_in,
    grad_low,
    dk_acc,
    dv_acc,
    dq_t,
    grads,
    unit_core,
    unit_far,
    qkv_part,
    qkv_near,
    qkv_last,
    qkv_home,
    qkv_sum,
    vec_slots,
    vec_row,
    vec_part,
    vec_in,
    qkv_own,
    pair_in,
    give_out,
    give_in,
    mix_send,
    mix_recv,
    line_send,
    line_recv,
    send_sems,
    recv_sems,
):
    d = lax.axis_index("dp")
    s = lax.axis_index("seq")
    z, x = d // 2, d % 2
    y, c = s // 2, s % 2
    links = Links(send_sems, recv_sems)
    send, recv = links.send, links.recv
    core_dev = (d, y * 2 + (1 - c))
    y_dev = (d, (1 - y) * 2 + c)
    yc_dev = (d, (1 - y) * 2 + (1 - c))
    x_dev = (z * 2 + (1 - x), s)
    zs = [None] + [(z + k) % 4 for k in range(1, 4)]
    from_z = [None] + [(z + 4 - k) % 4 for k in range(1, 4)]
    z_devs = [None] + [(zs[k] * 2 + x, s) for k in range(1, 4)]

    barrier = pltpu.get_barrier_semaphore()
    for device in (core_dev, y_dev, yc_dev, x_dev, z_devs[1], z_devs[2], z_devs[3]):
        pl.semaphore_signal(barrier, inc=1, device_id=device, device_id_type=MESH_ID)

    for member in range(4):
        for p in range(2):
            cols = slice(MINE * member + PAIR * p, MINE * member + PAIR * (p + 1))
            stage[p, member] = jnp.concatenate(
                [wq_ref[:, cols], wk_ref[:, cols], wv_ref[:, cols], jnp.zeros((SHARE, PACK - 3 * PAIR), BF16)],
                axis=1,
            )
    for p in range(2):
        qkv_own[p, s] = stage[p, s]
    tokens[s] = x_ref[...]
    vec_slots[y, x, z, c] = vec_ref[...]
    shards = {"o": wo_ref, "h": wh_ref, "b": wb_ref}
    slot_of = {"o": 0, "h": 1, "b": 2}
    for m in "ohb":
        pair_in[slot_of[m], c] = shards[m][:, half(c)]
    pl.semaphore_wait(barrier, 7)

    group = ((1, core_dev), (2, y_dev), (3, yc_dev))
    peers = (None, y * 2 + (1 - c), (1 - y) * 2 + c, (1 - y) * 2 + (1 - c))
    def to_group(p):
        for k, device in ((2, y_dev), (3, yc_dev), (1, core_dev)):
            send(("a2a", p, k), stage.at[p, peers[k]], qkv_own.at[p, s], device)

    fulls = {"o": full_o, "h": full_h, "b": full_b}
    first_x = {"o": 1, "h": 0, "b": 1 - c}
    far_x = {"b": 1 - c, "h": 1 - c, "o": c}

    def spot(along, first, second):
        on_x = along * first + (1 - along) * second
        on_y = along * second + (1 - along) * first
        return (x + on_x) % 2, strip((y + on_y) % 2)

    def devs_of(along):
        def device(on_x):
            return ((z * 2 + (x + on_x) % 2), ((y + 1 - on_x) % 2) * 2 + c)

        return device(along), device(1 - along)

    up_dev = (jnp.minimum(z + 1, 3) * 2 + x, s)
    down_dev = (jnp.maximum(z - 1, 0) * 2 + x, s)
    streams = [0, 1] + [(m, e) for m in "ohb" for e in (0, 1)]

    def line_piece(stream, zz, far):
        if stream in (0, 1):
            return qkv_w.at[stream, zz * 2 + (x + far) % 2]
        m, e = stream
        xx, rows = spot(first_x[m], e, far)
        return fulls[m].at[zz, xx, rows, half(c)]

    def line_copy(kind, stream, hop, zz, far=0):
        if kind == 2:
            device = x_dev if stream in (0, 1) else devs_of(first_x[stream[0]])[1]
        else:
            device = (up_dev, down_dev)[kind]
        index = streams.index(stream)
        piece = line_piece(stream, zz, far)
        return pltpu.make_async_remote_copy(
            src_ref=piece,
            dst_ref=piece,
            send_sem=line_send.at[kind, index, hop],
            recv_sem=line_recv.at[kind, index, hop],
            device_id=device,
            device_id_type=MESH_ID,
        )

    def line_far(stream, zz):
        line_copy(2, stream, zz, zz).start()

    def line_first(stream):
        @pl.when(z < 3)
        def _():
            line_copy(0, stream, 1, z).start()

        @pl.when(z > 0)
        def _():
            line_copy(1, stream, 1, z).start()

        line_far(stream, z)

    def line_step(stream, hop):
        @pl.when(z >= hop)
        def _():
            line_copy(0, stream, hop, z - hop).wait_recv()
            if hop < 3:

                @pl.when(z < 3)
                def _():
                    line_copy(0, stream, hop + 1, z - hop).start()

            line_far(stream, z - hop)

        @pl.when(z + hop <= 3)
        def _():
            line_copy(1, stream, hop, z + hop).wait_recv()
            if hop < 3:

                @pl.when(z > 0)
                def _():
                    line_copy(1, stream, hop + 1, z + hop).start()

            line_far(stream, z + hop)

    def line_done(stream):
        for zz in range(4):
            line_copy(2, stream, zz, zz, 1).wait_recv()

    def line_sent(stream):
        for hop in (1, 2, 3):

            @pl.when((z >= hop - 1) & (z < 3))
            def _():
                line_copy(0, stream, hop, z).wait_send()

            @pl.when((z + hop - 1 <= 3) & (z > 0))
            def _():
                line_copy(1, stream, hop, z).wait_send()

        for zz in range(4):
            line_copy(2, stream, zz, z).wait_send()

    def to_core(m, far):
        for e in (0, 1):
            xx, rows = spot(first_x[m], e, far)
            piece = fulls[m].at[:, xx, rows, half(c)]
            send((m, far, e), piece, piece, core_dev)

    def gather_side(m):
        to_core(m, 0)

    def gather_core(m):
        line_done((m, 0))
        line_done((m, 1))
        to_core(m, 1)

    def gather_done(m):
        recv(*[(m, far, e) for far in (0, 1) for e in (0, 1)])

    def own_rows(p):
        recv(*[("a2a", p, k) for k in (1, 2, 3)])
        qkv_w[p, d] = jnp.concatenate([qkv_own[p, member] for member in range(4)], axis=0)

    def own_first(m):
        recv(("pair", m))
        piece = jnp.concatenate([pair_in[slot_of[m], 0], pair_in[slot_of[m], 1]], axis=0)
        fulls[m][z, x, strip(y), half(c)] = piece
        mine = fulls[m].at[z, x, strip(y), half(c)]
        send((m, "first"), mine, mine, devs_of(first_x[m])[0])

    to_group(0)
    for m in "ohb":
        send(("pair", m), shards[m].at[:, half(1 - c)], pair_in.at[slot_of[m], c], core_dev)
    send("vy", vec_ref, vec_slots.at[y, x, z, c], y_dev)
    to_group(1)
    own_first("o")
    send("xy", x_ref, tokens.at[s], y_dev)
    send("xc", x_ref, tokens.at[s], core_dev)
    own_first("h")
    own_first("b")
    own_rows(0)
    line_first(0)
    recv("vy")
    piece = vec_slots.at[:, x, z, c]
    send("vx", piece, piece, x_dev)
    line_first(("o", 0))
    own_rows(1)
    recv("vx")
    for k in (1, 2, 3):
        piece = vec_slots.at[:, :, z, c]
        send(("vz", k), piece, piece, z_devs[k])
    line_step(0, 1)
    line_first(1)
    line_step(0, 2)
    recv(("vz", 1), ("vz", 2), ("vz", 3))
    piece = vec_slots.at[:, :, :, c]
    send("vc", piece, piece, core_dev)
    recv(("o", "first"))
    line_first(("o", 1))
    line_step(0, 3)
    line_step(1, 1)
    recv("vc")
    vec_row[...] = jnp.zeros_like(vec_row)
    for slot in range(32):
        start = slot * SHARE
        low = start // 128 * 128
        piece = jnp.concatenate(
            [vec_slots[slot // 2 % 2, slot // 4 % 2, slot // 8, slot % 2], jnp.zeros((8, 128), F32)], axis=1
        )
        if start > low:
            piece = pltpu.roll(piece, start - low, 1)
        vec_row[:, low : low + 256] += piece

    def norm_of(member, count):
        def norm_rows(step, carry):
            for j in range(count):
                rows = tile(step, 64)
                value = tokens[member + j, rows, :].astype(F32)
                unit = value * lax.rsqrt(jnp.mean(value * value, axis=-1, keepdims=True) + 1e-06)
                tokens[member + j, rows, :] = (unit * vec_row[0:1, :WIDTH]).astype(BF16)
            return carry

        lax.fori_loop(0, ROWS // 64, norm_rows, 0)

    recv("xc")
    norm_of(y * 2, 2)
    line_step(("o", 0), 1)
    recv("xy")
    piece = tokens.at[peers[2]]
    send("xyc", piece, piece, core_dev)
    line_step(1, 2)
    line_step(("o", 1), 1)
    recv("xyc")
    links.sent("xyc")
    norm_of((1 - y) * 2, 2)

    def own(row):
        value = vec_row[row : row + 1, 0:MINE]
        for member in range(1, 4):
            value = jnp.where(s == member, vec_row[row : row + 1, MINE * member : MINE * (member + 1)], value)
        return value

    query_log = own(2)
    factor = query_gain / math.sqrt(HEAD_DIM)
    scale = (jnp.maximum(query_log, 0.0) + jnp.log1p(jnp.exp(-jnp.abs(query_log)))) * factor
    query_bias, value_bias = own(1), own(3)

    weights = [qkv_w.at[p].reshape(WIDTH, PACK) for p in range(2)]

    def project_pair(p):
        lanes = slice(PAIR * p, PAIR * (p + 1))

        def project(i, carry):
            rows = tile(i, ROWS)
            raw = dot_nn(tokens[i], weights[p][...])
            query = ((raw[:, :PAIR] + query_bias[:, lanes]) * scale[:, lanes]).astype(BF16)
            key = raw[:, PAIR : 2 * PAIR].astype(BF16)
            val = (raw[:, 2 * PAIR : 3 * PAIR] + value_bias[:, lanes]).astype(BF16)
            queries_n[p, i] = query
            queries_t[lanes, rows] = query.T
            keys_t[lanes, rows] = key.T
            vals_t[lanes, rows] = val.T
            for h in range(2):
                keys[2 * p + h, rows, :] = key[:, HEAD_DIM * h : HEAD_DIM * (h + 1)]
                vals[2 * p + h, rows, :] = val[:, HEAD_DIM * h : HEAD_DIM * (h + 1)]
            return carry

        lax.fori_loop(0, 4, project, 0)

    key_place = lax.broadcasted_iota(jnp.int32, (ROWS, ROWS), 0)
    query_place = lax.broadcasted_iota(jnp.int32, (ROWS, ROWS), 1)
    allowed = key_place <= query_place

    def attend(p, i):
        low, high = i * ROWS, (i + 1) * ROWS

        def head(h, carry):
            rows = tile(h, HEAD_DIM)
            query = queries_t[rows, low:high]
            near = jnp.where(allowed, dot_nn(keys[h, low:high, :], query), masked_score)
            largest = jnp.max(near, axis=0, keepdims=True)
            if i:
                before = dot_nn(keys[h, 0:low, :], query)
                largest = jnp.maximum(largest, jnp.max(before, axis=0, keepdims=True))
            near = jnp.exp(near - largest)
            total = jnp.sum(near, axis=0, keepdims=True)
            mixed = dot_nn(vals_t[rows, low:high], near.astype(BF16))
            if i:
                before = jnp.exp(before - largest)
                total += jnp.sum(before, axis=0, keepdims=True)
                mixed += dot_nn(vals_t[rows, 0:low], before.astype(BF16))
            lse[h, :, low:high] = largest + jnp.log(total)
            mix_out[i, rows, :] = (mixed / total).astype(BF16)
            return carry

        lax.fori_loop(2 * p, 2 * p + 2, head, 0)

    def mix_copy(p, dest, source):
        return pltpu.make_async_remote_copy(
            src_ref=mix_out.at[dest, PAIR * p : PAIR * (p + 1)],
            dst_ref=mix_in.at[source, PAIR * p : PAIR * (p + 1)],
            send_sem=mix_send.at[p, dest],
            recv_sem=mix_recv.at[p, source],
            device_id=(d, dest),
            device_id_type=MESH_ID,
        )

    def attend_and_send(p, i):
        attend(p, i)

        @pl.when(s != i)
        def _():
            mix_copy(p, i, s).start()

        @pl.when(s == i)
        def _():
            mix_in[i, PAIR * p : PAIR * (p + 1)] = mix_out[i, PAIR * p : PAIR * (p + 1)]

    line_done(0)
    project_pair(0)
    line_step(1, 3)
    line_step(("o", 0), 2)
    attend_and_send(0, 3)
    recv(("h", "first"))
    line_first(("h", 0))
    line_step(("o", 1), 2)
    attend_and_send(0, 2)
    line_first(("h", 1))
    line_step(("o", 0), 3)
    attend_and_send(0, 1)
    line_step(("o", 1), 3)
    gather_side("o")
    attend_and_send(0, 0)
    line_step(("h", 0), 1)
    recv(("b", "first"))
    line_first(("b", 0))
    line_done(1)
    project_pair(1)
    line_step(("h", 1), 1)
    line_first(("b", 1))
    attend_and_send(1, 3)
    line_step(("h", 0), 2)
    line_step(("h", 1), 2)
    gather_core("o")
    attend_and_send(1, 2)
    line_step(("b", 0), 1)
    line_step(("b", 1), 1)
    attend_and_send(1, 1)
    line_step(("h", 0), 3)
    line_step(("h", 1), 3)
    attend_and_send(1, 0)
    gather_side("h")
    for p in range(2):
        for k in (1, 2, 3):
            mix_copy(p, peers[k], peers[k]).wait_recv()
    gather_done("o")

    mix[...] = mix_in[...].reshape(WIDTH, ROWS).T
    mats = {m: fulls[m].reshape(WIDTH, WIDTH) for m in "ohb"}

    def middle_step(j, carry):
        cols = tile(j, 256)
        middle[:, cols] = x_ref[:, cols].astype(F32) + dot_nn(mix[...], mats["o"][:, cols])
        return carry

    lax.fori_loop(0, 5, middle_step, 0)

    def rms_inverse(value):
        return lax.rsqrt(jnp.mean(value * value, axis=-1, keepdims=True) + 1e-06)

    def norm_two(step, carry):
        rows = tile(step, 64)
        value = middle[rows, :]
        norm2[rows, :] = (value * rms_inverse(value) * vec_row[4:5, :WIDTH]).astype(BF16)
        return carry

    lax.fori_loop(0, ROWS // 64, norm_two, 0)
    line_step(("b", 0), 2)
    line_step(("b", 1), 2)
    gather_core("h")
    gather_done("h")

    def hidden_step(j, carry):
        cols = tile(j, 256)
        value = dot_nn(norm2[...], mats["h"][:, cols])
        hidden[:, cols] = value
        active[:, cols] = (value * jax.nn.sigmoid(value)).astype(BF16)
        return carry

    lax.fori_loop(0, 5, hidden_step, 0)

    place = s * ROWS + lax.broadcasted_iota(jnp.int32, (ROWS, 1), 0)
    valid = place < len_ref[0]

    def grad_y():
        return jnp.where(valid, cot_ref[...], jnp.zeros((ROWS, WIDTH), BF16))

    parts = {"b": part_b, "h": full_b, "o": full_h}
    outs = {"b": gb_ref, "h": gh_ref, "o": go_ref}
    order = {"b": 0, "h": 1, "o": 2}

    def weight_grad(m, left):
        flat = parts[m].reshape(WIDTH, WIDTH)
        right = grad_y() if m == "b" else grad_low[...]

        def step(j, carry):
            flat[tile(j, 256), :] = left(j, right).astype(BF16)
            return carry

        lax.fori_loop(0, 5, step, 0)

    def part_at(m, far, near):
        xx, rows = spot(far_x[m], far, near)
        return parts[m].at[:, xx, rows, half(c)]

    def part_for_core(m, far, near):
        xx, rows = spot(1 - far_x[m], far, near)
        return parts[m].at[:, xx, rows, half(1 - c)]

    def core_at(m, far, near):
        return core_in.at[order[m], far, near]

    def add_into(target, other):
        def step(zz, carry):
            target[zz] = (target[zz].astype(F32) + other[zz].astype(F32)).astype(BF16)
            return carry

        lax.fori_loop(0, 4, step, 0)

    def grad_devs(m):
        return devs_of(far_x[m])

    def scatter_core(m):
        for far in (1, 0):
            for near in (1, 0):
                send(("gc", m, far, near), part_for_core(m, far, near), core_at(m, far, near), core_dev)

    def scatter_far(m):
        far_dev, near_dev = grad_devs(m)
        for near in (1, 0):
            recv(("gc", m, 1, near))
            add_into(part_at(m, 1, near), core_at(m, 1, near))
            send(("gf", m, near), part_at(m, 1, near), far_in.at[order[m], near], far_dev)
        for near in (1, 0):
            recv(("gc", m, 0, near))
            add_into(part_at(m, 0, near), core_at(m, 0, near))

    def scatter_near(m):
        far_dev, near_dev = grad_devs(m)
        recv(("gf", m, 1))
        add_into(part_at(m, 0, 1), far_in.at[order[m], 1])
        send(("gn", m), part_at(m, 0, 1), near_in.at[order[m]], near_dev)
        recv(("gf", m, 0))
        add_into(part_at(m, 0, 0), far_in.at[order[m], 0])

    def scatter_z(m):
        recv(("gn", m))
        add_into(part_at(m, 0, 0), near_in.at[order[m]])
        for k in (1, 2, 3):
            send(("gz", m, k), part_at(m, 0, 0).at[zs[k]], last_in.at[order[m], k - 1], z_devs[k])

    def scatter_sum(m):
        total = part_at(m, 0, 0)[z].astype(F32)
        for k in (1, 2, 3):
            recv(("gz", m, k))
            total += last_in[order[m], k - 1].astype(F32)
        outs[m][:, half(c)] = jnp.where(c == 0, total[:SHARE], total[SHARE:])
        give_out[order[m]] = jnp.where(c == 0, total[SHARE:], total[:SHARE])
        send(("give", m), give_out.at[order[m]], give_in.at[order[m]], core_dev)

    def scatter_done(m):
        recv(("give", m))
        outs[m][:, half(1 - c)] = give_in[order[m]]

    weight_grad("b", lambda j, right: dot_tn(active[:, tile(j, 256)], right))
    scatter_core("b")
    line_step(("b", 0), 3)
    line_step(("b", 1), 3)
    gather_side("b")
    gather_core("b")
    gather_done("b")
    scatter_far("b")

    def back_step(j, carry):
        cols = tile(j, 256)
        value = hidden[:, cols]
        sigma = jax.nn.sigmoid(value)
        grad = dot_nt(grad_y(), mats["b"][cols, :])
        grad_low[:, cols] = (grad * sigma * (1.0 + value * (1.0 - sigma))).astype(BF16)
        out_ref[:, cols] = jnp.where(
            valid, middle[:, cols] + dot_nn(active[...], mats["b"][:, cols]), 0.0
        ).astype(BF16)
        return carry

    lax.fori_loop(0, 5, back_step, 0)
    links.sent_of("b")
    line_sent(("b", 0))
    line_sent(("b", 1))
    weight_grad("h", lambda j, right: dot_tn(norm2[:, tile(j, 256)], right))
    scatter_core("h")

    def normed_step(j, carry):
        hidden[:, tile(j, 256)] = dot_nt(grad_low[...], mats["h"][tile(j, 256), :])
        return carry

    lax.fori_loop(0, 5, normed_step, 0)
    vec_part[...] = jnp.zeros_like(vec_part)

    def middle_back(step, carry):
        rows = tile(step, 64)
        value = middle[rows, :]
        inverse = rms_inverse(value)
        unit = value * inverse
        grad = hidden[rows, :]
        vec_part[4:5, :] += jnp.sum(grad * unit, axis=0, keepdims=True)
        scaled = grad * vec_row[4:5, :WIDTH]
        inside = (s * ROWS + step * 64 + lax.broadcasted_iota(jnp.int32, (64, 1), 0)) < len_ref[0]
        base = jnp.where(inside, cot_ref[rows, :].astype(F32), 0.0)
        total = base + inverse * (scaled - unit * jnp.mean(scaled * unit, axis=-1, keepdims=True))
        ig_ref[rows, :] = total
        grad_low[rows, :] = total.astype(BF16)
        return carry

    lax.fori_loop(0, ROWS // 64, middle_back, 0)

    def mixed_back(member, carry):
        gmix_out[member] = dot_nt(mats["o"][tile(member, MINE), :], grad_low[...]).astype(BF16)
        return carry

    lax.fori_loop(0, 4, mixed_back, 0)
    for p in range(2):
        for k, device in ((2, y_dev), (3, yc_dev), (1, core_dev)):
            rows = slice(PAIR * p, PAIR * (p + 1))
            send(("gm", p, k), gmix_out.at[peers[k], rows], gmix_in.at[s, rows], device)
    gmix_in[s] = gmix_out[s]
    scatter_far("h")
    links.sent_of("h")
    line_sent(("h", 0))
    line_sent(("h", 1))
    mixed_flat = mix_in.reshape(WIDTH, ROWS)
    weight_grad("o", lambda j, right: dot_nn(mixed_flat[tile(j, 256), :], right))
    scatter_core("o")
    scatter_near("b")

    def attend_back(h):
        rows = slice(HEAD_DIM * h, HEAD_DIM * (h + 1))
        dk_acc[...] = jnp.zeros_like(dk_acc)
        dv_acc[...] = jnp.zeros_like(dv_acc)
        for i in range(4):
            low, high = i * ROWS, (i + 1) * ROWS
            query = queries_t[rows, low:high]
            grad = gmix_in[i, rows, :]
            log_total = lse[h, :, low:high]
            spans = [(0, low), (low, high)] if i else [(low, high)]
            held = []
            inner = jnp.zeros((1, ROWS), F32)
            for first, last in spans:
                scores = dot_nn(keys[h, first:last, :], query)
                if first == low:
                    scores = jnp.where(allowed, scores, masked_score)
                probs = jnp.exp(scores - log_total)
                grad_probs = dot_nn(vals[h, first:last, :], grad)
                inner += jnp.sum(probs * grad_probs, axis=0, keepdims=True)
                held.append((first, last, probs, grad_probs))
            grad_query = jnp.zeros((HEAD_DIM, ROWS), F32)
            for first, last, probs, grad_probs in held:
                grad_scores = (probs * (grad_probs - inner)).astype(BF16)
                grad_query += dot_nn(keys_t[rows, first:last], grad_scores)
                dk_acc[first:last, :] += dot_nt(grad_scores, query)
                dv_acc[first:last, :] += dot_nt(probs.astype(BF16), grad)
            dq_t[rows, low:high] = grad_query
        first = PAIR + HEAD_DIM * (h % 2)
        grads[h // 2, :, first : first + HEAD_DIM] = dk_acc[...].astype(BF16)
        grads[h // 2, :, first + PAIR : first + PAIR + HEAD_DIM] = dv_acc[...].astype(BF16)

    def finish_pair(p):
        lanes = slice(PAIR * p, PAIR * (p + 1))
        pair_scale = scale[:, lanes]
        bias_grad = jnp.zeros((1, PAIR), F32)
        scale_grad = jnp.zeros((1, PAIR), F32)
        value_grad = jnp.zeros((1, PAIR), F32)
        grads[p, :, 3 * PAIR :] = jnp.zeros((SLOTS, PACK - 3 * PAIR), BF16)
        for i in range(4):
            rows = slice(i * ROWS, (i + 1) * ROWS)
            grad = dq_t[lanes, rows].T
            low_grad = (grad * pair_scale).astype(BF16)
            grads[p, rows, 0:PAIR] = low_grad
            bias_grad += jnp.sum(low_grad.astype(F32), axis=0, keepdims=True)
            scale_grad += jnp.sum(grad * queries_n[p, i].astype(F32), axis=0, keepdims=True)
            value_grad += jnp.sum(grads[p, rows, 2 * PAIR : 3 * PAIR].astype(F32), axis=0, keepdims=True)
        scale_grad = scale_grad / pair_scale * jax.nn.sigmoid(query_log[:, lanes]) * factor
        return bias_grad, scale_grad, value_grad

    def qkv_grad_pair(p):
        flat = qkv_part.at[p].reshape(WIDTH, PACK)

        def qkv_grad(j, carry):
            total = jnp.zeros((256, PACK), F32)
            for i in range(4):
                total += dot_tn(tokens[i, :, tile(j, 256)], grads[p, i * ROWS : (i + 1) * ROWS, :])
            flat[tile(j, 256), :] = total.astype(BF16)
            return carry

        lax.fori_loop(0, 5, qkv_grad, 0)
        for k in (1, 2, 3):
            send(("px", p, k), qkv_part.at[p, zs[k], 1 - x], qkv_near.at[p, k], x_dev)
        send(("px", p, 0), qkv_part.at[p, z, 1 - x], qkv_near.at[p, 0], x_dev)

    def qkv_z(p, k):
        recv(("px", p, k))
        qkv_part[p, zs[k], x] = (qkv_part[p, zs[k], x].astype(F32) + qkv_near[p, k].astype(F32)).astype(BF16)
        send(("pz", p, k), qkv_part.at[p, zs[k], x], qkv_last.at[p, k - 1], z_devs[k])

    def qkv_sum_pair(p):
        recv(("px", p, 0))
        total = qkv_part[p, z, x].astype(F32) + qkv_near[p, 0].astype(F32)
        for k in (1, 2, 3):
            recv(("pz", p, k))
            total += qkv_last[p, k - 1].astype(F32)
        for member in range(4):
            qkv_sum[p, member] = total[SHARE * member : SHARE * (member + 1), :].astype(BF16)
        for k, device in ((2, y_dev), (3, yc_dev), (1, core_dev)):
            send(("ph", p, k), qkv_sum.at[p, peers[k]], qkv_home.at[p, s], device)
        qkv_home[p, s] = qkv_sum[p, s]

    recv(("gm", 0, 1), ("gm", 0, 2), ("gm", 0, 3))
    attend_back(0)
    scatter_far("o")
    attend_back(1)
    pair_grads = [finish_pair(0)]
    qkv_grad_pair(0)
    recv(("gm", 1, 1), ("gm", 1, 2), ("gm", 1, 3))
    scatter_near("h")
    attend_back(2)
    scatter_z("b")
    qkv_z(0, 1)
    attend_back(3)
    qkv_z(0, 2)
    pair_grads.append(finish_pair(1))
    qkv_grad_pair(1)
    for row in range(3):
        value = jnp.concatenate([pair_grads[0][row], pair_grads[1][row]], axis=1)
        vec_part[row + 1 : row + 2, :] = jnp.concatenate(
            [jnp.where(s == member, value, 0.0) for member in range(4)], axis=1
        )

    def unit_rows(member):
        def unit_grad(j, carry):
            cols = tile(j, 256)
            value = dot_nt(grads[0, tile(member, ROWS), :], weights[0][cols, :])
            value += dot_nt(grads[1, tile(member, ROWS), :], weights[1][cols, :])
            tokens[member, :, cols] = value.astype(BF16)
            return carry

        lax.fori_loop(0, 5, unit_grad, 0)

    unit_rows((1 - y) * 2 + (1 - c))
    send(("uc", 1), tokens.at[(1 - y) * 2 + (1 - c)], unit_core.at[1], core_dev)
    far_member = (1 - y) * 2 + c
    unit_rows(far_member)
    recv(("uc", 1))
    tokens[far_member] = (tokens[far_member].astype(F32) + unit_core[1].astype(F32)).astype(BF16)
    send("uy", tokens.at[far_member], unit_far, y_dev)
    unit_rows(y * 2 + (1 - c))
    send(("uc", 0), tokens.at[y * 2 + (1 - c)], unit_core.at[0], core_dev)
    unit_rows(s)
    recv(("uc", 0))
    qkv_z(0, 3)
    scatter_near("o")
    scatter_z("h")
    scatter_sum("b")
    qkv_sum_pair(0)
    scatter_z("o")
    qkv_z(1, 1)
    scatter_sum("h")
    recv("uy")

    def input_back(step, carry):
        rows = tile(step, 64)
        value = x_ref[rows, :].astype(F32)
        inverse = rms_inverse(value)
        unit = value * inverse
        grad = (
            tokens[s, rows, :].astype(F32) + unit_core[0, rows, :].astype(F32) + unit_far[rows, :].astype(F32)
        )
        vec_part[0:1, :] += jnp.sum(grad * unit, axis=0, keepdims=True)
        scaled = grad * vec_row[0:1, :WIDTH]
        ig_ref[rows, :] += inverse * (scaled - unit * jnp.mean(scaled * unit, axis=-1, keepdims=True))
        return carry

    lax.fori_loop(0, ROWS // 64, input_back, 0)
    for k, device in ((2, y_dev), (3, yc_dev), (1, core_dev)):
        send(("sg", k), vec_part, vec_in.at[k - 1], device)
    qkv_z(1, 2)
    recv(("sg", 1), ("sg", 2), ("sg", 3))
    links.sent(("sg", 1), ("sg", 2), ("sg", 3))
    vec_part[...] += vec_in[0] + vec_in[1] + vec_in[2]
    send("sx", vec_part, vec_in.at[3], x_dev)
    qkv_z(1, 3)
    scatter_sum("o")
    recv("sx")
    links.sent("sx")
    vec_part[...] += vec_in[3]
    for k in (1, 2, 3):
        send(("sz", k), vec_part, vec_in.at[3 + k], z_devs[k])
    qkv_sum_pair(1)
    recv(("sz", 1), ("sz", 2), ("sz", 3))
    total = vec_part[...] + vec_in[4] + vec_in[5] + vec_in[6]
    gvec_ref[...] = pltpu.roll(total, WIDTH - (d * 4 + s) * SHARE, 1)[:, :128]
    for m in "bho":
        scatter_done(m)
    for p in range(2):
        recv(("ph", p, 1), ("ph", p, 2), ("ph", p, 3))
        for index, ref in enumerate((gq_ref, gk_ref, gv_ref)):
            for member in range(4):
                first = MINE * member + PAIR * p
                ref[:, first : first + PAIR] = qkv_home[
                    p, member, :, PAIR * index : PAIR * (index + 1)
                ].astype(F32)
    links.sent_all()
    line_sent(("o", 0))
    line_sent(("o", 1))
    for p in range(2):
        line_sent(p)
        for i in range(4):

            @pl.when(s != i)
            def _():
                mix_copy(p, i, s).wait_send()


def finish_kernel(*refs):
    sources, gvec, targets, held, sems = refs[:8], refs[8], refs[9:22], refs[22:30], refs[30]
    places = (1, 0, 3, 6, 7, 9, 11, 12)
    loads = [pltpu.make_async_copy(sources[i], held[i], sems.at[0, i]) for i in range(8)]
    stores = [pltpu.make_async_copy(held[i], targets[places[i]], sems.at[1, i]) for i in range(8)]
    for copy in loads:
        copy.start()
    for row, place in enumerate((2, 4, 5, 8, 10)):
        targets[place][...] = gvec[row, :SHARE]
    for load, store in zip(loads, stores):
        load.wait()
        store.start()
    for copy in stores:
        copy.wait()


def fused_shards(
    inputs,
    lengths,
    cotangent,
    gain_attn,
    w_query,
    bias_query,
    query_scale,
    w_key,
    w_value,
    bias_value,
    w_out,
    gain_mlp,
    w_hidden,
    w_back,
):
    vectors = sum(
        jnp.pad(value.astype(F32)[None], ((row, 7 - row), (0, 128 - SHARE)))
        for row, value in enumerate((gain_attn, bias_query, query_scale, bias_value, gain_mlp))
    )
    vmem = pl.BlockSpec(memory_space=pltpu.VMEM)
    whole = (4, 2, 4 * SHARE, WIDTH)
    buffers = [
        (whole, BF16),
        (whole, BF16),
        (whole, BF16),
        (whole, BF16),
        ((3, 2, 2, 4, 2 * SHARE, WIDTH // 2), BF16),
        ((3, 2, 4, 2 * SHARE, WIDTH // 2), BF16),
        ((3, 4, 2 * SHARE, WIDTH // 2), BF16),
        ((3, 3, 2 * SHARE, WIDTH // 2), BF16),
        ((2, 8, 4 * SHARE, PACK), BF16),
        ((2, 4, SHARE, PACK), BF16),
        ((4, ROWS, WIDTH), BF16),
        ((4, SLOTS, HEAD_DIM), BF16),
        ((4, SLOTS, HEAD_DIM), BF16),
        ((MINE, SLOTS), BF16),
        ((MINE, SLOTS), BF16),
        ((MINE, SLOTS), BF16),
        ((2, 4, ROWS, PAIR), BF16),
        ((4, 1, SLOTS), F32),
        ((4, MINE, ROWS), BF16),
        ((4, MINE, ROWS), BF16),
        ((ROWS, WIDTH), BF16),
        ((ROWS, WIDTH), F32),
        ((ROWS, WIDTH), F32),
        ((ROWS, WIDTH), BF16),
        ((ROWS, WIDTH), BF16),
        ((4, MINE, ROWS), BF16),
        ((4, MINE, ROWS), BF16),
        ((ROWS, WIDTH), BF16),
        ((SLOTS, HEAD_DIM), F32),
        ((SLOTS, HEAD_DIM), F32),
        ((MINE, SLOTS), F32),
        ((2, SLOTS, PACK), BF16),
        ((2, ROWS, WIDTH), BF16),
        ((ROWS, WIDTH), BF16),
        ((2, 4, 2, 4 * SHARE, PACK), BF16),
        ((2, 4, 4 * SHARE, PACK), BF16),
        ((2, 3, 4 * SHARE, PACK), BF16),
        ((2, 4, SHARE, PACK), BF16),
        ((2, 4, SHARE, PACK), BF16),
        ((2, 2, 4, 2, 8, 128), F32),
        ((8, WIDTH + 128), F32),
        ((8, WIDTH), F32),
        ((7, 8, WIDTH), F32),
        ((2, 4, SHARE, PACK), BF16),
        ((3, 2, SHARE, WIDTH // 2), BF16),
        ((3, SHARE, WIDTH // 2), F32),
        ((3, SHARE, WIDTH // 2), F32),
    ]
    scratch = [pltpu.VMEM(shape, kind) for shape, kind in buffers]
    scratch += [pltpu.SemaphoreType.DMA((2, 4))] * 2 + [pltpu.SemaphoreType.DMA((3, 8, 4))] * 2
    scratch += [pltpu.SemaphoreType.DMA((COPIES,))] * 2
    square = jax.ShapeDtypeStruct((SHARE, WIDTH), F32)
    results = pl.pallas_call(
        layer_kernel,
        out_shape=(
            jax.ShapeDtypeStruct((ROWS, WIDTH), BF16),
            jax.ShapeDtypeStruct((ROWS, WIDTH), F32),
            jax.ShapeDtypeStruct((8, 128), F32),
            square,
            square,
            square,
            square,
            square,
            square,
        ),
        in_specs=[vmem, pl.BlockSpec(memory_space=pltpu.SMEM)] + [vmem] * 8,
        out_specs=tuple([vmem] * 9),
        scratch_shapes=scratch,
        compiler_params=pltpu.CompilerParams(
            collective_id=0, has_side_effects=True, vmem_limit_bytes=66 * 1000 * 1000
        ),
        cost_estimate=pl.CostEstimate(flops=25_000_000_000, bytes_accessed=10_000_000, transcendentals=10_000_000),
    )(
        inputs.reshape(ROWS, WIDTH),
        lengths,
        cotangent.reshape(ROWS, WIDTH),
        vectors,
        w_query,
        w_key,
        w_value,
        w_out,
        w_hidden,
        w_back,
    )
    out, input_grad, gvec, gq, gk, gv, go, gh, gb = results
    moved = (input_grad, out, gq, gk, gv, go, gh, gb)
    anywhere = pl.BlockSpec(memory_space=pl.ANY)
    vector = jax.ShapeDtypeStruct((SHARE,), F32)
    shapes = [jax.ShapeDtypeStruct((ROWS, WIDTH), BF16), jax.ShapeDtypeStruct((ROWS, WIDTH), F32), vector, square]
    shapes += [vector, vector, square, square, vector, square, vector, square, square]
    done = pl.pallas_call(
        finish_kernel,
        out_shape=tuple(shapes),
        in_specs=[anywhere] * 8 + [vmem],
        out_specs=tuple(vmem if shape is vector else anywhere for shape in shapes),
        scratch_shapes=[pltpu.VMEM(array.shape, array.dtype) for array in moved]
        + [pltpu.SemaphoreType.DMA((2, 8))],
        compiler_params=pltpu.CompilerParams(vmem_limit_bytes=66 * 1000 * 1000),
    )(*moved, gvec)
    return (done[0].reshape(inputs.shape), done[1].reshape(inputs.shape), *done[2:])


def solution(mesh):
    placed = (
        P("dp", "seq", None),
        P("dp"),
        P("dp", "seq", None),
        P(("dp", "seq")),
        P(("dp", "seq"), None),
        P(("dp", "seq")),
        P(("dp", "seq")),
        P(("dp", "seq"), None),
        P(("dp", "seq"), None),
        P(("dp", "seq")),
        P(("dp", "seq"), None),
        P(("dp", "seq")),
        P(("dp", "seq"), None),
        P(("dp", "seq"), None),
    )
    return jax.shard_map(
        fused_shards if fits(mesh) else shards,
        mesh=mesh,
        in_specs=placed,
        out_specs=(
            P("dp", "seq", None),
            P("dp", "seq", None),
            P(("dp", "seq")),
            P(("dp", "seq"), None),
            P(("dp", "seq")),
            P(("dp", "seq")),
            P(("dp", "seq"), None),
            P(("dp", "seq"), None),
            P(("dp", "seq")),
            P(("dp", "seq"), None),
            P(("dp", "seq")),
            P(("dp", "seq"), None),
            P(("dp", "seq"), None),
        ),
        check_vma=False,
    )
```

```python
import math

import jax
import jax.numpy as jnp
from jax import lax
from jax.experimental import pallas as pl
from jax.experimental.pallas import tpu as pltpu
from jax.sharding import PartitionSpec as P

HEADS = 16
HEAD_DIM = 80


query_gain = 1.442695041
masked_score = -1e30


def normed(values):
    squares = jnp.mean(values * values, axis=-1, keepdims=True)
    inverse = lax.rsqrt(squares + 1e-06)
    return (values * inverse, inverse)


def norm_back(grad_in, unit, inverse, gain):
    scaled = grad_in * gain
    return inverse * (scaled - unit * jnp.mean(scaled * unit, axis=-1, keepdims=True))


def row_product(left, right):
    return lax.dot_general(
        left, right, (((0,), (0,)), ((), ())), preferred_element_type=jnp.float32
    )


def back_product(left, right):
    return lax.dot_general(
        left, right, (((1,), (1,)), ((), ())), preferred_element_type=jnp.float32
    )


def shards(
    inputs,
    lengths,
    cotangent,
    gain_attn,
    w_query,
    bias_query,
    query_scale,
    w_key,
    w_value,
    bias_value,
    w_out,
    gain_mlp,
    w_hidden,
    w_back,
):
    seq_dev, group_rows, width = inputs.shape
    tok_rows = seq_dev * group_rows
    head_count = HEADS
    head_width = HEAD_DIM
    gathered = (
        lax.all_gather(gain_attn, ("dp", "seq"), axis=0, tiled=True),
        lax.all_gather(w_query, ("dp", "seq"), axis=0, tiled=True),
        lax.all_gather(bias_query, ("dp", "seq"), axis=0, tiled=True),
        lax.all_gather(query_scale, ("dp", "seq"), axis=0, tiled=True),
        lax.all_gather(w_key, ("dp", "seq"), axis=0, tiled=True),
        lax.all_gather(w_value, ("dp", "seq"), axis=0, tiled=True),
        lax.all_gather(bias_value, ("dp", "seq"), axis=0, tiled=True),
        lax.all_gather(w_out, ("dp", "seq"), axis=0, tiled=True),
        lax.all_gather(gain_mlp, ("dp", "seq"), axis=0, tiled=True),
        lax.all_gather(w_hidden, ("dp", "seq"), axis=0, tiled=True),
        lax.all_gather(w_back, ("dp", "seq"), axis=0, tiled=True),
    )
    (
        norm_one,
        query_mat,
        query_bias,
        query_log,
        key_mat,
        value_mat,
        value_bias,
        output_mat,
        norm_two,
        hidden_mat,
        back_mat,
    ) = gathered
    ff_width = hidden_mat.shape[1]
    offset = lax.axis_index("seq") * group_rows
    place = offset + jnp.arange(group_rows, dtype=jnp.int32)
    valid = place[None, :] < lengths[:, None]
    row_valid = valid.reshape(tok_rows, 1)
    inputs_rows = inputs.reshape(tok_rows, width).astype(jnp.float32)
    unit_one, inverse_one = normed(inputs_rows)
    gain_one = norm_one.astype(jnp.float32)
    normed_one = (unit_one * gain_one).astype(jnp.bfloat16)
    query_raw = jnp.dot(
        normed_one, query_mat, preferred_element_type=jnp.float32
    ) + query_bias.astype(jnp.float32)
    query_logf = query_log.astype(jnp.float32)
    scale_vec = jax.nn.softplus(query_logf) * (query_gain / math.sqrt(head_width))
    queries = (query_raw * scale_vec).astype(jnp.bfloat16)
    keys_local = jnp.dot(normed_one, key_mat, preferred_element_type=jnp.float32).astype(
        jnp.bfloat16
    )
    values_local = (
        jnp.dot(normed_one, value_mat, preferred_element_type=jnp.float32)
        + value_bias.astype(jnp.float32)
    ).astype(jnp.bfloat16)
    keys_three = keys_local.reshape(seq_dev, group_rows, width)
    values_three = values_local.reshape(seq_dev, group_rows, width)
    queries_three = queries.reshape(seq_dev, group_rows, width)
    keys_all, values_all = (
        lax.all_gather(keys_three, "seq", axis=1, tiled=True),
        lax.all_gather(values_three, "seq", axis=1, tiled=True),
    )
    seq_slots = keys_all.shape[1]
    key_place = jnp.arange(seq_slots, dtype=jnp.int32)
    allowed = key_place[None, :] <= place[:, None]

    def attend(pieces):
        query_block, key_block, value_block = pieces
        query_heads = query_block.reshape(group_rows, head_count, head_width)
        key_heads = key_block.reshape(seq_slots, head_count, head_width)
        value_heads = value_block.reshape(seq_slots, head_count, head_width)
        scores = jnp.einsum(
            "qhd,khd->hqk", query_heads, key_heads, preferred_element_type=jnp.float32
        )
        scores = jnp.where(allowed[None], scores, masked_score)
        largest = jnp.max(scores, axis=-1, keepdims=True)
        raised = jnp.exp(scores - largest)
        totals = jnp.sum(raised, axis=-1, keepdims=True)
        weights_soft = (raised / totals).astype(jnp.bfloat16)
        mixed = jnp.einsum(
            "hqk,khd->qhd", weights_soft, value_heads, preferred_element_type=jnp.float32
        )
        log_total = largest[..., 0] + jnp.log(totals[..., 0])
        return (mixed.reshape(group_rows, width).astype(jnp.bfloat16), log_total)

    mixed_three, log_totals = lax.map(attend, (queries_three, keys_all, values_all))
    mixed = mixed_three.reshape(tok_rows, width)
    middle = inputs_rows + jnp.dot(mixed, output_mat, preferred_element_type=jnp.float32)
    unit_two, inverse_two = normed(middle)
    gain_two = norm_two.astype(jnp.float32)
    normed_two = (unit_two * gain_two).astype(jnp.bfloat16)
    hidden = jnp.dot(normed_two, hidden_mat, preferred_element_type=jnp.float32)
    active = jax.nn.silu(hidden).astype(jnp.bfloat16)
    result = middle + jnp.dot(active, back_mat, preferred_element_type=jnp.float32)
    outputs = (
        jnp.where(row_valid, result, 0.0).astype(jnp.bfloat16).reshape(seq_dev, group_rows, width)
    )
    again = (
        lax.all_gather(gain_attn, ("dp", "seq"), axis=0, tiled=True),
        lax.all_gather(w_query, ("dp", "seq"), axis=0, tiled=True),
        lax.all_gather(w_key, ("dp", "seq"), axis=0, tiled=True),
        lax.all_gather(w_value, ("dp", "seq"), axis=0, tiled=True),
        lax.all_gather(w_out, ("dp", "seq"), axis=0, tiled=True),
        lax.all_gather(gain_mlp, ("dp", "seq"), axis=0, tiled=True),
        lax.all_gather(w_hidden, ("dp", "seq"), axis=0, tiled=True),
        lax.all_gather(w_back, ("dp", "seq"), axis=0, tiled=True),
    )
    norm_one, query_mat, key_mat, value_mat, output_mat, norm_two, hidden_mat, back_mat = again
    gain_one = norm_one.astype(jnp.float32)
    gain_two = norm_two.astype(jnp.float32)
    keys_back, values_back = (
        lax.all_gather(keys_three, "seq", axis=1, tiled=True),
        lax.all_gather(values_three, "seq", axis=1, tiled=True),
    )
    cot_rows = cotangent.reshape(tok_rows, width)
    grad_out = jnp.where(row_valid, cot_rows, jnp.zeros_like(cot_rows))
    grad_active = back_product(grad_out, back_mat)
    sigma = jax.nn.sigmoid(hidden)
    grad_hidden = (grad_active * sigma * (1.0 + hidden * (1.0 - sigma))).astype(jnp.bfloat16)
    grad_normed_two = back_product(grad_hidden, hidden_mat)
    grad_gain_two = jnp.sum(grad_normed_two * unit_two, axis=0)
    grad_middle = grad_out.astype(jnp.float32) + norm_back(
        grad_normed_two, unit_two, inverse_two, gain_two
    )
    grad_middle_low = grad_middle.astype(jnp.bfloat16)
    grad_mixed = back_product(grad_middle_low, output_mat).astype(jnp.bfloat16)
    grad_mixed_three = grad_mixed.reshape(seq_dev, group_rows, width)

    def attend_query(pieces):
        query_block, key_block, value_block, grad_block, log_total = pieces
        query_heads = query_block.reshape(group_rows, head_count, head_width)
        key_heads = key_block.reshape(seq_slots, head_count, head_width)
        value_heads = value_block.reshape(seq_slots, head_count, head_width)
        grad_heads = grad_block.reshape(group_rows, head_count, head_width)
        scores = jnp.einsum(
            "qhd,khd->hqk", query_heads, key_heads, preferred_element_type=jnp.float32
        )
        scores = jnp.where(allowed[None], scores, masked_score)
        weights_soft = jnp.exp(scores - log_total[..., None])
        grad_soft = jnp.einsum(
            "qhd,khd->hqk", grad_heads, value_heads, preferred_element_type=jnp.float32
        )
        inner = jnp.sum(weights_soft * grad_soft, axis=-1, keepdims=True)
        grad_scores = (weights_soft * (grad_soft - inner)).astype(jnp.bfloat16)
        grad_queries = jnp.einsum(
            "hqk,khd->qhd", grad_scores, key_heads, preferred_element_type=jnp.float32
        )
        return (grad_queries.reshape(group_rows, width), inner[..., 0])

    grad_queries, inner_rows = lax.map(
        attend_query, (queries_three, keys_back, values_back, grad_mixed_three, log_totals)
    )
    queries_every, grad_every = (
        lax.all_gather(queries_three, "seq", axis=1, tiled=True),
        lax.all_gather(grad_mixed_three, "seq", axis=1, tiled=True),
    )
    lse_every, inner_every = (
        lax.all_gather(log_totals, "seq", axis=2, tiled=True),
        lax.all_gather(inner_rows, "seq", axis=2, tiled=True),
    )
    later = key_place[:, None] >= place[None, :]

    def key_side(pieces):
        query_block, grad_block, key_block, value_block, lse_block, inner_block = pieces
        query_heads = query_block.reshape(seq_slots, head_count, head_width)
        grad_heads = grad_block.reshape(seq_slots, head_count, head_width)
        key_heads = key_block.reshape(group_rows, head_count, head_width)
        value_heads = value_block.reshape(group_rows, head_count, head_width)
        scores = jnp.einsum(
            "qhd,khd->hqk", query_heads, key_heads, preferred_element_type=jnp.float32
        )
        scores = jnp.where(later[None], scores, masked_score)
        weights_soft = jnp.exp(scores - lse_block[..., None])
        weights_low = weights_soft.astype(jnp.bfloat16)
        grad_soft = jnp.einsum(
            "qhd,khd->hqk", grad_heads, value_heads, preferred_element_type=jnp.float32
        )
        grad_scores = (weights_soft * (grad_soft - inner_block[..., None])).astype(jnp.bfloat16)
        grad_keys = jnp.einsum(
            "hqk,qhd->khd", grad_scores, query_heads, preferred_element_type=jnp.float32
        )
        grad_values = jnp.einsum(
            "hqk,qhd->khd", weights_low, grad_heads, preferred_element_type=jnp.float32
        )
        return (grad_keys.reshape(group_rows, width), grad_values.reshape(group_rows, width))

    grad_keys_sum, grad_values_sum = lax.map(
        key_side, (queries_every, grad_every, keys_three, values_three, lse_every, inner_every)
    )
    grad_keys = grad_keys_sum.reshape(tok_rows, width).astype(jnp.bfloat16)
    grad_values = grad_values_sum.reshape(tok_rows, width).astype(jnp.bfloat16)
    grad_queries = grad_queries.reshape(tok_rows, width)
    grad_query_raw = (grad_queries * scale_vec).astype(jnp.bfloat16)
    grad_scale = jnp.sum(grad_queries * query_raw, axis=0)
    grad_query_log = grad_scale * jax.nn.sigmoid(query_logf) * (query_gain / math.sqrt(head_width))
    grad_query_bias = jnp.sum(grad_query_raw.astype(jnp.float32), axis=0)
    grad_value_bias = jnp.sum(grad_values.astype(jnp.float32), axis=0)
    grad_normed_one = (
        back_product(grad_query_raw, query_mat)
        + back_product(grad_keys, key_mat)
        + back_product(grad_values, value_mat)
    )
    grad_gain_one = jnp.sum(grad_normed_one * unit_one, axis=0)
    input_grad = grad_middle + norm_back(grad_normed_one, unit_one, inverse_one, gain_one)
    dp_count = lax.axis_size("dp")
    seq_count = lax.axis_size("seq")
    share = width // (dp_count * seq_count)
    share_ff = ff_width // (dp_count * seq_count)
    left_parts = (
        lax.all_to_all(
            normed_one.reshape(tok_rows, dp_count, seq_count, share),
            "seq",
            split_axis=2,
            concat_axis=0,
            tiled=True,
        ),
        lax.all_to_all(
            mixed.reshape(tok_rows, dp_count, seq_count, share),
            "seq",
            split_axis=2,
            concat_axis=0,
            tiled=True,
        ),
        lax.all_to_all(
            normed_two.reshape(tok_rows, dp_count, seq_count, share),
            "seq",
            split_axis=2,
            concat_axis=0,
            tiled=True,
        ),
        lax.all_to_all(
            active.reshape(tok_rows, dp_count, seq_count, share_ff),
            "seq",
            split_axis=2,
            concat_axis=0,
            tiled=True,
        ),
    )
    left_normed_one = left_parts[0].reshape(-1, dp_count * share)
    left_mixed = left_parts[1].reshape(-1, dp_count * share)
    left_normed_two = left_parts[2].reshape(-1, dp_count * share)
    left_active = left_parts[3].reshape(-1, dp_count * share_ff)
    right_parts = (
        lax.all_gather(grad_query_raw, "seq", axis=0, tiled=True),
        lax.all_gather(grad_keys, "seq", axis=0, tiled=True),
        lax.all_gather(grad_values, "seq", axis=0, tiled=True),
        lax.all_gather(grad_middle_low, "seq", axis=0, tiled=True),
        lax.all_gather(grad_hidden, "seq", axis=0, tiled=True),
        lax.all_gather(grad_out, "seq", axis=0, tiled=True),
    )
    right_query, right_keys, right_values, right_middle, right_hidden, right_out = right_parts
    part_query_mat = row_product(left_normed_one, right_query)
    part_key_mat = row_product(left_normed_one, right_keys)
    part_value_mat = row_product(left_normed_one, right_values)
    part_output_mat = row_product(left_mixed, right_middle)
    part_hidden_mat = row_product(left_normed_two, right_hidden)
    part_back_mat = row_product(left_active, right_out)
    matrices = (
        lax.psum_scatter(
            part_query_mat.astype(jnp.bfloat16), "dp", scatter_dimension=0, tiled=True
        ).astype(jnp.float32),
        lax.psum_scatter(
            part_key_mat.astype(jnp.bfloat16), "dp", scatter_dimension=0, tiled=True
        ).astype(jnp.float32),
        lax.psum_scatter(
            part_value_mat.astype(jnp.bfloat16), "dp", scatter_dimension=0, tiled=True
        ).astype(jnp.float32),
        lax.psum_scatter(
            part_output_mat.astype(jnp.bfloat16), "dp", scatter_dimension=0, tiled=True
        ).astype(jnp.float32),
        lax.psum_scatter(
            part_hidden_mat.astype(jnp.bfloat16), "dp", scatter_dimension=0, tiled=True
        ).astype(jnp.float32),
        lax.psum_scatter(
            part_back_mat.astype(jnp.bfloat16), "dp", scatter_dimension=0, tiled=True
        ).astype(jnp.float32),
    )
    vectors = (
        lax.psum_scatter(grad_gain_one, ("dp", "seq"), scatter_dimension=0, tiled=True),
        lax.psum_scatter(grad_query_bias, ("dp", "seq"), scatter_dimension=0, tiled=True),
        lax.psum_scatter(grad_query_log, ("dp", "seq"), scatter_dimension=0, tiled=True),
        lax.psum_scatter(grad_value_bias, ("dp", "seq"), scatter_dimension=0, tiled=True),
        lax.psum_scatter(grad_gain_two, ("dp", "seq"), scatter_dimension=0, tiled=True),
    )
    return (
        outputs,
        input_grad.reshape(seq_dev, group_rows, width),
        vectors[0],
        matrices[0],
        vectors[1],
        vectors[2],
        matrices[1],
        matrices[2],
        vectors[3],
        matrices[3],
        vectors[4],
        matrices[4],
        matrices[5],
    )


F32 = jnp.float32
BF16 = jnp.bfloat16
MESH_ID = pl.DeviceIdType.MESH
ROWS = 256
WIDTH = 1280
SHARE = 40
MINE = 320
SLOTS = 1024
PACK = 512
PAIR = 160
COPIES = 38


def fits(mesh):
    return mesh.shape["dp"] == 8 and mesh.shape["seq"] == 4


def dot_nn(left, right):
    return jnp.dot(left, right, preferred_element_type=F32)


def dot_nt(left, right):
    return lax.dot_general(left, right, (((1,), (1,)), ((), ())), preferred_element_type=F32)


def dot_tn(left, right):
    return lax.dot_general(left, right, (((0,), (0,)), ((), ())), preferred_element_type=F32)


def tile(index, size):
    return pl.ds(pl.multiple_of(index * size, size), size)


def strip(yy):
    return pl.ds(pl.multiple_of(yy * 2 * SHARE, 16), 2 * SHARE)


def half(cc):
    return pl.ds(pl.multiple_of(cc * (WIDTH // 2), 128), WIDTH // 2)


class Outputs:
    def __init__(self, sems):
        self.sems, self.open = sems, []

    def start(self, held, target):
        copy = pltpu.make_async_copy(held, target, self.sems.at[len(self.open)])
        copy.start()
        self.open.append(copy)

    def wait(self):
        for copy in self.open:
            copy.wait()


class Links:
    def __init__(self, send_sems, recv_sems, device):
        self.send_sems, self.recv_sems, self.device = send_sems, recv_sems, device
        self.count = 0
        self.open = {}

    def copy(self, index, src, dst, device):
        return pltpu.make_async_remote_copy(
            src_ref=src,
            dst_ref=dst,
            send_sem=self.send_sems.at[index],
            recv_sem=self.recv_sems.at[index],
            device_id=device,
            device_id_type=MESH_ID,
        )

    def next_index(self):
        self.count += 1
        assert self.count <= COPIES
        return self.count - 1

    def group(self, key, whole):
        self.open[key] = self.copy(self.next_index(), whole, whole, self.device), self.count - 1

    def send(self, key, src, dst, device, group=None):
        if group is not None:
            self.copy(self.open[group][1], src, dst, device).start()
            return
        index = self.next_index()
        copy = self.copy(index, src, dst, device)
        copy.start()
        self.open[key] = copy, index

    def recv(self, *keys):
        for key in keys:
            self.open[key][0].wait_recv()

    def sent(self, *keys):
        for key in keys:
            self.open.pop(key)[0].wait_send()

    def sent_of(self, name):
        for key in list(self.open):
            if key[0] == name:
                self.sent(key)

    def sent_all(self):
        self.sent(*list(self.open))


def layer_kernel(
    x_ref,
    len_ref,
    cot_ref,
    vec_ref,
    wq_ref,
    wk_ref,
    wv_ref,
    wo_ref,
    wh_ref,
    wb_ref,
    out_hbm,
    ig_hbm,
    gvec_hbm,
    gq_hbm,
    gk_hbm,
    gv_hbm,
    go_hbm,
    gh_hbm,
    gb_hbm,
    out_ref,
    ig_ref,
    gvec_ref,
    gq_ref,
    gk_ref,
    gv_ref,
    go_ref,
    gh_ref,
    gb_ref,
    full_o,
    full_h,
    full_b,
    part_b,
    core_in,
    far_in,
    line_in,
    last_in,
    qkv_w,
    stage,
    tokens,
    keys,
    vals,
    queries_t,
    keys_t,
    vals_t,
    queries_n,
    lse,
    mix_out,
    mix_in,
    mix,
    middle,
    hidden,
    norm2,
    active,
    gmix_in,
    grad_low,
    dk_acc,
    dv_acc,
    dq_t,
    grads,
    unit_core,
    unit_far,
    qkv_part,
    qkv_near,
    qkv_line,
    qkv_home,
    vec_slots,
    vec_row,
    vec_part,
    vec_in,
    qkv_own,
    pair_in,
    give_out,
    give_in,
    out_sems,
    mix_send,
    mix_recv,
    line_send,
    line_recv,
    sum_send,
    sum_recv,
    far_recv,
    send_sems,
    recv_sems,
):
    d = lax.axis_index("dp")
    s = lax.axis_index("seq")
    z, x = d // 2, d % 2
    y, c = s // 2, s % 2
    results = Outputs(out_sems)
    core_dev = (d, y * 2 + (1 - c))
    links = Links(send_sems, recv_sems, core_dev)
    send, recv = links.send, links.recv
    y_dev = (d, (1 - y) * 2 + c)
    yc_dev = (d, (1 - y) * 2 + (1 - c))
    x_dev = (z * 2 + (1 - x), s)
    zs = [None] + [(z + k) % 4 for k in range(1, 4)]
    from_z = [None] + [(z + 4 - k) % 4 for k in range(1, 4)]
    z_devs = [None] + [(zs[k] * 2 + x, s) for k in range(1, 4)]

    barrier = pltpu.get_barrier_semaphore()
    for device in (core_dev, y_dev, yc_dev, x_dev, z_devs[1], z_devs[2], z_devs[3]):
        pl.semaphore_signal(barrier, inc=1, device_id=device, device_id_type=MESH_ID)

    for member in range(4):
        for p in range(2):
            cols = slice(MINE * member + PAIR * p, MINE * member + PAIR * (p + 1))
            stage[p, member] = jnp.concatenate(
                [wq_ref[:, cols], wk_ref[:, cols], wv_ref[:, cols], jnp.zeros((SHARE, PACK - 3 * PAIR), BF16)],
                axis=1,
            )
    for p in range(2):
        qkv_own[p, s] = stage[p, s]
    tokens[s] = x_ref[...]
    vec_slots[y, x, z, c] = vec_ref[...]
    shards = {"o": wo_ref, "h": wh_ref, "b": wb_ref}
    slot_of = {"o": 0, "h": 1, "b": 2}
    for m in "ohb":
        pair_in[slot_of[m], c] = shards[m][:, half(c)]
    pl.semaphore_wait(barrier, 7)

    group = ((1, core_dev), (2, y_dev), (3, yc_dev))
    peers = (None, y * 2 + (1 - c), (1 - y) * 2 + c, (1 - y) * 2 + (1 - c))
    def to_group(p):
        links.group(("a2a", p), qkv_own.at[p, pl.ds(0, 3)])
        for k, device in ((2, y_dev), (3, yc_dev), (1, core_dev)):
            send(None, stage.at[p, peers[k]], qkv_own.at[p, s], device, ("a2a", p))

    fulls = {"o": full_o, "h": full_h, "b": full_b}
    first_x = {"o": 1, "h": 0, "b": 1 - c}
    last_x = {"b": c, "h": c, "o": 1}
    last_x_other = {"b": 1 - c, "h": 1 - c, "o": 1}

    def spot(along, first, second):
        on_x = along * first + (1 - along) * second
        on_y = along * second + (1 - along) * first
        return (x + on_x) % 2, strip((y + on_y) % 2)

    def devs_of(along):
        def device(on_x):
            return ((z * 2 + (x + on_x) % 2), ((y + 1 - on_x) % 2) * 2 + c)

        return device(along), device(1 - along)

    up_dev = (jnp.minimum(z + 1, 3) * 2 + x, s)
    down_dev = (jnp.maximum(z - 1, 0) * 2 + x, s)
    streams = [0, 1] + [(m, e) for m in "ohb" for e in (0, 1)]

    def line_piece(stream, zz, far):
        if stream in (0, 1):
            return qkv_w.at[stream, zz * 2 + (x + far) % 2]
        m, e = stream
        xx, rows = spot(first_x[m], e, far)
        return fulls[m].at[zz, xx, rows, half(c)]

    def line_copy(kind, stream, hop, zz):
        if kind == 2:
            device = x_dev if stream in (0, 1) else devs_of(first_x[stream[0]])[1]
        else:
            device = (up_dev, down_dev)[kind]
        index = streams.index(stream)
        piece = line_piece(stream, zz, 0)
        return pltpu.make_async_remote_copy(
            src_ref=piece,
            dst_ref=piece,
            send_sem=line_send.at[kind, index],
            recv_sem=far_recv.at[0, index] if kind == 2 else line_recv.at[kind, index, hop - 1],
            device_id=device,
            device_id_type=MESH_ID,
        )

    def pieces(stream, count, sends, recvs):
        if stream in (0, 1):
            whole = qkv_w.at[stream, pl.ds(0, count)]
        else:
            whole = fulls[stream[0]].at[pl.ds(0, count), 0, pl.ds(0, 2 * SHARE), half(c)]
        return pltpu.make_async_remote_copy(
            src_ref=whole,
            dst_ref=whole,
            send_sem=sends,
            recv_sem=recvs,
            device_id=core_dev,
            device_id_type=MESH_ID,
        )

    def line_far(stream, zz):
        line_copy(2, stream, zz, zz).start()

    def line_first(stream):
        @pl.when(z < 3)
        def _():
            line_copy(0, stream, 1, z).start()

        @pl.when(z > 0)
        def _():
            line_copy(1, stream, 1, z).start()

        line_far(stream, z)

    def line_step(stream, hop):
        @pl.when(z >= hop)
        def _():
            line_copy(0, stream, hop, z - hop).wait_recv()
            if hop < 3:

                @pl.when(z < 3)
                def _():
                    line_copy(0, stream, hop + 1, z - hop).start()

            line_far(stream, z - hop)

        @pl.when(z + hop <= 3)
        def _():
            line_copy(1, stream, hop, z + hop).wait_recv()
            if hop < 3:

                @pl.when(z > 0)
                def _():
                    line_copy(1, stream, hop + 1, z + hop).start()

            line_far(stream, z + hop)

    def line_done(stream):
        index = streams.index(stream)
        pieces(stream, 4, line_send.at[2, index], far_recv.at[0, index]).wait_recv()

    def line_sent(stream):
        index = streams.index(stream)
        for zz in range(3):

            @pl.when(z == zz)
            def _():
                pieces(stream, zz + 1, line_send.at[0, index], far_recv.at[0, index]).wait_send()

            @pl.when(z == zz + 1)
            def _():
                pieces(stream, 3 - zz, line_send.at[1, index], far_recv.at[0, index]).wait_send()

        pieces(stream, 4, line_send.at[2, index], far_recv.at[0, index]).wait_send()

    def to_core(m, far):
        if far == 0:
            links.group((m, "c"), fulls[m].at[:, :, :, half(c)])
        for e in (0, 1):
            xx, rows = spot(first_x[m], e, far)
            piece = fulls[m].at[:, xx, rows, half(c)]
            send(None, piece, piece, core_dev, (m, "c"))

    def gather_side(m):
        to_core(m, 0)

    def gather_core(m):
        line_done((m, 0))
        line_done((m, 1))
        to_core(m, 1)

    def gather_done(m):
        recv((m, "c"))

    def own_rows(p):
        recv(("a2a", p))
        qkv_w[p, d] = jnp.concatenate([qkv_own[p, member] for member in range(4)], axis=0)

    def own_first(m):
        if m == "o":
            recv("pair")
        piece = jnp.concatenate([pair_in[slot_of[m], 0], pair_in[slot_of[m], 1]], axis=0)
        fulls[m][z, x, strip(y), half(c)] = piece
        mine = fulls[m].at[z, x, strip(y), half(c)]
        send((m, "first"), mine, mine, devs_of(first_x[m])[0])

    to_group(0)
    links.group("pair", pair_in.at[:, 0])
    for m in "ohb":
        send(None, shards[m].at[:, half(1 - c)], pair_in.at[slot_of[m], c], core_dev, "pair")
    send("vy", vec_ref, vec_slots.at[y, x, z, c], y_dev)
    to_group(1)
    own_first("o")
    send("xy", x_ref, tokens.at[s], y_dev)
    send("xc", x_ref, tokens.at[s], core_dev)
    own_first("h")
    own_first("b")
    own_rows(0)
    line_first(0)
    recv("vy")
    piece = vec_slots.at[:, x, z, c]
    send("vx", piece, piece, x_dev)
    line_first(("o", 0))
    own_rows(1)
    recv("vx")
    links.group("vz", vec_slots.at[:, :, pl.ds(0, 3), c])
    for k in (1, 2, 3):
        piece = vec_slots.at[:, :, z, c]
        send(None, piece, piece, z_devs[k], "vz")
    line_step(0, 1)
    line_first(1)
    line_step(0, 2)
    recv("vz")
    piece = vec_slots.at[:, :, :, c]
    send("vc", piece, piece, core_dev)
    recv(("o", "first"))
    line_first(("o", 1))
    line_step(0, 3)
    line_step(1, 1)
    recv("vc")
    vec_row[...] = jnp.zeros_like(vec_row)
    for slot in range(32):
        start = slot * SHARE
        low = start // 128 * 128
        piece = jnp.concatenate(
            [vec_slots[slot // 2 % 2, slot // 4 % 2, slot // 8, slot % 2], jnp.zeros((8, 128), F32)], axis=1
        )
        if start > low:
            piece = pltpu.roll(piece, start - low, 1)
        vec_row[:, low : low + 256] += piece

    def norm_of(member, count):
        def norm_rows(step, carry):
            for j in range(count):
                rows = tile(step, 64)
                value = tokens[member + j, rows, :].astype(F32)
                unit = value * lax.rsqrt(jnp.mean(value * value, axis=-1, keepdims=True) + 1e-06)
                tokens[member + j, rows, :] = (unit * vec_row[0:1, :WIDTH]).astype(BF16)
            return carry

        lax.fori_loop(0, ROWS // 64, norm_rows, 0)

    recv("xc")
    norm_of(y * 2, 2)
    line_step(("o", 0), 1)
    recv("xy")
    piece = tokens.at[peers[2]]
    send("xyc", piece, piece, core_dev)
    line_step(1, 2)
    line_step(("o", 1), 1)
    recv("xyc")
    links.sent("xyc")
    norm_of((1 - y) * 2, 2)

    def own(row):
        value = vec_row[row : row + 1, 0:MINE]
        for member in range(1, 4):
            value = jnp.where(s == member, vec_row[row : row + 1, MINE * member : MINE * (member + 1)], value)
        return value

    query_log = own(2)
    factor = query_gain / math.sqrt(HEAD_DIM)
    scale = (jnp.maximum(query_log, 0.0) + jnp.log1p(jnp.exp(-jnp.abs(query_log)))) * factor
    query_bias, value_bias = own(1), own(3)

    weights = [qkv_w.at[p].reshape(WIDTH, PACK) for p in range(2)]

    def project_pair(p):
        lanes = slice(PAIR * p, PAIR * (p + 1))

        def project(i, carry):
            rows = tile(i, ROWS)
            raw = dot_nn(tokens[i], weights[p][...])
            query = ((raw[:, :PAIR] + query_bias[:, lanes]) * scale[:, lanes]).astype(BF16)
            key = raw[:, PAIR : 2 * PAIR].astype(BF16)
            val = (raw[:, 2 * PAIR : 3 * PAIR] + value_bias[:, lanes]).astype(BF16)
            queries_n[p, i] = query
            queries_t[lanes, rows] = query.T
            keys_t[lanes, rows] = key.T
            vals_t[lanes, rows] = val.T
            for h in range(2):
                keys[2 * p + h, rows, :] = key[:, HEAD_DIM * h : HEAD_DIM * (h + 1)]
                vals[2 * p + h, rows, :] = val[:, HEAD_DIM * h : HEAD_DIM * (h + 1)]
            return carry

        lax.fori_loop(0, 4, project, 0)

    key_place = lax.broadcasted_iota(jnp.int32, (ROWS, ROWS), 0)
    query_place = lax.broadcasted_iota(jnp.int32, (ROWS, ROWS), 1)
    allowed = key_place <= query_place

    def attend(p, i):
        low, high = i * ROWS, (i + 1) * ROWS

        def head(h, carry):
            rows = tile(h, HEAD_DIM)
            query = queries_t[rows, low:high]
            near = jnp.where(allowed, dot_nn(keys[h, low:high, :], query), masked_score)
            largest = jnp.max(near, axis=0, keepdims=True)
            if i:
                before = dot_nn(keys[h, 0:low, :], query)
                largest = jnp.maximum(largest, jnp.max(before, axis=0, keepdims=True))
            near = jnp.exp(near - largest)
            total = jnp.sum(near, axis=0, keepdims=True)
            mixed = dot_nn(vals_t[rows, low:high], near.astype(BF16))
            if i:
                before = jnp.exp(before - largest)
                total += jnp.sum(before, axis=0, keepdims=True)
                mixed += dot_nn(vals_t[rows, 0:low], before.astype(BF16))
            lse[h, :, low:high] = largest + jnp.log(total)
            mix_out[i, rows, :] = (mixed / total).astype(BF16)
            return carry

        lax.fori_loop(2 * p, 2 * p + 2, head, 0)

    def mix_copy(p, dest, source):
        return pltpu.make_async_remote_copy(
            src_ref=mix_out.at[dest, PAIR * p : PAIR * (p + 1)],
            dst_ref=mix_in.at[source, PAIR * p : PAIR * (p + 1)],
            send_sem=mix_send,
            recv_sem=mix_recv,
            device_id=(d, dest),
            device_id_type=MESH_ID,
        )

    def attend_and_send(p, i):
        attend(p, i)

        @pl.when(s != i)
        def _():
            mix_copy(p, i, s).start()

        @pl.when(s == i)
        def _():
            mix_in[i, PAIR * p : PAIR * (p + 1)] = mix_out[i, PAIR * p : PAIR * (p + 1)]

    line_done(0)
    project_pair(0)
    line_step(1, 3)
    line_step(("o", 0), 2)
    attend_and_send(0, 3)
    recv(("h", "first"))
    line_first(("h", 0))
    line_step(("o", 1), 2)
    attend_and_send(0, 2)
    line_first(("h", 1))
    line_step(("o", 0), 3)
    attend_and_send(0, 1)
    line_step(("o", 1), 3)
    gather_side("o")
    attend_and_send(0, 0)
    line_step(("h", 0), 1)
    recv(("b", "first"))
    line_first(("b", 0))
    line_done(1)
    project_pair(1)
    line_step(("h", 1), 1)
    line_first(("b", 1))
    attend_and_send(1, 3)
    line_step(("h", 0), 2)
    line_step(("h", 1), 2)
    gather_core("o")
    attend_and_send(1, 2)
    line_step(("b", 0), 1)
    line_step(("b", 1), 1)
    attend_and_send(1, 1)
    line_step(("h", 0), 3)
    line_step(("h", 1), 3)
    attend_and_send(1, 0)
    gather_side("h")
    mix_whole = pltpu.make_async_remote_copy(
        src_ref=mix_in.at[pl.ds(0, 3)],
        dst_ref=mix_in.at[pl.ds(0, 3)],
        send_sem=mix_send,
        recv_sem=mix_recv,
        device_id=core_dev,
        device_id_type=MESH_ID,
    )
    mix_whole.wait_recv()
    gather_done("o")

    mix[...] = mix_in[...].reshape(WIDTH, ROWS).T
    mats = {m: fulls[m].reshape(WIDTH, WIDTH) for m in "ohb"}

    def middle_step(j, carry):
        cols = tile(j, 256)
        middle[:, cols] = x_ref[:, cols].astype(F32) + dot_nn(mix[...], mats["o"][:, cols])
        return carry

    lax.fori_loop(0, 5, middle_step, 0)

    def rms_inverse(value):
        return lax.rsqrt(jnp.mean(value * value, axis=-1, keepdims=True) + 1e-06)

    def norm_two(step, carry):
        rows = tile(step, 64)
        value = middle[rows, :]
        norm2[rows, :] = (value * rms_inverse(value) * vec_row[4:5, :WIDTH]).astype(BF16)
        return carry

    lax.fori_loop(0, ROWS // 64, norm_two, 0)
    line_step(("b", 0), 2)
    line_step(("b", 1), 2)
    gather_core("h")
    gather_done("h")

    def hidden_step(j, carry):
        cols = tile(j, 256)
        value = dot_nn(norm2[...], mats["h"][:, cols])
        hidden[:, cols] = value
        active[:, cols] = (value * jax.nn.sigmoid(value)).astype(BF16)
        return carry

    lax.fori_loop(0, 5, hidden_step, 0)

    place = s * ROWS + lax.broadcasted_iota(jnp.int32, (ROWS, 1), 0)
    valid = place < len_ref[0]

    def grad_y():
        return jnp.where(valid, cot_ref[...], jnp.zeros((ROWS, WIDTH), BF16))

    parts = {"b": part_b, "h": full_h, "o": full_b}
    outs = {"b": gb_ref, "h": gh_ref, "o": go_ref}
    outs_hbm = {"b": gb_hbm, "h": gh_hbm, "o": go_hbm}
    order = {"b": 0, "h": 1, "o": 2}

    def weight_grad(m, left):
        flat = parts[m].reshape(WIDTH, WIDTH)
        right = {"b": grad_y, "h": lambda: mix[...], "o": lambda: grad_low[...]}[m]()

        def step(j, carry):
            flat[tile(j, 256), :] = left(j, right).astype(BF16)
            return carry

        lax.fori_loop(0, 5, step, 0)

    def sum_piece(stream, zz, far):
        if stream in (0, 1):
            return qkv_part.at[stream, zz, (x + far) % 2]
        m, e = stream
        xx, rows = spot(last_x[m], e, far)
        return parts[m].at[zz, xx, rows, half(c)]

    def sum_in(kind, stream, zz):
        if stream in (0, 1):
            return qkv_near.at[stream, zz] if kind == 2 else qkv_line.at[kind, stream, zz - 1 + kind]
        index = streams.index(stream) - 2
        return far_in.at[index, zz] if kind == 2 else line_in.at[kind, index, zz - 1 + kind]

    def sum_copy(kind, stream, zz):
        if kind == 2:
            device = x_dev if stream in (0, 1) else devs_of(last_x[stream[0]])[1]
        else:
            device = (up_dev, down_dev)[kind]
        index = streams.index(stream)
        return pltpu.make_async_remote_copy(
            src_ref=sum_piece(stream, zz, kind // 2),
            dst_ref=sum_in(kind, stream, zz),
            send_sem=sum_send.at[kind, index],
            recv_sem=far_recv.at[1, index] if kind == 2 else sum_recv.at[kind, index, zz - 1 + kind],
            device_id=device,
            device_id_type=MESH_ID,
        )

    def add_in(kind, stream, zz):
        if kind < 2:
            sum_copy(kind, stream, zz).wait_recv()
        piece = sum_piece(stream, zz, 0)
        piece[...] = (piece[...].astype(F32) + sum_in(kind, stream, zz)[...].astype(F32)).astype(BF16)

    def add_far(stream):
        index = streams.index(stream)
        pieces(stream, 4, sum_send.at[2, index], far_recv.at[1, index]).wait_recv()
        for zz in range(4):
            add_in(2, stream, zz)

    def sum_far(stream):
        for zz in (3, 0, 2, 1):
            sum_copy(2, stream, zz).start()

    def sum_step(stream, step):
        if step == 0:
            add_far(stream)
        above, below = z + 3 - step, z + step - 3

        @pl.when((z >= 1) & (z <= step))
        def _():
            add_in(0, stream, above)

        @pl.when((z <= 2) & (3 - z <= step))
        def _():
            add_in(1, stream, below)

        if step < 3:

            @pl.when((z <= step) & (z > 0))
            def _():
                sum_copy(0, stream, above).start()

            @pl.when((3 - z <= step) & (z < 3))
            def _():
                sum_copy(1, stream, below).start()

        if step == 0:
            @pl.when(z == 0)
            def _():
                for zz in (3, 2, 1):
                    sum_copy(0, stream, zz).start()

            @pl.when(z == 3)
            def _():
                for zz in (0, 1, 2):
                    sum_copy(1, stream, zz).start()

    direct = (1,)

    def direct_copy(stream, k):
        index = streams.index(stream)
        return pltpu.make_async_remote_copy(
            src_ref=sum_piece(stream, zs[k], 0),
            dst_ref=sum_in(0, stream, k),
            send_sem=sum_send.at[0, index],
            recv_sem=sum_recv.at[0, index, 0],
            device_id=z_devs[k],
            device_id_type=MESH_ID,
        )

    def direct_start(stream):
        add_far(stream)
        for k in (2, 1, 3):
            direct_copy(stream, k).start()

    def direct_done(stream):
        total = sum_piece(stream, z, 0)[...].astype(F32)
        index = streams.index(stream)
        pieces(stream, 3, sum_send.at[0, index], sum_recv.at[0, index, 0]).wait_recv()
        for k in (1, 2, 3):
            total += sum_in(0, stream, k)[...].astype(F32)
        sum_piece(stream, z, 0)[...] = total.astype(BF16)

    def sum_sent(stream):
        index = streams.index(stream)
        recvs = far_recv.at[1, index]
        if stream in direct:
            pieces(stream, 3, sum_send.at[0, index], recvs).wait_send()
        else:
            for zz in range(3):

                @pl.when(z == zz)
                def _():
                    pieces(stream, 3 - zz, sum_send.at[0, index], recvs).wait_send()

                @pl.when(z == zz + 1)
                def _():
                    pieces(stream, zz + 1, sum_send.at[1, index], recvs).wait_send()

        pieces(stream, 4, sum_send.at[2, index], recvs).wait_send()

    def core_piece(m, far, e):
        xx, rows = spot(last_x[m], e, far)
        return parts[m].at[:, xx, rows, half(c)]

    def scatter_core(m):
        for far in (1, 0):
            links.group(("gc", m, far), core_in.at[order[m], far])
            for e in (0, 1):
                xx, rows = spot(last_x_other[m], e, far)
                piece = parts[m].at[:, xx, rows, half(1 - c)]
                send(None, piece, core_in.at[order[m], far, e], core_dev, ("gc", m, far))

    def core_add(m, far, e):
        if e == 0:
            recv(("gc", m, far))
        target, other = core_piece(m, far, e), core_in.at[order[m], far, e]

        def step(zz, carry):
            target[zz] = (target[zz].astype(F32) + other[zz].astype(F32)).astype(BF16)
            return carry

        lax.fori_loop(0, 4, step, 0)

    def scatter_far(m):
        for e in (0, 1):
            core_add(m, 1, e)
            sum_far((m, e))
        for e in (0, 1):
            core_add(m, 0, e)

    def both(m, step):
        sum_step((m, 0), step)
        sum_step((m, 1), step)

    def scatter_last(m):
        send(("gl", m), sum_piece((m, 1), z, 0), last_in.at[order[m]], devs_of(last_x[m])[0])

    def scatter_sum(m):
        recv(("gl", m))
        total = sum_piece((m, 0), z, 0)[...].astype(F32) + last_in[order[m]].astype(F32)
        outs[m][:, half(c)] = jnp.where(c == 0, total[:SHARE], total[SHARE:])
        give_out[order[m]] = jnp.where(c == 0, total[SHARE:], total[:SHARE])
        send(("give", m), give_out.at[order[m]], give_in.at[order[m]], core_dev)

    def scatter_done(m):
        recv(("give", m))
        outs[m][:, half(1 - c)] = give_in[order[m]]
        results.start(outs[m], outs_hbm[m])

    weight_grad("b", lambda j, right: dot_tn(active[:, tile(j, 256)], right))
    scatter_core("b")
    line_step(("b", 0), 3)
    line_step(("b", 1), 3)
    gather_side("b")
    scatter_far("b")
    gather_core("b")
    gather_done("b")

    def back_step(j, carry):
        cols = tile(j, 256)
        value = hidden[:, cols]
        sigma = jax.nn.sigmoid(value)
        grad = dot_nt(grad_y(), mats["b"][cols, :])
        grad_low[:, cols] = (grad * sigma * (1.0 + value * (1.0 - sigma))).astype(BF16)
        return carry

    lax.fori_loop(0, 5, back_step, 0)
    mix[...] = grad_low[...]

    def normed_step(j, carry):
        hidden[:, tile(j, 256)] = dot_nt(grad_low[...], mats["h"][tile(j, 256), :])
        return carry

    lax.fori_loop(0, 5, normed_step, 0)
    links.sent_of("h")
    line_sent(("h", 0))
    line_sent(("h", 1))
    weight_grad("h", lambda j, right: dot_tn(norm2[:, tile(j, 256)], right))
    scatter_core("h")
    both("b", 0)
    vec_part[...] = jnp.zeros_like(vec_part)

    def middle_back(step, carry):
        rows = tile(step, 64)
        value = middle[rows, :]
        inverse = rms_inverse(value)
        unit = value * inverse
        grad = hidden[rows, :]
        vec_part[4:5, :] += jnp.sum(grad * unit, axis=0, keepdims=True)
        scaled = grad * vec_row[4:5, :WIDTH]
        inside = (s * ROWS + step * 64 + lax.broadcasted_iota(jnp.int32, (64, 1), 0)) < len_ref[0]
        base = jnp.where(inside, cot_ref[rows, :].astype(F32), 0.0)
        total = base + inverse * (scaled - unit * jnp.mean(scaled * unit, axis=-1, keepdims=True))
        ig_ref[rows, :] = total
        grad_low[rows, :] = total.astype(BF16)
        return carry

    lax.fori_loop(0, ROWS // 64, middle_back, 0)

    mix_whole.wait_send()

    def mixed_back(member, carry):
        mix_out[member] = dot_nt(mats["o"][tile(member, MINE), :], grad_low[...]).astype(BF16)
        return carry

    lax.fori_loop(0, 4, mixed_back, 0)
    for p in range(2):
        rows = slice(PAIR * p, PAIR * (p + 1))
        links.group(("gm", p), gmix_in.at[pl.ds(0, 3), rows])
        for k, device in ((2, y_dev), (3, yc_dev), (1, core_dev)):
            send(None, mix_out.at[peers[k], rows], gmix_in.at[s, rows], device, ("gm", p))
    gmix_in[s] = mix_out[s]
    scatter_far("h")

    def out_step(j, carry):
        cols = tile(j, 256)
        value = middle[:, cols] + dot_nn(active[...], mats["b"][:, cols])
        out_ref[:, cols] = jnp.where(valid, value, 0.0).astype(BF16)
        return carry

    lax.fori_loop(0, 5, out_step, 0)
    results.start(out_ref, out_hbm)
    links.sent_of("b")
    line_sent(("b", 0))
    line_sent(("b", 1))
    mixed_flat = mix_in.reshape(WIDTH, ROWS)
    weight_grad("o", lambda j, right: dot_nn(mixed_flat[tile(j, 256), :], right))
    scatter_core("o")

    def attend_back(h):
        rows = slice(HEAD_DIM * h, HEAD_DIM * (h + 1))
        dk_acc[...] = jnp.zeros_like(dk_acc)
        dv_acc[...] = jnp.zeros_like(dv_acc)
        for i in range(4):
            low, high = i * ROWS, (i + 1) * ROWS
            query = queries_t[rows, low:high]
            grad = gmix_in[i, rows, :]
            log_total = lse[h, :, low:high]
            spans = [(0, low), (low, high)] if i else [(low, high)]
            held = []
            inner = jnp.zeros((1, ROWS), F32)
            for first, last in spans:
                scores = dot_nn(keys[h, first:last, :], query)
                if first == low:
                    scores = jnp.where(allowed, scores, masked_score)
                probs = jnp.exp(scores - log_total)
                grad_probs = dot_nn(vals[h, first:last, :], grad)
                inner += jnp.sum(probs * grad_probs, axis=0, keepdims=True)
                held.append((first, last, probs, grad_probs))
            grad_query = jnp.zeros((HEAD_DIM, ROWS), F32)
            for first, last, probs, grad_probs in held:
                grad_scores = (probs * (grad_probs - inner)).astype(BF16)
                grad_query += dot_nn(keys_t[rows, first:last], grad_scores)
                dk_acc[first:last, :] += dot_nt(grad_scores, query)
                dv_acc[first:last, :] += dot_nt(probs.astype(BF16), grad)
            dq_t[HEAD_DIM * (h % 2) : HEAD_DIM * (h % 2 + 1), low:high] = grad_query
        first = PAIR + HEAD_DIM * (h % 2)
        grads[h // 2, :, first : first + HEAD_DIM] = dk_acc[...].astype(BF16)
        grads[h // 2, :, first + PAIR : first + PAIR + HEAD_DIM] = dv_acc[...].astype(BF16)

    def finish_pair(p):
        lanes = slice(PAIR * p, PAIR * (p + 1))
        pair_scale = scale[:, lanes]
        bias_grad = jnp.zeros((1, PAIR), F32)
        scale_grad = jnp.zeros((1, PAIR), F32)
        value_grad = jnp.zeros((1, PAIR), F32)
        grads[p, :, 3 * PAIR :] = jnp.zeros((SLOTS, PACK - 3 * PAIR), BF16)
        for i in range(4):
            rows = slice(i * ROWS, (i + 1) * ROWS)
            grad = dq_t[:, rows].T
            low_grad = (grad * pair_scale).astype(BF16)
            grads[p, rows, 0:PAIR] = low_grad
            bias_grad += jnp.sum(low_grad.astype(F32), axis=0, keepdims=True)
            scale_grad += jnp.sum(grad * queries_n[p, i].astype(F32), axis=0, keepdims=True)
            value_grad += jnp.sum(grads[p, rows, 2 * PAIR : 3 * PAIR].astype(F32), axis=0, keepdims=True)
        scale_grad = scale_grad / pair_scale * jax.nn.sigmoid(query_log[:, lanes]) * factor
        return bias_grad, scale_grad, value_grad

    def qkv_grad_pair(p):
        flat = qkv_part.at[p].reshape(WIDTH, PACK)

        def qkv_grad(j, carry):
            total = jnp.zeros((256, PACK), F32)
            for i in range(4):
                total += dot_tn(tokens[i, :, tile(j, 256)], grads[p, i * ROWS : (i + 1) * ROWS, :])
            flat[tile(j, 256), :] = total.astype(BF16)
            return carry

        lax.fori_loop(0, 5, qkv_grad, 0)
        sum_far(p)

    def qkv_sum_pair(p):
        links.sent(("a2a", p))
        if p in direct:
            direct_done(p)
        total = qkv_part[p, z, x].astype(F32)
        for member in range(4):
            stage[p, member] = total[SHARE * member : SHARE * (member + 1), :].astype(BF16)
        links.group(("ph", p), qkv_home.at[p, pl.ds(0, 3)])
        for k, device in ((2, y_dev), (3, yc_dev), (1, core_dev)):
            send(None, stage.at[p, peers[k]], qkv_home.at[p, s], device, ("ph", p))
        qkv_home[p, s] = stage[p, s]

    both("b", 1)
    recv(("gm", 0))
    attend_back(0)
    scatter_far("o")
    both("b", 2)
    attend_back(1)
    pair_grads = [finish_pair(0)]
    qkv_grad_pair(0)
    both("b", 3)
    scatter_last("b")
    both("h", 0)
    recv(("gm", 1))
    attend_back(2)
    attend_back(3)
    both("h", 1)
    pair_grads.append(finish_pair(1))
    qkv_grad_pair(1)
    both("h", 2)
    for row in range(3):
        value = jnp.concatenate([pair_grads[0][row], pair_grads[1][row]], axis=1)
        vec_part[row + 1 : row + 2, :] = jnp.concatenate(
            [jnp.where(s == member, value, 0.0) for member in range(4)], axis=1
        )

    def unit_rows(member):
        def unit_grad(j, carry):
            cols = tile(j, 256)
            value = dot_nt(grads[0, tile(member, ROWS), :], weights[0][cols, :])
            value += dot_nt(grads[1, tile(member, ROWS), :], weights[1][cols, :])
            tokens[member, :, cols] = value.astype(BF16)
            return carry

        lax.fori_loop(0, 5, unit_grad, 0)

    unit_rows((1 - y) * 2 + (1 - c))
    send(("uc", 1), tokens.at[(1 - y) * 2 + (1 - c)], unit_core.at[1], core_dev)
    far_member = (1 - y) * 2 + c
    sum_step(0, 0)
    unit_rows(far_member)
    recv(("uc", 1))
    tokens[far_member] = (tokens[far_member].astype(F32) + unit_core[1].astype(F32)).astype(BF16)
    send("uy", tokens.at[far_member], unit_far, y_dev)
    both("h", 3)
    scatter_last("h")
    sum_step(0, 1)
    unit_rows(y * 2 + (1 - c))
    send(("uc", 0), tokens.at[y * 2 + (1 - c)], unit_core.at[0], core_dev)
    both("o", 0)
    unit_rows(s)
    recv(("uc", 0))
    sum_step(0, 2)
    both("o", 1)
    direct_start(1)
    sum_step(0, 3)
    qkv_sum_pair(0)
    both("o", 2)
    recv("uy")

    def unpack(p):
        recv(("ph", p))
        for index, ref in enumerate((gq_ref, gk_ref, gv_ref)):
            for member in range(4):
                first = MINE * member + PAIR * p
                ref[:, first : first + PAIR] = qkv_home[
                    p, member, :, PAIR * index : PAIR * (index + 1)
                ].astype(F32)

    def input_back(step, carry):
        rows = tile(step, 64)
        value = x_ref[rows, :].astype(F32)
        inverse = rms_inverse(value)
        unit = value * inverse
        grad = (
            tokens[s, rows, :].astype(F32) + unit_core[0, rows, :].astype(F32) + unit_far[rows, :].astype(F32)
        )
        vec_part[0:1, :] += jnp.sum(grad * unit, axis=0, keepdims=True)
        scaled = grad * vec_row[0:1, :WIDTH]
        ig_ref[rows, :] += inverse * (scaled - unit * jnp.mean(scaled * unit, axis=-1, keepdims=True))
        return carry

    lax.fori_loop(0, ROWS // 64, input_back, 0)
    results.start(ig_ref, ig_hbm)
    links.group("sg", vec_in.at[pl.ds(0, 3)])
    for k, device in ((2, y_dev), (3, yc_dev), (1, core_dev)):
        send(None, vec_part, vec_in.at[k - 1], device, "sg")
    scatter_sum("b")
    scatter_sum("h")
    recv("sg")
    links.sent("sg")
    vec_part[...] += vec_in[0] + vec_in[1] + vec_in[2]
    send("sx", vec_part, vec_in.at[3], x_dev)
    both("o", 3)
    scatter_last("o")
    recv("sx")
    links.sent("sx")
    vec_part[...] += vec_in[3]
    links.group("sz", vec_in.at[pl.ds(4, 3)])
    for k in (1, 2, 3):
        send(None, vec_part, vec_in.at[3 + k], z_devs[k], "sz")
    scatter_done("b")
    scatter_done("h")
    qkv_sum_pair(1)
    scatter_sum("o")
    unpack(0)
    recv("sz")
    total = vec_part[...] + vec_in[4] + vec_in[5] + vec_in[6]
    gvec_ref[...] = pltpu.roll(total, WIDTH - (d * 4 + s) * SHARE, 1)[:, :128]
    results.start(gvec_ref, gvec_hbm)
    scatter_done("o")
    unpack(1)
    for held, target in ((gq_ref, gq_hbm), (gk_ref, gk_hbm), (gv_ref, gv_hbm)):
        results.start(held, target)
    results.wait()
    links.sent_all()
    line_sent(("o", 0))
    line_sent(("o", 1))
    for stream in streams:
        sum_sent(stream)
    line_sent(0)
    line_sent(1)


def finish_kernel(*refs):
    sources, gvec, targets, held = refs[:8], refs[8], refs[9:22], refs[22:30]
    vectors, sems = refs[30:35], refs[35]
    places = (1, 0, 3, 6, 7, 9, 11, 12)
    rows = (2, 4, 5, 8, 10)
    loads = [pltpu.make_async_copy(sources[i], held[i], sems.at[0, i]) for i in range(8)]
    stores = [pltpu.make_async_copy(held[i], targets[places[i]], sems.at[1, i]) for i in range(8)]
    small = [pltpu.make_async_copy(vectors[i], targets[rows[i]], sems.at[1, 8 + i]) for i in range(5)]
    for copy in loads:
        copy.start()
    for row in range(5):
        vectors[row][...] = gvec[row, :SHARE]
        small[row].start()
    for load, store in zip(loads, stores):
        load.wait()
        store.start()
    for copy in stores + small:
        copy.wait()


def fused_shards(
    inputs,
    lengths,
    cotangent,
    gain_attn,
    w_query,
    bias_query,
    query_scale,
    w_key,
    w_value,
    bias_value,
    w_out,
    gain_mlp,
    w_hidden,
    w_back,
):
    vectors = sum(
        jnp.pad(value.astype(F32)[None], ((row, 7 - row), (0, 128 - SHARE)))
        for row, value in enumerate((gain_attn, bias_query, query_scale, bias_value, gain_mlp))
    )
    vmem = pl.BlockSpec(memory_space=pltpu.VMEM)
    whole = (4, 2, 4 * SHARE, WIDTH)
    buffers = [
        ((ROWS, WIDTH), BF16),
        ((ROWS, WIDTH), F32),
        ((8, 128), F32),
    ]
    buffers += [((SHARE, WIDTH), F32)] * 6
    buffers += [
        (whole, BF16),
        (whole, BF16),
        (whole, BF16),
        (whole, BF16),
        ((3, 2, 2, 4, 2 * SHARE, WIDTH // 2), BF16),
        ((6, 4, 2 * SHARE, WIDTH // 2), BF16),
        ((2, 6, 3, 2 * SHARE, WIDTH // 2), BF16),
        ((3, 2 * SHARE, WIDTH // 2), BF16),
        ((2, 8, 4 * SHARE, PACK), BF16),
        ((2, 4, SHARE, PACK), BF16),
        ((4, ROWS, WIDTH), BF16),
        ((4, SLOTS, HEAD_DIM), BF16),
        ((4, SLOTS, HEAD_DIM), BF16),
        ((MINE, SLOTS), BF16),
        ((MINE, SLOTS), BF16),
        ((MINE, SLOTS), BF16),
        ((2, 4, ROWS, PAIR), BF16),
        ((4, 1, SLOTS), F32),
        ((4, MINE, ROWS), BF16),
        ((4, MINE, ROWS), BF16),
        ((ROWS, WIDTH), BF16),
        ((ROWS, WIDTH), F32),
        ((ROWS, WIDTH), F32),
        ((ROWS, WIDTH), BF16),
        ((ROWS, WIDTH), BF16),
        ((4, MINE, ROWS), BF16),
        ((ROWS, WIDTH), BF16),
        ((SLOTS, HEAD_DIM), F32),
        ((SLOTS, HEAD_DIM), F32),
        ((PAIR, SLOTS), F32),
        ((2, SLOTS, PACK), BF16),
        ((2, ROWS, WIDTH), BF16),
        ((ROWS, WIDTH), BF16),
        ((2, 4, 2, 4 * SHARE, PACK), BF16),
        ((2, 4, 4 * SHARE, PACK), BF16),
        ((2, 2, 3, 4 * SHARE, PACK), BF16),
        ((2, 4, SHARE, PACK), BF16),
        ((2, 2, 4, 2, 8, 128), F32),
        ((8, WIDTH + 128), F32),
        ((8, WIDTH), F32),
        ((7, 8, WIDTH), F32),
        ((2, 4, SHARE, PACK), BF16),
        ((3, 2, SHARE, WIDTH // 2), BF16),
        ((3, SHARE, WIDTH // 2), F32),
        ((3, SHARE, WIDTH // 2), F32),
    ]
    scratch = [pltpu.VMEM(shape, kind) for shape, kind in buffers]
    scratch += [pltpu.SemaphoreType.DMA((9,))]
    dma = pltpu.SemaphoreType.DMA
    scratch += [dma, dma] + [dma((3, 8)), dma((2, 8, 3))] * 2 + [dma((2, 8))]
    scratch += [dma((COPIES,))] * 2
    square = jax.ShapeDtypeStruct((SHARE, WIDTH), F32)
    results = pl.pallas_call(
        layer_kernel,
        out_shape=(
            jax.ShapeDtypeStruct((ROWS, WIDTH), BF16),
            jax.ShapeDtypeStruct((ROWS, WIDTH), F32),
            jax.ShapeDtypeStruct((8, 128), F32),
            square,
            square,
            square,
            square,
            square,
            square,
        ),
        in_specs=[vmem, pl.BlockSpec(memory_space=pltpu.SMEM)] + [vmem] * 8,
        out_specs=tuple([pl.BlockSpec(memory_space=pl.ANY)] * 9),
        scratch_shapes=scratch,
        compiler_params=pltpu.CompilerParams(
            collective_id=0, has_side_effects=True, vmem_limit_bytes=66 * 1000 * 1000
        ),
        cost_estimate=pl.CostEstimate(flops=25_000_000_000, bytes_accessed=10_000_000, transcendentals=10_000_000),
    )(
        inputs.reshape(ROWS, WIDTH),
        lengths,
        cotangent.reshape(ROWS, WIDTH),
        vectors,
        w_query,
        w_key,
        w_value,
        w_out,
        w_hidden,
        w_back,
    )
    out, input_grad, gvec, gq, gk, gv, go, gh, gb = results
    moved = (input_grad, out, gq, gk, gv, go, gh, gb)
    anywhere = pl.BlockSpec(memory_space=pl.ANY)
    vector = jax.ShapeDtypeStruct((SHARE,), F32)
    shapes = [jax.ShapeDtypeStruct((ROWS, WIDTH), BF16), jax.ShapeDtypeStruct((ROWS, WIDTH), F32), vector, square]
    shapes += [vector, vector, square, square, vector, square, vector, square, square]
    done = pl.pallas_call(
        finish_kernel,
        out_shape=tuple(shapes),
        in_specs=[anywhere] * 8 + [vmem],
        out_specs=tuple([anywhere] * 13),
        scratch_shapes=[pltpu.VMEM(array.shape, array.dtype) for array in moved]
        + [pltpu.VMEM((SHARE,), F32)] * 5
        + [pltpu.SemaphoreType.DMA((2, 13))],
        compiler_params=pltpu.CompilerParams(vmem_limit_bytes=66 * 1000 * 1000),
    )(*moved, gvec)
    return (done[0].reshape(inputs.shape), done[1].reshape(inputs.shape), *done[2:])


def solution(mesh):
    placed = (
        P("dp", "seq", None),
        P("dp"),
        P("dp", "seq", None),
        P(("dp", "seq")),
        P(("dp", "seq"), None),
        P(("dp", "seq")),
        P(("dp", "seq")),
        P(("dp", "seq"), None),
        P(("dp", "seq"), None),
        P(("dp", "seq")),
        P(("dp", "seq"), None),
        P(("dp", "seq")),
        P(("dp", "seq"), None),
        P(("dp", "seq"), None),
    )
    return jax.shard_map(
        fused_shards if fits(mesh) else shards,
        mesh=mesh,
        in_specs=placed,
        out_specs=(
            P("dp", "seq", None),
            P("dp", "seq", None),
            P(("dp", "seq")),
            P(("dp", "seq"), None),
            P(("dp", "seq")),
            P(("dp", "seq")),
            P(("dp", "seq"), None),
            P(("dp", "seq"), None),
            P(("dp", "seq")),
            P(("dp", "seq"), None),
            P(("dp", "seq")),
            P(("dp", "seq"), None),
            P(("dp", "seq"), None),
        ),
        check_vma=False,
    )
```

```python
import math

import jax
import jax.numpy as jnp
from jax import lax
from jax.experimental import pallas as pl
from jax.experimental.pallas import tpu as pltpu
from jax.sharding import PartitionSpec as P

HEADS = 16
HEAD_DIM = 80


query_gain = 1.442695041
masked_score = -1e30


def normed(values):
    squares = jnp.mean(values * values, axis=-1, keepdims=True)
    inverse = lax.rsqrt(squares + 1e-06)
    return (values * inverse, inverse)


def norm_back(grad_in, unit, inverse, gain):
    scaled = grad_in * gain
    return inverse * (scaled - unit * jnp.mean(scaled * unit, axis=-1, keepdims=True))


def row_product(left, right):
    return lax.dot_general(
        left, right, (((0,), (0,)), ((), ())), preferred_element_type=jnp.float32
    )


def back_product(left, right):
    return lax.dot_general(
        left, right, (((1,), (1,)), ((), ())), preferred_element_type=jnp.float32
    )


def shards(
    inputs,
    lengths,
    cotangent,
    gain_attn,
    w_query,
    bias_query,
    query_scale,
    w_key,
    w_value,
    bias_value,
    w_out,
    gain_mlp,
    w_hidden,
    w_back,
):
    seq_dev, group_rows, width = inputs.shape
    tok_rows = seq_dev * group_rows
    head_count = HEADS
    head_width = HEAD_DIM
    gathered = (
        lax.all_gather(gain_attn, ("dp", "seq"), axis=0, tiled=True),
        lax.all_gather(w_query, ("dp", "seq"), axis=0, tiled=True),
        lax.all_gather(bias_query, ("dp", "seq"), axis=0, tiled=True),
        lax.all_gather(query_scale, ("dp", "seq"), axis=0, tiled=True),
        lax.all_gather(w_key, ("dp", "seq"), axis=0, tiled=True),
        lax.all_gather(w_value, ("dp", "seq"), axis=0, tiled=True),
        lax.all_gather(bias_value, ("dp", "seq"), axis=0, tiled=True),
        lax.all_gather(w_out, ("dp", "seq"), axis=0, tiled=True),
        lax.all_gather(gain_mlp, ("dp", "seq"), axis=0, tiled=True),
        lax.all_gather(w_hidden, ("dp", "seq"), axis=0, tiled=True),
        lax.all_gather(w_back, ("dp", "seq"), axis=0, tiled=True),
    )
    (
        norm_one,
        query_mat,
        query_bias,
        query_log,
        key_mat,
        value_mat,
        value_bias,
        output_mat,
        norm_two,
        hidden_mat,
        back_mat,
    ) = gathered
    ff_width = hidden_mat.shape[1]
    offset = lax.axis_index("seq") * group_rows
    place = offset + jnp.arange(group_rows, dtype=jnp.int32)
    valid = place[None, :] < lengths[:, None]
    row_valid = valid.reshape(tok_rows, 1)
    inputs_rows = inputs.reshape(tok_rows, width).astype(jnp.float32)
    unit_one, inverse_one = normed(inputs_rows)
    gain_one = norm_one.astype(jnp.float32)
    normed_one = (unit_one * gain_one).astype(jnp.bfloat16)
    query_raw = jnp.dot(
        normed_one, query_mat, preferred_element_type=jnp.float32
    ) + query_bias.astype(jnp.float32)
    query_logf = query_log.astype(jnp.float32)
    scale_vec = jax.nn.softplus(query_logf) * (query_gain / math.sqrt(head_width))
    queries = (query_raw * scale_vec).astype(jnp.bfloat16)
    keys_local = jnp.dot(normed_one, key_mat, preferred_element_type=jnp.float32).astype(
        jnp.bfloat16
    )
    values_local = (
        jnp.dot(normed_one, value_mat, preferred_element_type=jnp.float32)
        + value_bias.astype(jnp.float32)
    ).astype(jnp.bfloat16)
    keys_three = keys_local.reshape(seq_dev, group_rows, width)
    values_three = values_local.reshape(seq_dev, group_rows, width)
    queries_three = queries.reshape(seq_dev, group_rows, width)
    keys_all, values_all = (
        lax.all_gather(keys_three, "seq", axis=1, tiled=True),
        lax.all_gather(values_three, "seq", axis=1, tiled=True),
    )
    seq_slots = keys_all.shape[1]
    key_place = jnp.arange(seq_slots, dtype=jnp.int32)
    allowed = key_place[None, :] <= place[:, None]

    def attend(pieces):
        query_block, key_block, value_block = pieces
        query_heads = query_block.reshape(group_rows, head_count, head_width)
        key_heads = key_block.reshape(seq_slots, head_count, head_width)
        value_heads = value_block.reshape(seq_slots, head_count, head_width)
        scores = jnp.einsum(
            "qhd,khd->hqk", query_heads, key_heads, preferred_element_type=jnp.float32
        )
        scores = jnp.where(allowed[None], scores, masked_score)
        largest = jnp.max(scores, axis=-1, keepdims=True)
        raised = jnp.exp(scores - largest)
        totals = jnp.sum(raised, axis=-1, keepdims=True)
        weights_soft = (raised / totals).astype(jnp.bfloat16)
        mixed = jnp.einsum(
            "hqk,khd->qhd", weights_soft, value_heads, preferred_element_type=jnp.float32
        )
        log_total = largest[..., 0] + jnp.log(totals[..., 0])
        return (mixed.reshape(group_rows, width).astype(jnp.bfloat16), log_total)

    mixed_three, log_totals = lax.map(attend, (queries_three, keys_all, values_all))
    mixed = mixed_three.reshape(tok_rows, width)
    middle = inputs_rows + jnp.dot(mixed, output_mat, preferred_element_type=jnp.float32)
    unit_two, inverse_two = normed(middle)
    gain_two = norm_two.astype(jnp.float32)
    normed_two = (unit_two * gain_two).astype(jnp.bfloat16)
    hidden = jnp.dot(normed_two, hidden_mat, preferred_element_type=jnp.float32)
    active = jax.nn.silu(hidden).astype(jnp.bfloat16)
    result = middle + jnp.dot(active, back_mat, preferred_element_type=jnp.float32)
    outputs = (
        jnp.where(row_valid, result, 0.0).astype(jnp.bfloat16).reshape(seq_dev, group_rows, width)
    )
    again = (
        lax.all_gather(gain_attn, ("dp", "seq"), axis=0, tiled=True),
        lax.all_gather(w_query, ("dp", "seq"), axis=0, tiled=True),
        lax.all_gather(w_key, ("dp", "seq"), axis=0, tiled=True),
        lax.all_gather(w_value, ("dp", "seq"), axis=0, tiled=True),
        lax.all_gather(w_out, ("dp", "seq"), axis=0, tiled=True),
        lax.all_gather(gain_mlp, ("dp", "seq"), axis=0, tiled=True),
        lax.all_gather(w_hidden, ("dp", "seq"), axis=0, tiled=True),
        lax.all_gather(w_back, ("dp", "seq"), axis=0, tiled=True),
    )
    norm_one, query_mat, key_mat, value_mat, output_mat, norm_two, hidden_mat, back_mat = again
    gain_one = norm_one.astype(jnp.float32)
    gain_two = norm_two.astype(jnp.float32)
    keys_back, values_back = (
        lax.all_gather(keys_three, "seq", axis=1, tiled=True),
        lax.all_gather(values_three, "seq", axis=1, tiled=True),
    )
    cot_rows = cotangent.reshape(tok_rows, width)
    grad_out = jnp.where(row_valid, cot_rows, jnp.zeros_like(cot_rows))
    grad_active = back_product(grad_out, back_mat)
    sigma = jax.nn.sigmoid(hidden)
    grad_hidden = (grad_active * sigma * (1.0 + hidden * (1.0 - sigma))).astype(jnp.bfloat16)
    grad_normed_two = back_product(grad_hidden, hidden_mat)
    grad_gain_two = jnp.sum(grad_normed_two * unit_two, axis=0)
    grad_middle = grad_out.astype(jnp.float32) + norm_back(
        grad_normed_two, unit_two, inverse_two, gain_two
    )
    grad_middle_low = grad_middle.astype(jnp.bfloat16)
    grad_mixed = back_product(grad_middle_low, output_mat).astype(jnp.bfloat16)
    grad_mixed_three = grad_mixed.reshape(seq_dev, group_rows, width)

    def attend_query(pieces):
        query_block, key_block, value_block, grad_block, log_total = pieces
        query_heads = query_block.reshape(group_rows, head_count, head_width)
        key_heads = key_block.reshape(seq_slots, head_count, head_width)
        value_heads = value_block.reshape(seq_slots, head_count, head_width)
        grad_heads = grad_block.reshape(group_rows, head_count, head_width)
        scores = jnp.einsum(
            "qhd,khd->hqk", query_heads, key_heads, preferred_element_type=jnp.float32
        )
        scores = jnp.where(allowed[None], scores, masked_score)
        weights_soft = jnp.exp(scores - log_total[..., None])
        grad_soft = jnp.einsum(
            "qhd,khd->hqk", grad_heads, value_heads, preferred_element_type=jnp.float32
        )
        inner = jnp.sum(weights_soft * grad_soft, axis=-1, keepdims=True)
        grad_scores = (weights_soft * (grad_soft - inner)).astype(jnp.bfloat16)
        grad_queries = jnp.einsum(
            "hqk,khd->qhd", grad_scores, key_heads, preferred_element_type=jnp.float32
        )
        return (grad_queries.reshape(group_rows, width), inner[..., 0])

    grad_queries, inner_rows = lax.map(
        attend_query, (queries_three, keys_back, values_back, grad_mixed_three, log_totals)
    )
    queries_every, grad_every = (
        lax.all_gather(queries_three, "seq", axis=1, tiled=True),
        lax.all_gather(grad_mixed_three, "seq", axis=1, tiled=True),
    )
    lse_every, inner_every = (
        lax.all_gather(log_totals, "seq", axis=2, tiled=True),
        lax.all_gather(inner_rows, "seq", axis=2, tiled=True),
    )
    later = key_place[:, None] >= place[None, :]

    def key_side(pieces):
        query_block, grad_block, key_block, value_block, lse_block, inner_block = pieces
        query_heads = query_block.reshape(seq_slots, head_count, head_width)
        grad_heads = grad_block.reshape(seq_slots, head_count, head_width)
        key_heads = key_block.reshape(group_rows, head_count, head_width)
        value_heads = value_block.reshape(group_rows, head_count, head_width)
        scores = jnp.einsum(
            "qhd,khd->hqk", query_heads, key_heads, preferred_element_type=jnp.float32
        )
        scores = jnp.where(later[None], scores, masked_score)
        weights_soft = jnp.exp(scores - lse_block[..., None])
        weights_low = weights_soft.astype(jnp.bfloat16)
        grad_soft = jnp.einsum(
            "qhd,khd->hqk", grad_heads, value_heads, preferred_element_type=jnp.float32
        )
        grad_scores = (weights_soft * (grad_soft - inner_block[..., None])).astype(jnp.bfloat16)
        grad_keys = jnp.einsum(
            "hqk,qhd->khd", grad_scores, query_heads, preferred_element_type=jnp.float32
        )
        grad_values = jnp.einsum(
            "hqk,qhd->khd", weights_low, grad_heads, preferred_element_type=jnp.float32
        )
        return (grad_keys.reshape(group_rows, width), grad_values.reshape(group_rows, width))

    grad_keys_sum, grad_values_sum = lax.map(
        key_side, (queries_every, grad_every, keys_three, values_three, lse_every, inner_every)
    )
    grad_keys = grad_keys_sum.reshape(tok_rows, width).astype(jnp.bfloat16)
    grad_values = grad_values_sum.reshape(tok_rows, width).astype(jnp.bfloat16)
    grad_queries = grad_queries.reshape(tok_rows, width)
    grad_query_raw = (grad_queries * scale_vec).astype(jnp.bfloat16)
    grad_scale = jnp.sum(grad_queries * query_raw, axis=0)
    grad_query_log = grad_scale * jax.nn.sigmoid(query_logf) * (query_gain / math.sqrt(head_width))
    grad_query_bias = jnp.sum(grad_query_raw.astype(jnp.float32), axis=0)
    grad_value_bias = jnp.sum(grad_values.astype(jnp.float32), axis=0)
    grad_normed_one = (
        back_product(grad_query_raw, query_mat)
        + back_product(grad_keys, key_mat)
        + back_product(grad_values, value_mat)
    )
    grad_gain_one = jnp.sum(grad_normed_one * unit_one, axis=0)
    input_grad = grad_middle + norm_back(grad_normed_one, unit_one, inverse_one, gain_one)
    dp_count = lax.axis_size("dp")
    seq_count = lax.axis_size("seq")
    share = width // (dp_count * seq_count)
    share_ff = ff_width // (dp_count * seq_count)
    left_parts = (
        lax.all_to_all(
            normed_one.reshape(tok_rows, dp_count, seq_count, share),
            "seq",
            split_axis=2,
            concat_axis=0,
            tiled=True,
        ),
        lax.all_to_all(
            mixed.reshape(tok_rows, dp_count, seq_count, share),
            "seq",
            split_axis=2,
            concat_axis=0,
            tiled=True,
        ),
        lax.all_to_all(
            normed_two.reshape(tok_rows, dp_count, seq_count, share),
            "seq",
            split_axis=2,
            concat_axis=0,
            tiled=True,
        ),
        lax.all_to_all(
            active.reshape(tok_rows, dp_count, seq_count, share_ff),
            "seq",
            split_axis=2,
            concat_axis=0,
            tiled=True,
        ),
    )
    left_normed_one = left_parts[0].reshape(-1, dp_count * share)
    left_mixed = left_parts[1].reshape(-1, dp_count * share)
    left_normed_two = left_parts[2].reshape(-1, dp_count * share)
    left_active = left_parts[3].reshape(-1, dp_count * share_ff)
    right_parts = (
        lax.all_gather(grad_query_raw, "seq", axis=0, tiled=True),
        lax.all_gather(grad_keys, "seq", axis=0, tiled=True),
        lax.all_gather(grad_values, "seq", axis=0, tiled=True),
        lax.all_gather(grad_middle_low, "seq", axis=0, tiled=True),
        lax.all_gather(grad_hidden, "seq", axis=0, tiled=True),
        lax.all_gather(grad_out, "seq", axis=0, tiled=True),
    )
    right_query, right_keys, right_values, right_middle, right_hidden, right_out = right_parts
    part_query_mat = row_product(left_normed_one, right_query)
    part_key_mat = row_product(left_normed_one, right_keys)
    part_value_mat = row_product(left_normed_one, right_values)
    part_output_mat = row_product(left_mixed, right_middle)
    part_hidden_mat = row_product(left_normed_two, right_hidden)
    part_back_mat = row_product(left_active, right_out)
    matrices = (
        lax.psum_scatter(
            part_query_mat.astype(jnp.bfloat16), "dp", scatter_dimension=0, tiled=True
        ).astype(jnp.float32),
        lax.psum_scatter(
            part_key_mat.astype(jnp.bfloat16), "dp", scatter_dimension=0, tiled=True
        ).astype(jnp.float32),
        lax.psum_scatter(
            part_value_mat.astype(jnp.bfloat16), "dp", scatter_dimension=0, tiled=True
        ).astype(jnp.float32),
        lax.psum_scatter(
            part_output_mat.astype(jnp.bfloat16), "dp", scatter_dimension=0, tiled=True
        ).astype(jnp.float32),
        lax.psum_scatter(
            part_hidden_mat.astype(jnp.bfloat16), "dp", scatter_dimension=0, tiled=True
        ).astype(jnp.float32),
        lax.psum_scatter(
            part_back_mat.astype(jnp.bfloat16), "dp", scatter_dimension=0, tiled=True
        ).astype(jnp.float32),
    )
    vectors = (
        lax.psum_scatter(grad_gain_one, ("dp", "seq"), scatter_dimension=0, tiled=True),
        lax.psum_scatter(grad_query_bias, ("dp", "seq"), scatter_dimension=0, tiled=True),
        lax.psum_scatter(grad_query_log, ("dp", "seq"), scatter_dimension=0, tiled=True),
        lax.psum_scatter(grad_value_bias, ("dp", "seq"), scatter_dimension=0, tiled=True),
        lax.psum_scatter(grad_gain_two, ("dp", "seq"), scatter_dimension=0, tiled=True),
    )
    return (
        outputs,
        input_grad.reshape(seq_dev, group_rows, width),
        vectors[0],
        matrices[0],
        vectors[1],
        vectors[2],
        matrices[1],
        matrices[2],
        vectors[3],
        matrices[3],
        vectors[4],
        matrices[4],
        matrices[5],
    )


F32 = jnp.float32
BF16 = jnp.bfloat16
MESH_ID = pl.DeviceIdType.MESH
ROWS = 256
WIDTH = 1280
SHARE = 40
MINE = 320
SLOTS = 1024
PACK = 512
PAIR = 160
COPIES = 38


def fits(mesh):
    return mesh.shape["dp"] == 8 and mesh.shape["seq"] == 4


def dot_nn(left, right):
    return jnp.dot(left, right, preferred_element_type=F32)


def dot_nt(left, right):
    return lax.dot_general(left, right, (((1,), (1,)), ((), ())), preferred_element_type=F32)


def dot_tn(left, right):
    return lax.dot_general(left, right, (((0,), (0,)), ((), ())), preferred_element_type=F32)


def tile(index, size):
    return pl.ds(pl.multiple_of(index * size, size), size)


def strip(yy):
    return pl.ds(pl.multiple_of(yy * 2 * SHARE, 16), 2 * SHARE)


def half(cc):
    return pl.ds(pl.multiple_of(cc * (WIDTH // 2), 128), WIDTH // 2)


class Outputs:
    def __init__(self, sems):
        self.sems, self.open = sems, []

    def start(self, held, target):
        copy = pltpu.make_async_copy(held, target, self.sems.at[len(self.open)])
        copy.start()
        self.open.append(copy)

    def wait(self):
        for copy in self.open:
            copy.wait()


class Links:
    def __init__(self, send_sems, recv_sems, device):
        self.send_sems, self.recv_sems, self.device = send_sems, recv_sems, device
        self.count = 0
        self.open = {}

    def copy(self, index, src, dst, device):
        return pltpu.make_async_remote_copy(
            src_ref=src,
            dst_ref=dst,
            send_sem=self.send_sems.at[index],
            recv_sem=self.recv_sems.at[index],
            device_id=device,
            device_id_type=MESH_ID,
        )

    def next_index(self):
        self.count += 1
        assert self.count <= COPIES
        return self.count - 1

    def group(self, key, whole):
        self.open[key] = self.copy(self.next_index(), whole, whole, self.device), self.count - 1

    def send(self, key, src, dst, device, group=None):
        if group is not None:
            self.copy(self.open[group][1], src, dst, device).start()
            return
        index = self.next_index()
        copy = self.copy(index, src, dst, device)
        copy.start()
        self.open[key] = copy, index

    def recv(self, *keys):
        for key in keys:
            self.open[key][0].wait_recv()

    def sent(self, *keys):
        for key in keys:
            self.open.pop(key)[0].wait_send()

    def sent_of(self, name):
        for key in list(self.open):
            if key[0] == name:
                self.sent(key)

    def sent_all(self):
        self.sent(*list(self.open))


def layer_kernel(
    x_ref,
    len_ref,
    cot_ref,
    vec_ref,
    wq_ref,
    wk_ref,
    wv_ref,
    wo_ref,
    wh_ref,
    wb_ref,
    out_hbm,
    ig_hbm,
    gvec_hbm,
    gq_hbm,
    gk_hbm,
    gv_hbm,
    go_hbm,
    gh_hbm,
    gb_hbm,
    out_ref,
    ig_ref,
    gvec_ref,
    gq_ref,
    gk_ref,
    gv_ref,
    go_ref,
    gh_ref,
    gb_ref,
    full_o,
    full_h,
    full_b,
    part_b,
    core_in,
    far_in,
    line_in,
    last_in,
    qkv_w,
    stage,
    tokens,
    keys,
    vals,
    queries_t,
    keys_t,
    vals_t,
    queries_n,
    lse,
    mix_out,
    mix_in,
    mix,
    middle,
    hidden,
    norm2,
    active,
    gmix_in,
    grad_low,
    dk_acc,
    dv_acc,
    dq_t,
    grads,
    unit_core,
    unit_far,
    qkv_part,
    qkv_near,
    qkv_line,
    qkv_home,
    vec_slots,
    vec_row,
    vec_part,
    vec_in,
    qkv_own,
    pair_in,
    give_out,
    give_in,
    out_sems,
    mix_send,
    mix_recv,
    line_send,
    line_recv,
    sum_send,
    sum_recv,
    far_recv,
    send_sems,
    recv_sems,
):
    d = lax.axis_index("dp")
    s = lax.axis_index("seq")
    z, x = d // 2, d % 2
    y, c = s // 2, s % 2
    results = Outputs(out_sems)
    core_dev = (d, y * 2 + (1 - c))
    links = Links(send_sems, recv_sems, core_dev)
    send, recv = links.send, links.recv
    y_dev = (d, (1 - y) * 2 + c)
    yc_dev = (d, (1 - y) * 2 + (1 - c))
    x_dev = (z * 2 + (1 - x), s)
    zs = [None] + [(z + k) % 4 for k in range(1, 4)]
    from_z = [None] + [(z + 4 - k) % 4 for k in range(1, 4)]
    z_devs = [None] + [(zs[k] * 2 + x, s) for k in range(1, 4)]

    barrier = pltpu.get_barrier_semaphore()
    for device in (core_dev, y_dev, yc_dev, x_dev, z_devs[1], z_devs[2], z_devs[3]):
        pl.semaphore_signal(barrier, inc=1, device_id=device, device_id_type=MESH_ID)

    for member in range(4):
        for p in range(2):
            cols = slice(MINE * member + PAIR * p, MINE * member + PAIR * (p + 1))
            stage[p, member] = jnp.concatenate(
                [wq_ref[:, cols], wk_ref[:, cols], wv_ref[:, cols], jnp.zeros((SHARE, PACK - 3 * PAIR), BF16)],
                axis=1,
            )
    for p in range(2):
        qkv_own[p, s] = stage[p, s]
    tokens[s] = x_ref[...]
    vec_slots[y, x, z, c] = vec_ref[...]
    shards = {"o": wo_ref, "h": wh_ref, "b": wb_ref}
    slot_of = {"o": 0, "h": 1, "b": 2}
    for m in "ohb":
        pair_in[slot_of[m], c] = shards[m][:, half(c)]
    pl.semaphore_wait(barrier, 7)

    group = ((1, core_dev), (2, y_dev), (3, yc_dev))
    peers = (None, y * 2 + (1 - c), (1 - y) * 2 + c, (1 - y) * 2 + (1 - c))
    def to_group(p):
        links.group(("a2a", p), qkv_own.at[p, pl.ds(0, 3)])
        for k, device in ((2, y_dev), (3, yc_dev), (1, core_dev)):
            send(None, stage.at[p, peers[k]], qkv_own.at[p, s], device, ("a2a", p))

    fulls = {"o": full_o, "h": full_h, "b": full_b}
    first_x = {"o": 1, "h": 0, "b": 1 - c}
    last_x = {"b": c, "h": c, "o": 1}
    last_x_other = {"b": 1 - c, "h": 1 - c, "o": 1}

    def spot(along, first, second):
        on_x = along * first + (1 - along) * second
        on_y = along * second + (1 - along) * first
        return (x + on_x) % 2, strip((y + on_y) % 2)

    def devs_of(along):
        def device(on_x):
            return ((z * 2 + (x + on_x) % 2), ((y + 1 - on_x) % 2) * 2 + c)

        return device(along), device(1 - along)

    up_dev = (jnp.minimum(z + 1, 3) * 2 + x, s)
    down_dev = (jnp.maximum(z - 1, 0) * 2 + x, s)
    streams = [0, 1] + [(m, e) for m in "ohb" for e in (0, 1)]

    def line_piece(stream, zz, far):
        if stream in (0, 1):
            return qkv_w.at[stream, zz * 2 + (x + far) % 2]
        m, e = stream
        xx, rows = spot(first_x[m], e, far)
        return fulls[m].at[zz, xx, rows, half(c)]

    def line_copy(kind, stream, hop, zz):
        if kind == 2:
            device = x_dev if stream in (0, 1) else devs_of(first_x[stream[0]])[1]
        else:
            device = (up_dev, down_dev)[kind]
        index = streams.index(stream)
        piece = line_piece(stream, zz, 0)
        return pltpu.make_async_remote_copy(
            src_ref=piece,
            dst_ref=piece,
            send_sem=line_send.at[kind, index],
            recv_sem=far_recv.at[0, index] if kind == 2 else line_recv.at[kind, index, hop - 1],
            device_id=device,
            device_id_type=MESH_ID,
        )

    def pieces(stream, count, sends, recvs):
        if stream in (0, 1):
            whole = qkv_w.at[stream, pl.ds(0, count)]
        else:
            whole = fulls[stream[0]].at[pl.ds(0, count), 0, pl.ds(0, 2 * SHARE), half(c)]
        return pltpu.make_async_remote_copy(
            src_ref=whole,
            dst_ref=whole,
            send_sem=sends,
            recv_sem=recvs,
            device_id=core_dev,
            device_id_type=MESH_ID,
        )

    def line_far(stream, zz):
        line_copy(2, stream, zz, zz).start()

    def line_first(stream):
        @pl.when(z < 3)
        def _():
            line_copy(0, stream, 1, z).start()

        @pl.when(z > 0)
        def _():
            line_copy(1, stream, 1, z).start()

        line_far(stream, z)

    def line_step(stream, hop):
        @pl.when(z >= hop)
        def _():
            line_copy(0, stream, hop, z - hop).wait_recv()
            if hop < 3:

                @pl.when(z < 3)
                def _():
                    line_copy(0, stream, hop + 1, z - hop).start()

            line_far(stream, z - hop)

        @pl.when(z + hop <= 3)
        def _():
            line_copy(1, stream, hop, z + hop).wait_recv()
            if hop < 3:

                @pl.when(z > 0)
                def _():
                    line_copy(1, stream, hop + 1, z + hop).start()

            line_far(stream, z + hop)

    def line_done(stream):
        index = streams.index(stream)
        pieces(stream, 4, line_send.at[2, index], far_recv.at[0, index]).wait_recv()

    def line_sent(stream):
        index = streams.index(stream)
        for zz in range(3):

            @pl.when(z == zz)
            def _():
                pieces(stream, zz + 1, line_send.at[0, index], far_recv.at[0, index]).wait_send()

            @pl.when(z == zz + 1)
            def _():
                pieces(stream, 3 - zz, line_send.at[1, index], far_recv.at[0, index]).wait_send()

        pieces(stream, 4, line_send.at[2, index], far_recv.at[0, index]).wait_send()

    def to_core(m, far):
        if far == 0:
            links.group((m, "c"), fulls[m].at[:, :, :, half(c)])
        for e in (0, 1):
            xx, rows = spot(first_x[m], e, far)
            piece = fulls[m].at[:, xx, rows, half(c)]
            send(None, piece, piece, core_dev, (m, "c"))

    def gather_side(m):
        to_core(m, 0)

    def gather_core(m):
        line_done((m, 0))
        line_done((m, 1))
        to_core(m, 1)

    def gather_done(m):
        recv((m, "c"))

    def own_rows(p):
        recv(("a2a", p))
        qkv_w[p, d] = jnp.concatenate([qkv_own[p, member] for member in range(4)], axis=0)

    def own_first(m):
        if m == "o":
            recv("pair")
        piece = jnp.concatenate([pair_in[slot_of[m], 0], pair_in[slot_of[m], 1]], axis=0)
        fulls[m][z, x, strip(y), half(c)] = piece
        mine = fulls[m].at[z, x, strip(y), half(c)]
        send((m, "first"), mine, mine, devs_of(first_x[m])[0])

    to_group(0)
    links.group("pair", pair_in.at[:, 0])
    for m in "ohb":
        send(None, shards[m].at[:, half(1 - c)], pair_in.at[slot_of[m], c], core_dev, "pair")
    send("vy", vec_ref, vec_slots.at[y, x, z, c], y_dev)
    to_group(1)
    own_first("o")
    send("xy", x_ref, tokens.at[s], y_dev)
    send("xc", x_ref, tokens.at[s], core_dev)
    own_first("h")
    own_first("b")
    own_rows(0)
    line_first(0)
    recv("vy")
    piece = vec_slots.at[:, x, z, c]
    send("vx", piece, piece, x_dev)
    line_first(("o", 0))
    own_rows(1)
    recv("vx")
    links.group("vz", vec_slots.at[:, :, pl.ds(0, 3), c])
    for k in (1, 2, 3):
        piece = vec_slots.at[:, :, z, c]
        send(None, piece, piece, z_devs[k], "vz")
    line_step(0, 1)
    line_first(1)
    line_step(0, 2)
    recv("vz")
    piece = vec_slots.at[:, :, :, c]
    send("vc", piece, piece, core_dev)
    recv(("o", "first"))
    line_first(("o", 1))
    line_step(0, 3)
    line_step(1, 1)
    recv("vc")
    vec_row[...] = jnp.zeros_like(vec_row)
    for slot in range(32):
        start = slot * SHARE
        low = start // 128 * 128
        piece = jnp.concatenate(
            [vec_slots[slot // 2 % 2, slot // 4 % 2, slot // 8, slot % 2], jnp.zeros((8, 128), F32)], axis=1
        )
        if start > low:
            piece = pltpu.roll(piece, start - low, 1)
        vec_row[:, low : low + 256] += piece

    def norm_of(member, count):
        def norm_rows(step, carry):
            for j in range(count):
                rows = tile(step, 64)
                value = tokens[member + j, rows, :].astype(F32)
                unit = value * lax.rsqrt(jnp.mean(value * value, axis=-1, keepdims=True) + 1e-06)
                tokens[member + j, rows, :] = (unit * vec_row[0:1, :WIDTH]).astype(BF16)
            return carry

        lax.fori_loop(0, ROWS // 64, norm_rows, 0)

    recv("xc")
    norm_of(y * 2, 2)
    line_step(("o", 0), 1)
    recv("xy")
    piece = tokens.at[peers[2]]
    send("xyc", piece, piece, core_dev)
    line_step(1, 2)
    line_step(("o", 1), 1)
    recv("xyc")
    links.sent("xyc")
    norm_of((1 - y) * 2, 2)

    def own(row):
        value = vec_row[row : row + 1, 0:MINE]
        for member in range(1, 4):
            value = jnp.where(s == member, vec_row[row : row + 1, MINE * member : MINE * (member + 1)], value)
        return value

    query_log = own(2)
    factor = query_gain / math.sqrt(HEAD_DIM)
    scale = (jnp.maximum(query_log, 0.0) + jnp.log1p(jnp.exp(-jnp.abs(query_log)))) * factor
    query_bias, value_bias = own(1), own(3)

    weights = [qkv_w.at[p].reshape(WIDTH, PACK) for p in range(2)]

    def project_pair(p):
        lanes = slice(PAIR * p, PAIR * (p + 1))

        def project(i, carry):
            rows = tile(i, ROWS)
            raw = dot_nn(tokens[i], weights[p][...])
            query = ((raw[:, :PAIR] + query_bias[:, lanes]) * scale[:, lanes]).astype(BF16)
            key = raw[:, PAIR : 2 * PAIR].astype(BF16)
            val = (raw[:, 2 * PAIR : 3 * PAIR] + value_bias[:, lanes]).astype(BF16)
            queries_n[p, i] = query
            queries_t[lanes, rows] = query.T
            keys_t[lanes, rows] = key.T
            vals_t[lanes, rows] = val.T
            for h in range(2):
                keys[2 * p + h, rows, :] = key[:, HEAD_DIM * h : HEAD_DIM * (h + 1)]
                vals[2 * p + h, rows, :] = val[:, HEAD_DIM * h : HEAD_DIM * (h + 1)]
            return carry

        lax.fori_loop(0, 4, project, 0)

    key_place = lax.broadcasted_iota(jnp.int32, (ROWS, ROWS), 0)
    query_place = lax.broadcasted_iota(jnp.int32, (ROWS, ROWS), 1)
    allowed = key_place <= query_place

    def attend(p, i):
        low, high = i * ROWS, (i + 1) * ROWS

        def head(h, carry):
            rows = tile(h, HEAD_DIM)
            query = queries_t[rows, low:high]
            near = jnp.where(allowed, dot_nn(keys[h, low:high, :], query), masked_score)
            largest = jnp.max(near, axis=0, keepdims=True)
            if i:
                before = dot_nn(keys[h, 0:low, :], query)
                largest = jnp.maximum(largest, jnp.max(before, axis=0, keepdims=True))
            near = jnp.exp(near - largest)
            total = jnp.sum(near, axis=0, keepdims=True)
            mixed = dot_nn(vals_t[rows, low:high], near.astype(BF16))
            if i:
                before = jnp.exp(before - largest)
                total += jnp.sum(before, axis=0, keepdims=True)
                mixed += dot_nn(vals_t[rows, 0:low], before.astype(BF16))
            lse[h, :, low:high] = largest + jnp.log(total)
            mix_out[i, rows, :] = (mixed / total).astype(BF16)
            return carry

        lax.fori_loop(2 * p, 2 * p + 2, head, 0)

    def mix_copy(p, dest, source):
        return pltpu.make_async_remote_copy(
            src_ref=mix_out.at[dest, PAIR * p : PAIR * (p + 1)],
            dst_ref=mix_in.at[source, PAIR * p : PAIR * (p + 1)],
            send_sem=mix_send,
            recv_sem=mix_recv,
            device_id=(d, dest),
            device_id_type=MESH_ID,
        )

    def attend_and_send(p, i):
        attend(p, i)

        @pl.when(s != i)
        def _():
            mix_copy(p, i, s).start()

        @pl.when(s == i)
        def _():
            mix_in[i, PAIR * p : PAIR * (p + 1)] = mix_out[i, PAIR * p : PAIR * (p + 1)]

    line_done(0)
    project_pair(0)
    line_step(1, 3)
    line_step(("o", 0), 2)
    attend_and_send(0, 3)
    recv(("h", "first"))
    line_first(("h", 0))
    line_step(("o", 1), 2)
    attend_and_send(0, 2)
    line_first(("h", 1))
    line_step(("o", 0), 3)
    attend_and_send(0, 1)
    line_step(("o", 1), 3)
    gather_side("o")
    attend_and_send(0, 0)
    line_step(("h", 0), 1)
    recv(("b", "first"))
    line_first(("b", 0))
    line_done(1)
    project_pair(1)
    line_step(("h", 1), 1)
    line_first(("b", 1))
    attend_and_send(1, 3)
    line_step(("h", 0), 2)
    line_step(("h", 1), 2)
    gather_core("o")
    attend_and_send(1, 2)
    line_step(("b", 0), 1)
    line_step(("b", 1), 1)
    attend_and_send(1, 1)
    line_step(("h", 0), 3)
    line_step(("h", 1), 3)
    attend_and_send(1, 0)
    gather_side("h")
    mix_whole = pltpu.make_async_remote_copy(
        src_ref=mix_in.at[pl.ds(0, 3)],
        dst_ref=mix_in.at[pl.ds(0, 3)],
        send_sem=mix_send,
        recv_sem=mix_recv,
        device_id=core_dev,
        device_id_type=MESH_ID,
    )
    mix_whole.wait_recv()
    gather_done("o")

    mix[...] = mix_in[...].reshape(WIDTH, ROWS).T
    mats = {m: fulls[m].reshape(WIDTH, WIDTH) for m in "ohb"}

    def middle_step(j, carry):
        cols = tile(j, 256)
        middle[:, cols] = x_ref[:, cols].astype(F32) + dot_nn(mix[...], mats["o"][:, cols])
        return carry

    lax.fori_loop(0, 5, middle_step, 0)

    def rms_inverse(value):
        return lax.rsqrt(jnp.mean(value * value, axis=-1, keepdims=True) + 1e-06)

    def norm_two(step, carry):
        rows = tile(step, 64)
        value = middle[rows, :]
        norm2[rows, :] = (value * rms_inverse(value) * vec_row[4:5, :WIDTH]).astype(BF16)
        return carry

    lax.fori_loop(0, ROWS // 64, norm_two, 0)
    line_step(("b", 0), 2)
    line_step(("b", 1), 2)
    gather_core("h")
    gather_done("h")

    def hidden_step(j, carry):
        cols = tile(j, 256)
        value = dot_nn(norm2[...], mats["h"][:, cols])
        hidden[:, cols] = value
        active[:, cols] = (value * jax.nn.sigmoid(value)).astype(BF16)
        return carry

    lax.fori_loop(0, 5, hidden_step, 0)

    place = s * ROWS + lax.broadcasted_iota(jnp.int32, (ROWS, 1), 0)
    valid = place < len_ref[0]

    def grad_y():
        return jnp.where(valid, cot_ref[...], jnp.zeros((ROWS, WIDTH), BF16))

    parts = {"b": part_b, "h": full_h, "o": full_b}
    outs = {"b": gb_ref, "h": gh_ref, "o": go_ref}
    outs_hbm = {"b": gb_hbm, "h": gh_hbm, "o": go_hbm}
    order = {"b": 0, "h": 1, "o": 2}

    def weight_grad(m, left):
        flat = parts[m].reshape(WIDTH, WIDTH)
        right = {"b": grad_y, "h": lambda: mix[...], "o": lambda: grad_low[...]}[m]()

        def step(j, carry):
            flat[tile(j, 256), :] = left(j, right).astype(BF16)
            return carry

        lax.fori_loop(0, 5, step, 0)

    def sum_piece(stream, zz, far):
        if stream in (0, 1):
            return qkv_part.at[stream, zz, (x + far) % 2]
        m, e = stream
        xx, rows = spot(last_x[m], e, far)
        return parts[m].at[zz, xx, rows, half(c)]

    def sum_in(kind, stream, zz):
        if stream in (0, 1):
            return qkv_near.at[stream, zz] if kind == 2 else qkv_line.at[kind, stream, zz - 1 + kind]
        index = streams.index(stream) - 2
        return far_in.at[index, zz] if kind == 2 else line_in.at[kind, index, zz - 1 + kind]

    def sum_copy(kind, stream, zz):
        if kind == 2:
            device = x_dev if stream in (0, 1) else devs_of(last_x[stream[0]])[1]
        else:
            device = (up_dev, down_dev)[kind]
        index = streams.index(stream)
        return pltpu.make_async_remote_copy(
            src_ref=sum_piece(stream, zz, kind // 2),
            dst_ref=sum_in(kind, stream, zz),
            send_sem=sum_send.at[kind, index],
            recv_sem=far_recv.at[1, index] if kind == 2 else sum_recv.at[kind, index, zz - 1 + kind],
            device_id=device,
            device_id_type=MESH_ID,
        )

    def add_in(kind, stream, zz):
        if kind < 2:
            sum_copy(kind, stream, zz).wait_recv()
        piece = sum_piece(stream, zz, 0)
        piece[...] = (piece[...].astype(F32) + sum_in(kind, stream, zz)[...].astype(F32)).astype(BF16)

    def add_far(stream):
        index = streams.index(stream)
        pieces(stream, 4, sum_send.at[2, index], far_recv.at[1, index]).wait_recv()
        for zz in range(4):
            add_in(2, stream, zz)

    def sum_far(stream):
        for zz in (3, 0, 2, 1):
            sum_copy(2, stream, zz).start()

    def near_copy(zz):
        return pltpu.make_async_remote_copy(
            src_ref=sum_piece(("o", 1), zz, 0),
            dst_ref=line_in.at[zz // 3, 1, zz % 3],
            send_sem=sum_send.at[0, 3],
            recv_sem=sum_recv.at[0, 3, 0],
            device_id=devs_of(last_x["o"])[0],
            device_id_type=MESH_ID,
        )

    def cross():
        add_far(("o", 1))
        for zz in (3, 0, 2, 1):
            near_copy(zz).start()

    def add_near():
        pieces(("o", 1), 4, sum_send.at[0, 3], sum_recv.at[0, 3, 0]).wait_recv()
        for zz in range(4):
            piece = sum_piece(("o", 0), zz, 0)
            piece[...] = (piece[...].astype(F32) + line_in[zz // 3, 1, zz % 3].astype(F32)).astype(BF16)

    def sum_step(stream, step):
        if step == 0:
            add_far(stream)
            if stream == ("o", 0):
                add_near()
        above, below = z + 3 - step, z + step - 3

        @pl.when((z >= 1) & (z <= step))
        def _():
            add_in(0, stream, above)

        @pl.when((z <= 2) & (3 - z <= step))
        def _():
            add_in(1, stream, below)

        if step < 3:

            @pl.when((z <= step) & (z > 0))
            def _():
                sum_copy(0, stream, above).start()

            @pl.when((3 - z <= step) & (z < 3))
            def _():
                sum_copy(1, stream, below).start()

        if step == 0:
            @pl.when(z == 0)
            def _():
                for zz in (3, 2, 1):
                    sum_copy(0, stream, zz).start()

            @pl.when(z == 3)
            def _():
                for zz in (0, 1, 2):
                    sum_copy(1, stream, zz).start()

    direct = (1, ("o", 0),)

    def direct_copy(stream, k):
        index = streams.index(stream)
        return pltpu.make_async_remote_copy(
            src_ref=sum_piece(stream, zs[k], 0),
            dst_ref=sum_in(0, stream, k),
            send_sem=sum_send.at[0, index],
            recv_sem=sum_recv.at[0, index, 0],
            device_id=z_devs[k],
            device_id_type=MESH_ID,
        )

    def direct_start(stream):
        add_far(stream)
        if stream == ("o", 0):
            add_near()
        for k in (2, 1, 3):
            direct_copy(stream, k).start()

    def direct_done(stream):
        total = sum_piece(stream, z, 0)[...].astype(F32)
        index = streams.index(stream)
        pieces(stream, 3, sum_send.at[0, index], sum_recv.at[0, index, 0]).wait_recv()
        for k in (1, 2, 3):
            total += sum_in(0, stream, k)[...].astype(F32)
        sum_piece(stream, z, 0)[...] = total.astype(BF16)

    def sum_sent(stream):
        index = streams.index(stream)
        recvs = far_recv.at[1, index]
        if stream == ("o", 1):
            pieces(stream, 4, sum_send.at[0, index], recvs).wait_send()
        elif stream in direct:
            pieces(stream, 3, sum_send.at[0, index], recvs).wait_send()
        else:
            for zz in range(3):

                @pl.when(z == zz)
                def _():
                    pieces(stream, 3 - zz, sum_send.at[0, index], recvs).wait_send()

                @pl.when(z == zz + 1)
                def _():
                    pieces(stream, zz + 1, sum_send.at[1, index], recvs).wait_send()

        pieces(stream, 4, sum_send.at[2, index], recvs).wait_send()

    def core_piece(m, far, e):
        xx, rows = spot(last_x[m], e, far)
        return parts[m].at[:, xx, rows, half(c)]

    def scatter_core(m):
        for far in (1, 0):
            links.group(("gc", m, far), core_in.at[order[m], far])
            for e in (0, 1):
                xx, rows = spot(last_x_other[m], e, far)
                piece = parts[m].at[:, xx, rows, half(1 - c)]
                send(None, piece, core_in.at[order[m], far, e], core_dev, ("gc", m, far))

    def core_add(m, far, e):
        if e == 0:
            recv(("gc", m, far))
        target, other = core_piece(m, far, e), core_in.at[order[m], far, e]

        def step(zz, carry):
            target[zz] = (target[zz].astype(F32) + other[zz].astype(F32)).astype(BF16)
            return carry

        lax.fori_loop(0, 4, step, 0)

    def scatter_far(m):
        for e in (0, 1):
            core_add(m, 1, e)
        for e in (1, 0) if m == "o" else (0, 1):
            sum_far((m, e))
        for e in (0, 1):
            core_add(m, 0, e)

    def both(m, step):
        sum_step((m, 0), step)
        if m != "o":
            sum_step((m, 1), step)

    def scatter_last(m):
        send(("gl", m), sum_piece((m, 1), z, 0), last_in.at[order[m]], devs_of(last_x[m])[0])

    def scatter_sum(m):
        total = sum_piece((m, 0), z, 0)[...].astype(F32)
        if m != "o":
            recv(("gl", m))
            total += last_in[order[m]].astype(F32)
        outs[m][:, half(c)] = jnp.where(c == 0, total[:SHARE], total[SHARE:])
        give_out[order[m]] = jnp.where(c == 0, total[SHARE:], total[:SHARE])
        send(("give", m), give_out.at[order[m]], give_in.at[order[m]], core_dev)

    def scatter_done(m):
        recv(("give", m))
        outs[m][:, half(1 - c)] = give_in[order[m]]
        results.start(outs[m], outs_hbm[m])

    weight_grad("b", lambda j, right: dot_tn(active[:, tile(j, 256)], right))
    scatter_core("b")
    line_step(("b", 0), 3)
    line_step(("b", 1), 3)
    gather_side("b")
    scatter_far("b")
    gather_core("b")
    gather_done("b")

    def back_step(j, carry):
        cols = tile(j, 256)
        value = hidden[:, cols]
        sigma = jax.nn.sigmoid(value)
        grad = dot_nt(grad_y(), mats["b"][cols, :])
        grad_low[:, cols] = (grad * sigma * (1.0 + value * (1.0 - sigma))).astype(BF16)
        return carry

    lax.fori_loop(0, 5, back_step, 0)
    mix[...] = grad_low[...]

    def normed_step(j, carry):
        hidden[:, tile(j, 256)] = dot_nt(grad_low[...], mats["h"][tile(j, 256), :])
        return carry

    lax.fori_loop(0, 5, normed_step, 0)
    links.sent_of("h")
    line_sent(("h", 0))
    line_sent(("h", 1))
    weight_grad("h", lambda j, right: dot_tn(norm2[:, tile(j, 256)], right))
    scatter_core("h")
    both("b", 0)
    vec_part[...] = jnp.zeros_like(vec_part)

    def middle_back(step, carry):
        rows = tile(step, 64)
        value = middle[rows, :]
        inverse = rms_inverse(value)
        unit = value * inverse
        grad = hidden[rows, :]
        vec_part[4:5, :] += jnp.sum(grad * unit, axis=0, keepdims=True)
        scaled = grad * vec_row[4:5, :WIDTH]
        inside = (s * ROWS + step * 64 + lax.broadcasted_iota(jnp.int32, (64, 1), 0)) < len_ref[0]
        base = jnp.where(inside, cot_ref[rows, :].astype(F32), 0.0)
        total = base + inverse * (scaled - unit * jnp.mean(scaled * unit, axis=-1, keepdims=True))
        ig_ref[rows, :] = total
        grad_low[rows, :] = total.astype(BF16)
        return carry

    lax.fori_loop(0, ROWS // 64, middle_back, 0)

    mix_whole.wait_send()

    def mixed_back(member, carry):
        mix_out[member] = dot_nt(mats["o"][tile(member, MINE), :], grad_low[...]).astype(BF16)
        return carry

    lax.fori_loop(0, 4, mixed_back, 0)
    for p in range(2):
        rows = slice(PAIR * p, PAIR * (p + 1))
        links.group(("gm", p), gmix_in.at[pl.ds(0, 3), rows])
        for k, device in ((2, y_dev), (3, yc_dev), (1, core_dev)):
            send(None, mix_out.at[peers[k], rows], gmix_in.at[s, rows], device, ("gm", p))
    gmix_in[s] = mix_out[s]
    scatter_far("h")

    def out_step(j, carry):
        cols = tile(j, 256)
        value = middle[:, cols] + dot_nn(active[...], mats["b"][:, cols])
        out_ref[:, cols] = jnp.where(valid, value, 0.0).astype(BF16)
        return carry

    lax.fori_loop(0, 5, out_step, 0)
    results.start(out_ref, out_hbm)
    links.sent_of("b")
    line_sent(("b", 0))
    line_sent(("b", 1))
    mixed_flat = mix_in.reshape(WIDTH, ROWS)
    weight_grad("o", lambda j, right: dot_nn(mixed_flat[tile(j, 256), :], right))
    scatter_core("o")

    def attend_back(h):
        rows = slice(HEAD_DIM * h, HEAD_DIM * (h + 1))
        dk_acc[...] = jnp.zeros_like(dk_acc)
        dv_acc[...] = jnp.zeros_like(dv_acc)
        for i in range(4):
            low, high = i * ROWS, (i + 1) * ROWS
            query = queries_t[rows, low:high]
            grad = gmix_in[i, rows, :]
            log_total = lse[h, :, low:high]
            spans = [(0, low), (low, high)] if i else [(low, high)]
            held = []
            inner = jnp.zeros((1, ROWS), F32)
            for first, last in spans:
                scores = dot_nn(keys[h, first:last, :], query)
                if first == low:
                    scores = jnp.where(allowed, scores, masked_score)
                probs = jnp.exp(scores - log_total)
                grad_probs = dot_nn(vals[h, first:last, :], grad)
                inner += jnp.sum(probs * grad_probs, axis=0, keepdims=True)
                held.append((first, last, probs, grad_probs))
            grad_query = jnp.zeros((HEAD_DIM, ROWS), F32)
            for first, last, probs, grad_probs in held:
                grad_scores = (probs * (grad_probs - inner)).astype(BF16)
                grad_query += dot_nn(keys_t[rows, first:last], grad_scores)
                dk_acc[first:last, :] += dot_nt(grad_scores, query)
                dv_acc[first:last, :] += dot_nt(probs.astype(BF16), grad)
            dq_t[HEAD_DIM * (h % 2) : HEAD_DIM * (h % 2 + 1), low:high] = grad_query
        first = PAIR + HEAD_DIM * (h % 2)
        grads[h // 2, :, first : first + HEAD_DIM] = dk_acc[...].astype(BF16)
        grads[h // 2, :, first + PAIR : first + PAIR + HEAD_DIM] = dv_acc[...].astype(BF16)

    def finish_pair(p):
        lanes = slice(PAIR * p, PAIR * (p + 1))
        pair_scale = scale[:, lanes]
        bias_grad = jnp.zeros((1, PAIR), F32)
        scale_grad = jnp.zeros((1, PAIR), F32)
        value_grad = jnp.zeros((1, PAIR), F32)
        grads[p, :, 3 * PAIR :] = jnp.zeros((SLOTS, PACK - 3 * PAIR), BF16)
        for i in range(4):
            rows = slice(i * ROWS, (i + 1) * ROWS)
            grad = dq_t[:, rows].T
            low_grad = (grad * pair_scale).astype(BF16)
            grads[p, rows, 0:PAIR] = low_grad
            bias_grad += jnp.sum(low_grad.astype(F32), axis=0, keepdims=True)
            scale_grad += jnp.sum(grad * queries_n[p, i].astype(F32), axis=0, keepdims=True)
            value_grad += jnp.sum(grads[p, rows, 2 * PAIR : 3 * PAIR].astype(F32), axis=0, keepdims=True)
        scale_grad = scale_grad / pair_scale * jax.nn.sigmoid(query_log[:, lanes]) * factor
        return bias_grad, scale_grad, value_grad

    def qkv_grad_pair(p):
        flat = qkv_part.at[p].reshape(WIDTH, PACK)

        def qkv_grad(j, carry):
            total = jnp.zeros((256, PACK), F32)
            for i in range(4):
                total += dot_tn(tokens[i, :, tile(j, 256)], grads[p, i * ROWS : (i + 1) * ROWS, :])
            flat[tile(j, 256), :] = total.astype(BF16)
            return carry

        lax.fori_loop(0, 5, qkv_grad, 0)
        sum_far(p)

    def qkv_sum_pair(p):
        links.sent(("a2a", p))
        if p in direct:
            direct_done(p)
        total = qkv_part[p, z, x].astype(F32)
        for member in range(4):
            stage[p, member] = total[SHARE * member : SHARE * (member + 1), :].astype(BF16)
        links.group(("ph", p), qkv_home.at[p, pl.ds(0, 3)])
        for k, device in ((2, y_dev), (3, yc_dev), (1, core_dev)):
            send(None, stage.at[p, peers[k]], qkv_home.at[p, s], device, ("ph", p))
        qkv_home[p, s] = stage[p, s]

    both("b", 1)
    recv(("gm", 0))
    attend_back(0)
    scatter_far("o")
    both("b", 2)
    attend_back(1)
    pair_grads = [finish_pair(0)]
    qkv_grad_pair(0)
    both("b", 3)
    scatter_last("b")
    both("h", 0)
    recv(("gm", 1))
    attend_back(2)
    attend_back(3)
    both("h", 1)
    pair_grads.append(finish_pair(1))
    qkv_grad_pair(1)
    both("h", 2)
    for row in range(3):
        value = jnp.concatenate([pair_grads[0][row], pair_grads[1][row]], axis=1)
        vec_part[row + 1 : row + 2, :] = jnp.concatenate(
            [jnp.where(s == member, value, 0.0) for member in range(4)], axis=1
        )

    def unit_rows(member):
        def unit_grad(j, carry):
            cols = tile(j, 256)
            value = dot_nt(grads[0, tile(member, ROWS), :], weights[0][cols, :])
            value += dot_nt(grads[1, tile(member, ROWS), :], weights[1][cols, :])
            tokens[member, :, cols] = value.astype(BF16)
            return carry

        lax.fori_loop(0, 5, unit_grad, 0)

    unit_rows((1 - y) * 2 + (1 - c))
    send(("uc", 1), tokens.at[(1 - y) * 2 + (1 - c)], unit_core.at[1], core_dev)
    far_member = (1 - y) * 2 + c
    sum_step(0, 0)
    unit_rows(far_member)
    recv(("uc", 1))
    tokens[far_member] = (tokens[far_member].astype(F32) + unit_core[1].astype(F32)).astype(BF16)
    send("uy", tokens.at[far_member], unit_far, y_dev)
    both("h", 3)
    scatter_last("h")
    sum_step(0, 1)
    unit_rows(y * 2 + (1 - c))
    send(("uc", 0), tokens.at[y * 2 + (1 - c)], unit_core.at[0], core_dev)
    cross()
    unit_rows(s)
    recv(("uc", 0))
    sum_step(0, 2)
    direct_start(1)
    sum_step(0, 3)
    qkv_sum_pair(0)
    direct_start(("o", 0))
    recv("uy")

    def unpack(p):
        recv(("ph", p))
        for index, ref in enumerate((gq_ref, gk_ref, gv_ref)):
            for member in range(4):
                first = MINE * member + PAIR * p
                ref[:, first : first + PAIR] = qkv_home[
                    p, member, :, PAIR * index : PAIR * (index + 1)
                ].astype(F32)

    def input_back(step, carry):
        rows = tile(step, 64)
        value = x_ref[rows, :].astype(F32)
        inverse = rms_inverse(value)
        unit = value * inverse
        grad = (
            tokens[s, rows, :].astype(F32) + unit_core[0, rows, :].astype(F32) + unit_far[rows, :].astype(F32)
        )
        vec_part[0:1, :] += jnp.sum(grad * unit, axis=0, keepdims=True)
        scaled = grad * vec_row[0:1, :WIDTH]
        ig_ref[rows, :] += inverse * (scaled - unit * jnp.mean(scaled * unit, axis=-1, keepdims=True))
        return carry

    lax.fori_loop(0, ROWS // 64, input_back, 0)
    results.start(ig_ref, ig_hbm)
    links.group("sg", vec_in.at[pl.ds(0, 3)])
    for k, device in ((2, y_dev), (3, yc_dev), (1, core_dev)):
        send(None, vec_part, vec_in.at[k - 1], device, "sg")
    scatter_sum("b")
    scatter_sum("h")
    recv("sg")
    links.sent("sg")
    vec_part[...] += vec_in[0] + vec_in[1] + vec_in[2]
    send("sx", vec_part, vec_in.at[3], x_dev)
    recv("sx")
    links.sent("sx")
    vec_part[...] += vec_in[3]
    links.group("sz", vec_in.at[pl.ds(4, 3)])
    for k in (1, 2, 3):
        send(None, vec_part, vec_in.at[3 + k], z_devs[k], "sz")
    scatter_done("b")
    scatter_done("h")
    qkv_sum_pair(1)
    direct_done(("o", 0))
    scatter_sum("o")
    unpack(0)
    recv("sz")
    total = vec_part[...] + vec_in[4] + vec_in[5] + vec_in[6]
    gvec_ref[...] = pltpu.roll(total, WIDTH - (d * 4 + s) * SHARE, 1)[:, :128]
    results.start(gvec_ref, gvec_hbm)
    scatter_done("o")
    unpack(1)
    for held, target in ((gq_ref, gq_hbm), (gk_ref, gk_hbm), (gv_ref, gv_hbm)):
        results.start(held, target)
    results.wait()
    links.sent_all()
    line_sent(("o", 0))
    line_sent(("o", 1))
    for stream in streams:
        sum_sent(stream)
    line_sent(0)
    line_sent(1)


def finish_kernel(*refs):
    sources, gvec, targets, held = refs[:8], refs[8], refs[9:22], refs[22:30]
    vectors, sems = refs[30:35], refs[35]
    places = (1, 0, 3, 6, 7, 9, 11, 12)
    rows = (2, 4, 5, 8, 10)
    loads = [pltpu.make_async_copy(sources[i], held[i], sems.at[0, i]) for i in range(8)]
    stores = [pltpu.make_async_copy(held[i], targets[places[i]], sems.at[1, i]) for i in range(8)]
    small = [pltpu.make_async_copy(vectors[i], targets[rows[i]], sems.at[1, 8 + i]) for i in range(5)]
    for copy in loads:
        copy.start()
    for row in range(5):
        vectors[row][...] = gvec[row, :SHARE]
        small[row].start()
    for load, store in zip(loads, stores):
        load.wait()
        store.start()
    for copy in stores + small:
        copy.wait()


def fused_shards(
    inputs,
    lengths,
    cotangent,
    gain_attn,
    w_query,
    bias_query,
    query_scale,
    w_key,
    w_value,
    bias_value,
    w_out,
    gain_mlp,
    w_hidden,
    w_back,
):
    vectors = sum(
        jnp.pad(value.astype(F32)[None], ((row, 7 - row), (0, 128 - SHARE)))
        for row, value in enumerate((gain_attn, bias_query, query_scale, bias_value, gain_mlp))
    )
    vmem = pl.BlockSpec(memory_space=pltpu.VMEM)
    whole = (4, 2, 4 * SHARE, WIDTH)
    buffers = [
        ((ROWS, WIDTH), BF16),
        ((ROWS, WIDTH), F32),
        ((8, 128), F32),
    ]
    buffers += [((SHARE, WIDTH), F32)] * 6
    buffers += [
        (whole, BF16),
        (whole, BF16),
        (whole, BF16),
        (whole, BF16),
        ((3, 2, 2, 4, 2 * SHARE, WIDTH // 2), BF16),
        ((6, 4, 2 * SHARE, WIDTH // 2), BF16),
        ((2, 6, 3, 2 * SHARE, WIDTH // 2), BF16),
        ((3, 2 * SHARE, WIDTH // 2), BF16),
        ((2, 8, 4 * SHARE, PACK), BF16),
        ((2, 4, SHARE, PACK), BF16),
        ((4, ROWS, WIDTH), BF16),
        ((4, SLOTS, HEAD_DIM), BF16),
        ((4, SLOTS, HEAD_DIM), BF16),
        ((MINE, SLOTS), BF16),
        ((MINE, SLOTS), BF16),
        ((MINE, SLOTS), BF16),
        ((2, 4, ROWS, PAIR), BF16),
        ((4, 1, SLOTS), F32),
        ((4, MINE, ROWS), BF16),
        ((4, MINE, ROWS), BF16),
        ((ROWS, WIDTH), BF16),
        ((ROWS, WIDTH), F32),
        ((ROWS, WIDTH), F32),
        ((ROWS, WIDTH), BF16),
        ((ROWS, WIDTH), BF16),
        ((4, MINE, ROWS), BF16),
        ((ROWS, WIDTH), BF16),
        ((SLOTS, HEAD_DIM), F32),
        ((SLOTS, HEAD_DIM), F32),
        ((PAIR, SLOTS), F32),
        ((2, SLOTS, PACK), BF16),
        ((2, ROWS, WIDTH), BF16),
        ((ROWS, WIDTH), BF16),
        ((2, 4, 2, 4 * SHARE, PACK), BF16),
        ((2, 4, 4 * SHARE, PACK), BF16),
        ((2, 2, 3, 4 * SHARE, PACK), BF16),
        ((2, 4, SHARE, PACK), BF16),
        ((2, 2, 4, 2, 8, 128), F32),
        ((8, WIDTH + 128), F32),
        ((8, WIDTH), F32),
        ((7, 8, WIDTH), F32),
        ((2, 4, SHARE, PACK), BF16),
        ((3, 2, SHARE, WIDTH // 2), BF16),
        ((3, SHARE, WIDTH // 2), F32),
        ((3, SHARE, WIDTH // 2), F32),
    ]
    scratch = [pltpu.VMEM(shape, kind) for shape, kind in buffers]
    scratch += [pltpu.SemaphoreType.DMA((9,))]
    dma = pltpu.SemaphoreType.DMA
    scratch += [dma, dma] + [dma((3, 8)), dma((2, 8, 3))] * 2 + [dma((2, 8))]
    scratch += [dma((COPIES,))] * 2
    square = jax.ShapeDtypeStruct((SHARE, WIDTH), F32)
    results = pl.pallas_call(
        layer_kernel,
        out_shape=(
            jax.ShapeDtypeStruct((ROWS, WIDTH), BF16),
            jax.ShapeDtypeStruct((ROWS, WIDTH), F32),
            jax.ShapeDtypeStruct((8, 128), F32),
            square,
            square,
            square,
            square,
            square,
            square,
        ),
        in_specs=[vmem, pl.BlockSpec(memory_space=pltpu.SMEM)] + [vmem] * 8,
        out_specs=tuple([pl.BlockSpec(memory_space=pl.ANY)] * 9),
        scratch_shapes=scratch,
        compiler_params=pltpu.CompilerParams(
            collective_id=0, has_side_effects=True, vmem_limit_bytes=66 * 1000 * 1000
        ),
        cost_estimate=pl.CostEstimate(flops=25_000_000_000, bytes_accessed=10_000_000, transcendentals=10_000_000),
    )(
        inputs.reshape(ROWS, WIDTH),
        lengths,
        cotangent.reshape(ROWS, WIDTH),
        vectors,
        w_query,
        w_key,
        w_value,
        w_out,
        w_hidden,
        w_back,
    )
    out, input_grad, gvec, gq, gk, gv, go, gh, gb = results
    moved = (input_grad, out, gq, gk, gv, go, gh, gb)
    anywhere = pl.BlockSpec(memory_space=pl.ANY)
    vector = jax.ShapeDtypeStruct((SHARE,), F32)
    shapes = [jax.ShapeDtypeStruct((ROWS, WIDTH), BF16), jax.ShapeDtypeStruct((ROWS, WIDTH), F32), vector, square]
    shapes += [vector, vector, square, square, vector, square, vector, square, square]
    done = pl.pallas_call(
        finish_kernel,
        out_shape=tuple(shapes),
        in_specs=[anywhere] * 8 + [vmem],
        out_specs=tuple([anywhere] * 13),
        scratch_shapes=[pltpu.VMEM(array.shape, array.dtype) for array in moved]
        + [pltpu.VMEM((SHARE,), F32)] * 5
        + [pltpu.SemaphoreType.DMA((2, 13))],
        compiler_params=pltpu.CompilerParams(vmem_limit_bytes=66 * 1000 * 1000),
    )(*moved, gvec)
    return (done[0].reshape(inputs.shape), done[1].reshape(inputs.shape), *done[2:])


def solution(mesh):
    placed = (
        P("dp", "seq", None),
        P("dp"),
        P("dp", "seq", None),
        P(("dp", "seq")),
        P(("dp", "seq"), None),
        P(("dp", "seq")),
        P(("dp", "seq")),
        P(("dp", "seq"), None),
        P(("dp", "seq"), None),
        P(("dp", "seq")),
        P(("dp", "seq"), None),
        P(("dp", "seq")),
        P(("dp", "seq"), None),
        P(("dp", "seq"), None),
    )
    return jax.shard_map(
        fused_shards if fits(mesh) else shards,
        mesh=mesh,
        in_specs=placed,
        out_specs=(
            P("dp", "seq", None),
            P("dp", "seq", None),
            P(("dp", "seq")),
            P(("dp", "seq"), None),
            P(("dp", "seq")),
            P(("dp", "seq")),
            P(("dp", "seq"), None),
            P(("dp", "seq"), None),
            P(("dp", "seq")),
            P(("dp", "seq"), None),
            P(("dp", "seq")),
            P(("dp", "seq"), None),
            P(("dp", "seq"), None),
        ),
        check_vma=False,
    )
```

```python
import math

import jax
import jax.numpy as jnp
from jax import lax
from jax.experimental import pallas as pl
from jax.experimental.pallas import tpu as pltpu
from jax.sharding import PartitionSpec as P

HEADS = 16
HEAD_DIM = 80


query_gain = 1.442695041
masked_score = -1e30


def normed(values):
    squares = jnp.mean(values * values, axis=-1, keepdims=True)
    inverse = lax.rsqrt(squares + 1e-06)
    return (values * inverse, inverse)


def norm_back(grad_in, unit, inverse, gain):
    scaled = grad_in * gain
    return inverse * (scaled - unit * jnp.mean(scaled * unit, axis=-1, keepdims=True))


def row_product(left, right):
    return lax.dot_general(
        left, right, (((0,), (0,)), ((), ())), preferred_element_type=jnp.float32
    )


def back_product(left, right):
    return lax.dot_general(
        left, right, (((1,), (1,)), ((), ())), preferred_element_type=jnp.float32
    )


def shards(
    inputs,
    lengths,
    cotangent,
    gain_attn,
    w_query,
    bias_query,
    query_scale,
    w_key,
    w_value,
    bias_value,
    w_out,
    gain_mlp,
    w_hidden,
    w_back,
):
    seq_dev, group_rows, width = inputs.shape
    tok_rows = seq_dev * group_rows
    head_count = HEADS
    head_width = HEAD_DIM
    gathered = (
        lax.all_gather(gain_attn, ("dp", "seq"), axis=0, tiled=True),
        lax.all_gather(w_query, ("dp", "seq"), axis=0, tiled=True),
        lax.all_gather(bias_query, ("dp", "seq"), axis=0, tiled=True),
        lax.all_gather(query_scale, ("dp", "seq"), axis=0, tiled=True),
        lax.all_gather(w_key, ("dp", "seq"), axis=0, tiled=True),
        lax.all_gather(w_value, ("dp", "seq"), axis=0, tiled=True),
        lax.all_gather(bias_value, ("dp", "seq"), axis=0, tiled=True),
        lax.all_gather(w_out, ("dp", "seq"), axis=0, tiled=True),
        lax.all_gather(gain_mlp, ("dp", "seq"), axis=0, tiled=True),
        lax.all_gather(w_hidden, ("dp", "seq"), axis=0, tiled=True),
        lax.all_gather(w_back, ("dp", "seq"), axis=0, tiled=True),
    )
    (
        norm_one,
        query_mat,
        query_bias,
        query_log,
        key_mat,
        value_mat,
        value_bias,
        output_mat,
        norm_two,
        hidden_mat,
        back_mat,
    ) = gathered
    ff_width = hidden_mat.shape[1]
    offset = lax.axis_index("seq") * group_rows
    place = offset + jnp.arange(group_rows, dtype=jnp.int32)
    valid = place[None, :] < lengths[:, None]
    row_valid = valid.reshape(tok_rows, 1)
    inputs_rows = inputs.reshape(tok_rows, width).astype(jnp.float32)
    unit_one, inverse_one = normed(inputs_rows)
    gain_one = norm_one.astype(jnp.float32)
    normed_one = (unit_one * gain_one).astype(jnp.bfloat16)
    query_raw = jnp.dot(
        normed_one, query_mat, preferred_element_type=jnp.float32
    ) + query_bias.astype(jnp.float32)
    query_logf = query_log.astype(jnp.float32)
    scale_vec = jax.nn.softplus(query_logf) * (query_gain / math.sqrt(head_width))
    queries = (query_raw * scale_vec).astype(jnp.bfloat16)
    keys_local = jnp.dot(normed_one, key_mat, preferred_element_type=jnp.float32).astype(
        jnp.bfloat16
    )
    values_local = (
        jnp.dot(normed_one, value_mat, preferred_element_type=jnp.float32)
        + value_bias.astype(jnp.float32)
    ).astype(jnp.bfloat16)
    keys_three = keys_local.reshape(seq_dev, group_rows, width)
    values_three = values_local.reshape(seq_dev, group_rows, width)
    queries_three = queries.reshape(seq_dev, group_rows, width)
    keys_all, values_all = (
        lax.all_gather(keys_three, "seq", axis=1, tiled=True),
        lax.all_gather(values_three, "seq", axis=1, tiled=True),
    )
    seq_slots = keys_all.shape[1]
    key_place = jnp.arange(seq_slots, dtype=jnp.int32)
    allowed = key_place[None, :] <= place[:, None]

    def attend(pieces):
        query_block, key_block, value_block = pieces
        query_heads = query_block.reshape(group_rows, head_count, head_width)
        key_heads = key_block.reshape(seq_slots, head_count, head_width)
        value_heads = value_block.reshape(seq_slots, head_count, head_width)
        scores = jnp.einsum(
            "qhd,khd->hqk", query_heads, key_heads, preferred_element_type=jnp.float32
        )
        scores = jnp.where(allowed[None], scores, masked_score)
        largest = jnp.max(scores, axis=-1, keepdims=True)
        raised = jnp.exp(scores - largest)
        totals = jnp.sum(raised, axis=-1, keepdims=True)
        weights_soft = (raised / totals).astype(jnp.bfloat16)
        mixed = jnp.einsum(
            "hqk,khd->qhd", weights_soft, value_heads, preferred_element_type=jnp.float32
        )
        log_total = largest[..., 0] + jnp.log(totals[..., 0])
        return (mixed.reshape(group_rows, width).astype(jnp.bfloat16), log_total)

    mixed_three, log_totals = lax.map(attend, (queries_three, keys_all, values_all))
    mixed = mixed_three.reshape(tok_rows, width)
    middle = inputs_rows + jnp.dot(mixed, output_mat, preferred_element_type=jnp.float32)
    unit_two, inverse_two = normed(middle)
    gain_two = norm_two.astype(jnp.float32)
    normed_two = (unit_two * gain_two).astype(jnp.bfloat16)
    hidden = jnp.dot(normed_two, hidden_mat, preferred_element_type=jnp.float32)
    active = jax.nn.silu(hidden).astype(jnp.bfloat16)
    result = middle + jnp.dot(active, back_mat, preferred_element_type=jnp.float32)
    outputs = (
        jnp.where(row_valid, result, 0.0).astype(jnp.bfloat16).reshape(seq_dev, group_rows, width)
    )
    again = (
        lax.all_gather(gain_attn, ("dp", "seq"), axis=0, tiled=True),
        lax.all_gather(w_query, ("dp", "seq"), axis=0, tiled=True),
        lax.all_gather(w_key, ("dp", "seq"), axis=0, tiled=True),
        lax.all_gather(w_value, ("dp", "seq"), axis=0, tiled=True),
        lax.all_gather(w_out, ("dp", "seq"), axis=0, tiled=True),
        lax.all_gather(gain_mlp, ("dp", "seq"), axis=0, tiled=True),
        lax.all_gather(w_hidden, ("dp", "seq"), axis=0, tiled=True),
        lax.all_gather(w_back, ("dp", "seq"), axis=0, tiled=True),
    )
    norm_one, query_mat, key_mat, value_mat, output_mat, norm_two, hidden_mat, back_mat = again
    gain_one = norm_one.astype(jnp.float32)
    gain_two = norm_two.astype(jnp.float32)
    keys_back, values_back = (
        lax.all_gather(keys_three, "seq", axis=1, tiled=True),
        lax.all_gather(values_three, "seq", axis=1, tiled=True),
    )
    cot_rows = cotangent.reshape(tok_rows, width)
    grad_out = jnp.where(row_valid, cot_rows, jnp.zeros_like(cot_rows))
    grad_active = back_product(grad_out, back_mat)
    sigma = jax.nn.sigmoid(hidden)
    grad_hidden = (grad_active * sigma * (1.0 + hidden * (1.0 - sigma))).astype(jnp.bfloat16)
    grad_normed_two = back_product(grad_hidden, hidden_mat)
    grad_gain_two = jnp.sum(grad_normed_two * unit_two, axis=0)
    grad_middle = grad_out.astype(jnp.float32) + norm_back(
        grad_normed_two, unit_two, inverse_two, gain_two
    )
    grad_middle_low = grad_middle.astype(jnp.bfloat16)
    grad_mixed = back_product(grad_middle_low, output_mat).astype(jnp.bfloat16)
    grad_mixed_three = grad_mixed.reshape(seq_dev, group_rows, width)

    def attend_query(pieces):
        query_block, key_block, value_block, grad_block, log_total = pieces
        query_heads = query_block.reshape(group_rows, head_count, head_width)
        key_heads = key_block.reshape(seq_slots, head_count, head_width)
        value_heads = value_block.reshape(seq_slots, head_count, head_width)
        grad_heads = grad_block.reshape(group_rows, head_count, head_width)
        scores = jnp.einsum(
            "qhd,khd->hqk", query_heads, key_heads, preferred_element_type=jnp.float32
        )
        scores = jnp.where(allowed[None], scores, masked_score)
        weights_soft = jnp.exp(scores - log_total[..., None])
        grad_soft = jnp.einsum(
            "qhd,khd->hqk", grad_heads, value_heads, preferred_element_type=jnp.float32
        )
        inner = jnp.sum(weights_soft * grad_soft, axis=-1, keepdims=True)
        grad_scores = (weights_soft * (grad_soft - inner)).astype(jnp.bfloat16)
        grad_queries = jnp.einsum(
            "hqk,khd->qhd", grad_scores, key_heads, preferred_element_type=jnp.float32
        )
        return (grad_queries.reshape(group_rows, width), inner[..., 0])

    grad_queries, inner_rows = lax.map(
        attend_query, (queries_three, keys_back, values_back, grad_mixed_three, log_totals)
    )
    queries_every, grad_every = (
        lax.all_gather(queries_three, "seq", axis=1, tiled=True),
        lax.all_gather(grad_mixed_three, "seq", axis=1, tiled=True),
    )
    lse_every, inner_every = (
        lax.all_gather(log_totals, "seq", axis=2, tiled=True),
        lax.all_gather(inner_rows, "seq", axis=2, tiled=True),
    )
    later = key_place[:, None] >= place[None, :]

    def key_side(pieces):
        query_block, grad_block, key_block, value_block, lse_block, inner_block = pieces
        query_heads = query_block.reshape(seq_slots, head_count, head_width)
        grad_heads = grad_block.reshape(seq_slots, head_count, head_width)
        key_heads = key_block.reshape(group_rows, head_count, head_width)
        value_heads = value_block.reshape(group_rows, head_count, head_width)
        scores = jnp.einsum(
            "qhd,khd->hqk", query_heads, key_heads, preferred_element_type=jnp.float32
        )
        scores = jnp.where(later[None], scores, masked_score)
        weights_soft = jnp.exp(scores - lse_block[..., None])
        weights_low = weights_soft.astype(jnp.bfloat16)
        grad_soft = jnp.einsum(
            "qhd,khd->hqk", grad_heads, value_heads, preferred_element_type=jnp.float32
        )
        grad_scores = (weights_soft * (grad_soft - inner_block[..., None])).astype(jnp.bfloat16)
        grad_keys = jnp.einsum(
            "hqk,qhd->khd", grad_scores, query_heads, preferred_element_type=jnp.float32
        )
        grad_values = jnp.einsum(
            "hqk,qhd->khd", weights_low, grad_heads, preferred_element_type=jnp.float32
        )
        return (grad_keys.reshape(group_rows, width), grad_values.reshape(group_rows, width))

    grad_keys_sum, grad_values_sum = lax.map(
        key_side, (queries_every, grad_every, keys_three, values_three, lse_every, inner_every)
    )
    grad_keys = grad_keys_sum.reshape(tok_rows, width).astype(jnp.bfloat16)
    grad_values = grad_values_sum.reshape(tok_rows, width).astype(jnp.bfloat16)
    grad_queries = grad_queries.reshape(tok_rows, width)
    grad_query_raw = (grad_queries * scale_vec).astype(jnp.bfloat16)
    grad_scale = jnp.sum(grad_queries * query_raw, axis=0)
    grad_query_log = grad_scale * jax.nn.sigmoid(query_logf) * (query_gain / math.sqrt(head_width))
    grad_query_bias = jnp.sum(grad_query_raw.astype(jnp.float32), axis=0)
    grad_value_bias = jnp.sum(grad_values.astype(jnp.float32), axis=0)
    grad_normed_one = (
        back_product(grad_query_raw, query_mat)
        + back_product(grad_keys, key_mat)
        + back_product(grad_values, value_mat)
    )
    grad_gain_one = jnp.sum(grad_normed_one * unit_one, axis=0)
    input_grad = grad_middle + norm_back(grad_normed_one, unit_one, inverse_one, gain_one)
    dp_count = lax.axis_size("dp")
    seq_count = lax.axis_size("seq")
    share = width // (dp_count * seq_count)
    share_ff = ff_width // (dp_count * seq_count)
    left_parts = (
        lax.all_to_all(
            normed_one.reshape(tok_rows, dp_count, seq_count, share),
            "seq",
            split_axis=2,
            concat_axis=0,
            tiled=True,
        ),
        lax.all_to_all(
            mixed.reshape(tok_rows, dp_count, seq_count, share),
            "seq",
            split_axis=2,
            concat_axis=0,
            tiled=True,
        ),
        lax.all_to_all(
            normed_two.reshape(tok_rows, dp_count, seq_count, share),
            "seq",
            split_axis=2,
            concat_axis=0,
            tiled=True,
        ),
        lax.all_to_all(
            active.reshape(tok_rows, dp_count, seq_count, share_ff),
            "seq",
            split_axis=2,
            concat_axis=0,
            tiled=True,
        ),
    )
    left_normed_one = left_parts[0].reshape(-1, dp_count * share)
    left_mixed = left_parts[1].reshape(-1, dp_count * share)
    left_normed_two = left_parts[2].reshape(-1, dp_count * share)
    left_active = left_parts[3].reshape(-1, dp_count * share_ff)
    right_parts = (
        lax.all_gather(grad_query_raw, "seq", axis=0, tiled=True),
        lax.all_gather(grad_keys, "seq", axis=0, tiled=True),
        lax.all_gather(grad_values, "seq", axis=0, tiled=True),
        lax.all_gather(grad_middle_low, "seq", axis=0, tiled=True),
        lax.all_gather(grad_hidden, "seq", axis=0, tiled=True),
        lax.all_gather(grad_out, "seq", axis=0, tiled=True),
    )
    right_query, right_keys, right_values, right_middle, right_hidden, right_out = right_parts
    part_query_mat = row_product(left_normed_one, right_query)
    part_key_mat = row_product(left_normed_one, right_keys)
    part_value_mat = row_product(left_normed_one, right_values)
    part_output_mat = row_product(left_mixed, right_middle)
    part_hidden_mat = row_product(left_normed_two, right_hidden)
    part_back_mat = row_product(left_active, right_out)
    matrices = (
        lax.psum_scatter(
            part_query_mat.astype(jnp.bfloat16), "dp", scatter_dimension=0, tiled=True
        ).astype(jnp.float32),
        lax.psum_scatter(
            part_key_mat.astype(jnp.bfloat16), "dp", scatter_dimension=0, tiled=True
        ).astype(jnp.float32),
        lax.psum_scatter(
            part_value_mat.astype(jnp.bfloat16), "dp", scatter_dimension=0, tiled=True
        ).astype(jnp.float32),
        lax.psum_scatter(
            part_output_mat.astype(jnp.bfloat16), "dp", scatter_dimension=0, tiled=True
        ).astype(jnp.float32),
        lax.psum_scatter(
            part_hidden_mat.astype(jnp.bfloat16), "dp", scatter_dimension=0, tiled=True
        ).astype(jnp.float32),
        lax.psum_scatter(
            part_back_mat.astype(jnp.bfloat16), "dp", scatter_dimension=0, tiled=True
        ).astype(jnp.float32),
    )
    vectors = (
        lax.psum_scatter(grad_gain_one, ("dp", "seq"), scatter_dimension=0, tiled=True),
        lax.psum_scatter(grad_query_bias, ("dp", "seq"), scatter_dimension=0, tiled=True),
        lax.psum_scatter(grad_query_log, ("dp", "seq"), scatter_dimension=0, tiled=True),
        lax.psum_scatter(grad_value_bias, ("dp", "seq"), scatter_dimension=0, tiled=True),
        lax.psum_scatter(grad_gain_two, ("dp", "seq"), scatter_dimension=0, tiled=True),
    )
    return (
        outputs,
        input_grad.reshape(seq_dev, group_rows, width),
        vectors[0],
        matrices[0],
        vectors[1],
        vectors[2],
        matrices[1],
        matrices[2],
        vectors[3],
        matrices[3],
        vectors[4],
        matrices[4],
        matrices[5],
    )


F32 = jnp.float32
BF16 = jnp.bfloat16
MESH_ID = pl.DeviceIdType.MESH
ROWS = 256
WIDTH = 1280
SHARE = 40
MINE = 320
SLOTS = 1024
PACK = 512
PAIR = 160
COPIES = 38


def fits(mesh):
    return mesh.shape["dp"] == 8 and mesh.shape["seq"] == 4


def dot_nn(left, right):
    return jnp.dot(left, right, preferred_element_type=F32)


def dot_nt(left, right):
    return lax.dot_general(left, right, (((1,), (1,)), ((), ())), preferred_element_type=F32)


def dot_tn(left, right):
    return lax.dot_general(left, right, (((0,), (0,)), ((), ())), preferred_element_type=F32)


def tile(index, size):
    return pl.ds(pl.multiple_of(index * size, size), size)


def strip(yy):
    return pl.ds(pl.multiple_of(yy * 2 * SHARE, 16), 2 * SHARE)


def half(cc):
    return pl.ds(pl.multiple_of(cc * (WIDTH // 2), 128), WIDTH // 2)


class Outputs:
    def __init__(self, sems):
        self.sems, self.open = sems, []

    def start(self, held, target):
        copy = pltpu.make_async_copy(held, target, self.sems.at[len(self.open)])
        copy.start()
        self.open.append(copy)

    def wait(self):
        for copy in self.open:
            copy.wait()


class Links:
    def __init__(self, send_sems, recv_sems, device):
        self.send_sems, self.recv_sems, self.device = send_sems, recv_sems, device
        self.count = 0
        self.open = {}

    def copy(self, index, src, dst, device):
        return pltpu.make_async_remote_copy(
            src_ref=src,
            dst_ref=dst,
            send_sem=self.send_sems.at[index],
            recv_sem=self.recv_sems.at[index],
            device_id=device,
            device_id_type=MESH_ID,
        )

    def next_index(self):
        self.count += 1
        assert self.count <= COPIES
        return self.count - 1

    def group(self, key, whole):
        self.open[key] = self.copy(self.next_index(), whole, whole, self.device), self.count - 1

    def send(self, key, src, dst, device, group=None):
        if group is not None:
            self.copy(self.open[group][1], src, dst, device).start()
            return
        index = self.next_index()
        copy = self.copy(index, src, dst, device)
        copy.start()
        self.open[key] = copy, index

    def recv(self, *keys):
        for key in keys:
            self.open[key][0].wait_recv()

    def sent(self, *keys):
        for key in keys:
            self.open.pop(key)[0].wait_send()

    def sent_of(self, name):
        for key in list(self.open):
            if key[0] == name:
                self.sent(key)

    def sent_all(self):
        self.sent(*list(self.open))


def layer_kernel(
    x_ref,
    len_ref,
    cot_ref,
    gain_ref,
    query_bias_ref,
    query_scale_ref,
    value_bias_ref,
    gain_mlp_ref,
    wq_ref,
    wk_ref,
    wv_ref,
    wo_ref,
    wh_ref,
    wb_ref,
    out_hbm,
    ig_hbm,
    gvec_hbm,
    gq_hbm,
    gk_hbm,
    gv_hbm,
    go_hbm,
    gh_hbm,
    gb_hbm,
    out_ref,
    ig_ref,
    gvec_ref,
    vec_ref,
    gq_ref,
    gk_ref,
    gv_ref,
    go_ref,
    gh_ref,
    gb_ref,
    full_o,
    full_h,
    full_b,
    part_b,
    core_in,
    far_in,
    line_in,
    last_in,
    qkv_w,
    stage,
    tokens,
    keys,
    vals,
    queries_t,
    keys_t,
    vals_t,
    queries_n,
    lse,
    mix_out,
    mix_in,
    mix,
    middle,
    hidden,
    norm2,
    active,
    gmix_in,
    grad_low,
    dk_acc,
    dv_acc,
    dq_t,
    grads,
    unit_core,
    unit_far,
    qkv_part,
    qkv_near,
    qkv_line,
    qkv_home,
    vec_slots,
    vec_row,
    vec_part,
    vec_in,
    qkv_own,
    pair_in,
    give_out,
    give_in,
    out_sems,
    mix_send,
    mix_recv,
    line_send,
    line_recv,
    sum_send,
    sum_recv,
    far_recv,
    send_sems,
    recv_sems,
):
    d = lax.axis_index("dp")
    s = lax.axis_index("seq")
    z, x = d // 2, d % 2
    y, c = s // 2, s % 2
    results = Outputs(out_sems)
    core_dev = (d, y * 2 + (1 - c))
    links = Links(send_sems, recv_sems, core_dev)
    send, recv = links.send, links.recv
    y_dev = (d, (1 - y) * 2 + c)
    yc_dev = (d, (1 - y) * 2 + (1 - c))
    x_dev = (z * 2 + (1 - x), s)
    zs = [None] + [(z + k) % 4 for k in range(1, 4)]
    from_z = [None] + [(z + 4 - k) % 4 for k in range(1, 4)]
    z_devs = [None] + [(zs[k] * 2 + x, s) for k in range(1, 4)]

    barrier = pltpu.get_barrier_semaphore()
    for device in (core_dev, y_dev, yc_dev, x_dev, z_devs[1], z_devs[2], z_devs[3]):
        pl.semaphore_signal(barrier, inc=1, device_id=device, device_id_type=MESH_ID)

    for member in range(4):
        for p in range(2):
            cols = slice(MINE * member + PAIR * p, MINE * member + PAIR * (p + 1))
            stage[p, member] = jnp.concatenate(
                [wq_ref[:, cols], wk_ref[:, cols], wv_ref[:, cols], jnp.zeros((SHARE, PACK - 3 * PAIR), BF16)],
                axis=1,
            )
    for p in range(2):
        qkv_own[p, s] = stage[p, s]
    tokens[s] = x_ref[...]
    vec_ref[...] = jnp.zeros_like(vec_ref)
    for row, ref in enumerate((gain_ref, query_bias_ref, query_scale_ref, value_bias_ref, gain_mlp_ref)):
        vec_ref[row : row + 1, :SHARE] = ref[...].astype(F32)
    vec_slots[y, x, z, c] = vec_ref[...]
    shards = {"o": wo_ref, "h": wh_ref, "b": wb_ref}
    slot_of = {"o": 0, "h": 1, "b": 2}
    for m in "ohb":
        pair_in[slot_of[m], c] = shards[m][:, half(c)]
    pl.semaphore_wait(barrier, 7)

    group = ((1, core_dev), (2, y_dev), (3, yc_dev))
    peers = (None, y * 2 + (1 - c), (1 - y) * 2 + c, (1 - y) * 2 + (1 - c))
    def to_group(p):
        links.group(("a2a", p), qkv_own.at[p, pl.ds(0, 3)])
        for k, device in ((2, y_dev), (3, yc_dev), (1, core_dev)):
            send(None, stage.at[p, peers[k]], qkv_own.at[p, s], device, ("a2a", p))

    fulls = {"o": full_o, "h": full_h, "b": full_b}
    first_x = {"o": 1, "h": 0, "b": 1 - c}
    last_x = {"b": c, "h": c, "o": 1}
    last_x_other = {"b": 1 - c, "h": 1 - c, "o": 1}

    def spot(along, first, second):
        on_x = along * first + (1 - along) * second
        on_y = along * second + (1 - along) * first
        return (x + on_x) % 2, strip((y + on_y) % 2)

    def devs_of(along):
        def device(on_x):
            return ((z * 2 + (x + on_x) % 2), ((y + 1 - on_x) % 2) * 2 + c)

        return device(along), device(1 - along)

    up_dev = (jnp.minimum(z + 1, 3) * 2 + x, s)
    down_dev = (jnp.maximum(z - 1, 0) * 2 + x, s)
    streams = [0, 1] + [(m, e) for m in "ohb" for e in (0, 1)]

    def line_piece(stream, zz, far):
        if stream in (0, 1):
            return qkv_w.at[stream, zz * 2 + (x + far) % 2]
        m, e = stream
        xx, rows = spot(first_x[m], e, far)
        return fulls[m].at[zz, xx, rows, half(c)]

    def line_copy(kind, stream, hop, zz):
        if kind == 2:
            device = x_dev if stream in (0, 1) else devs_of(first_x[stream[0]])[1]
        else:
            device = (up_dev, down_dev)[kind]
        index = streams.index(stream)
        piece = line_piece(stream, zz, 0)
        return pltpu.make_async_remote_copy(
            src_ref=piece,
            dst_ref=piece,
            send_sem=line_send.at[kind, index],
            recv_sem=far_recv.at[0, index] if kind == 2 else line_recv.at[kind, index, hop - 1],
            device_id=device,
            device_id_type=MESH_ID,
        )

    def pieces(stream, count, sends, recvs):
        if stream in (0, 1):
            whole = qkv_w.at[stream, pl.ds(0, count)]
        else:
            whole = fulls[stream[0]].at[pl.ds(0, count), 0, pl.ds(0, 2 * SHARE), half(c)]
        return pltpu.make_async_remote_copy(
            src_ref=whole,
            dst_ref=whole,
            send_sem=sends,
            recv_sem=recvs,
            device_id=core_dev,
            device_id_type=MESH_ID,
        )

    def line_far(stream, zz):
        line_copy(2, stream, zz, zz).start()

    def line_first(stream):
        @pl.when(z < 3)
        def _():
            line_copy(0, stream, 1, z).start()

        @pl.when(z > 0)
        def _():
            line_copy(1, stream, 1, z).start()

        line_far(stream, z)

    def line_step(stream, hop):
        @pl.when(z >= hop)
        def _():
            line_copy(0, stream, hop, z - hop).wait_recv()
            if hop < 3:

                @pl.when(z < 3)
                def _():
                    line_copy(0, stream, hop + 1, z - hop).start()

            line_far(stream, z - hop)

        @pl.when(z + hop <= 3)
        def _():
            line_copy(1, stream, hop, z + hop).wait_recv()
            if hop < 3:

                @pl.when(z > 0)
                def _():
                    line_copy(1, stream, hop + 1, z + hop).start()

            line_far(stream, z + hop)

    def line_done(stream):
        index = streams.index(stream)
        pieces(stream, 4, line_send.at[2, index], far_recv.at[0, index]).wait_recv()

    def line_sent(stream):
        index = streams.index(stream)
        for zz in range(3):

            @pl.when(z == zz)
            def _():
                pieces(stream, zz + 1, line_send.at[0, index], far_recv.at[0, index]).wait_send()

            @pl.when(z == zz + 1)
            def _():
                pieces(stream, 3 - zz, line_send.at[1, index], far_recv.at[0, index]).wait_send()

        pieces(stream, 4, line_send.at[2, index], far_recv.at[0, index]).wait_send()

    def to_core(m, far):
        if far == 0:
            links.group((m, "c"), fulls[m].at[:, :, :, half(c)])
        for e in (0, 1):
            xx, rows = spot(first_x[m], e, far)
            piece = fulls[m].at[:, xx, rows, half(c)]
            send(None, piece, piece, core_dev, (m, "c"))

    def gather_side(m):
        to_core(m, 0)

    def gather_core(m):
        line_done((m, 0))
        line_done((m, 1))
        to_core(m, 1)

    def gather_done(m):
        recv((m, "c"))

    def own_rows(p):
        recv(("a2a", p))
        qkv_w[p, d] = jnp.concatenate([qkv_own[p, member] for member in range(4)], axis=0)

    def own_first(m):
        if m == "o":
            recv("pair")
        piece = jnp.concatenate([pair_in[slot_of[m], 0], pair_in[slot_of[m], 1]], axis=0)
        fulls[m][z, x, strip(y), half(c)] = piece
        mine = fulls[m].at[z, x, strip(y), half(c)]
        send((m, "first"), mine, mine, devs_of(first_x[m])[0])

    to_group(0)
    links.group("pair", pair_in.at[:, 0])
    for m in "ohb":
        send(None, shards[m].at[:, half(1 - c)], pair_in.at[slot_of[m], c], core_dev, "pair")
    send("vy", vec_ref, vec_slots.at[y, x, z, c], y_dev)
    to_group(1)
    own_first("o")
    send("xy", x_ref, tokens.at[s], y_dev)
    send("xc", x_ref, tokens.at[s], core_dev)
    own_first("h")
    own_first("b")
    own_rows(0)
    line_first(0)
    recv("vy")
    piece = vec_slots.at[:, x, z, c]
    send("vx", piece, piece, x_dev)
    line_first(("o", 0))
    own_rows(1)
    recv("vx")
    links.group("vz", vec_slots.at[:, :, pl.ds(0, 3), c])
    for k in (1, 2, 3):
        piece = vec_slots.at[:, :, z, c]
        send(None, piece, piece, z_devs[k], "vz")
    line_step(0, 1)
    line_first(1)
    line_step(0, 2)
    recv("vz")
    piece = vec_slots.at[:, :, :, c]
    send("vc", piece, piece, core_dev)
    recv(("o", "first"))
    line_first(("o", 1))
    line_step(0, 3)
    line_step(1, 1)
    recv("vc")
    vec_row[...] = jnp.zeros_like(vec_row)
    for slot in range(32):
        start = slot * SHARE
        low = start // 128 * 128
        piece = jnp.concatenate(
            [vec_slots[slot // 2 % 2, slot // 4 % 2, slot // 8, slot % 2], jnp.zeros((8, 128), F32)], axis=1
        )
        if start > low:
            piece = pltpu.roll(piece, start - low, 1)
        vec_row[:, low : low + 256] += piece

    def norm_of(member, count):
        def norm_rows(step, carry):
            for j in range(count):
                rows = tile(step, 64)
                value = tokens[member + j, rows, :].astype(F32)
                unit = value * lax.rsqrt(jnp.mean(value * value, axis=-1, keepdims=True) + 1e-06)
                tokens[member + j, rows, :] = (unit * vec_row[0:1, :WIDTH]).astype(BF16)
            return carry

        lax.fori_loop(0, ROWS // 64, norm_rows, 0)

    recv("xc")
    norm_of(y * 2, 2)
    line_step(("o", 0), 1)
    recv("xy")
    piece = tokens.at[peers[2]]
    send("xyc", piece, piece, core_dev)
    line_step(1, 2)
    line_step(("o", 1), 1)
    recv("xyc")
    links.sent("xyc")
    norm_of((1 - y) * 2, 2)

    def own(row):
        value = vec_row[row : row + 1, 0:MINE]
        for member in range(1, 4):
            value = jnp.where(s == member, vec_row[row : row + 1, MINE * member : MINE * (member + 1)], value)
        return value

    query_log = own(2)
    factor = query_gain / math.sqrt(HEAD_DIM)
    scale = (jnp.maximum(query_log, 0.0) + jnp.log1p(jnp.exp(-jnp.abs(query_log)))) * factor
    query_bias, value_bias = own(1), own(3)

    weights = [qkv_w.at[p].reshape(WIDTH, PACK) for p in range(2)]

    def project_pair(p):
        lanes = slice(PAIR * p, PAIR * (p + 1))

        def project(i, carry):
            rows = tile(i, ROWS)
            raw = dot_nn(tokens[i], weights[p][...])
            query = ((raw[:, :PAIR] + query_bias[:, lanes]) * scale[:, lanes]).astype(BF16)
            key = raw[:, PAIR : 2 * PAIR].astype(BF16)
            val = (raw[:, 2 * PAIR : 3 * PAIR] + value_bias[:, lanes]).astype(BF16)
            queries_n[p, i] = query
            queries_t[lanes, rows] = query.T
            keys_t[lanes, rows] = key.T
            vals_t[lanes, rows] = val.T
            for h in range(2):
                keys[2 * p + h, rows, :] = key[:, HEAD_DIM * h : HEAD_DIM * (h + 1)]
                vals[2 * p + h, rows, :] = val[:, HEAD_DIM * h : HEAD_DIM * (h + 1)]
            return carry

        lax.fori_loop(0, 4, project, 0)

    key_place = lax.broadcasted_iota(jnp.int32, (ROWS, ROWS), 0)
    query_place = lax.broadcasted_iota(jnp.int32, (ROWS, ROWS), 1)
    allowed = key_place <= query_place

    def attend(p, i):
        low, high = i * ROWS, (i + 1) * ROWS

        def head(h, carry):
            rows = tile(h, HEAD_DIM)
            query = queries_t[rows, low:high]
            near = jnp.where(allowed, dot_nn(keys[h, low:high, :], query), masked_score)
            largest = jnp.max(near, axis=0, keepdims=True)
            if i:
                before = dot_nn(keys[h, 0:low, :], query)
                largest = jnp.maximum(largest, jnp.max(before, axis=0, keepdims=True))
            near = jnp.exp(near - largest)
            total = jnp.sum(near, axis=0, keepdims=True)
            mixed = dot_nn(vals_t[rows, low:high], near.astype(BF16))
            if i:
                before = jnp.exp(before - largest)
                total += jnp.sum(before, axis=0, keepdims=True)
                mixed += dot_nn(vals_t[rows, 0:low], before.astype(BF16))
            lse[h, :, low:high] = largest + jnp.log(total)
            mix_out[i, rows, :] = (mixed / total).astype(BF16)
            return carry

        lax.fori_loop(2 * p, 2 * p + 2, head, 0)

    def mix_copy(p, dest, source):
        return pltpu.make_async_remote_copy(
            src_ref=mix_out.at[dest, PAIR * p : PAIR * (p + 1)],
            dst_ref=mix_in.at[source, PAIR * p : PAIR * (p + 1)],
            send_sem=mix_send,
            recv_sem=mix_recv,
            device_id=(d, dest),
            device_id_type=MESH_ID,
        )

    def attend_and_send(p, i):
        attend(p, i)

        @pl.when(s != i)
        def _():
            mix_copy(p, i, s).start()

        @pl.when(s == i)
        def _():
            mix_in[i, PAIR * p : PAIR * (p + 1)] = mix_out[i, PAIR * p : PAIR * (p + 1)]

    line_done(0)
    project_pair(0)
    line_step(1, 3)
    line_step(("o", 0), 2)
    attend_and_send(0, 3)
    recv(("h", "first"))
    line_first(("h", 0))
    line_step(("o", 1), 2)
    attend_and_send(0, 2)
    line_first(("h", 1))
    line_step(("o", 0), 3)
    attend_and_send(0, 1)
    line_step(("o", 1), 3)
    gather_side("o")
    attend_and_send(0, 0)
    line_step(("h", 0), 1)
    recv(("b", "first"))
    line_first(("b", 0))
    line_done(1)
    project_pair(1)
    line_step(("h", 1), 1)
    line_first(("b", 1))
    attend_and_send(1, 3)
    line_step(("h", 0), 2)
    line_step(("h", 1), 2)
    gather_core("o")
    attend_and_send(1, 2)
    line_step(("b", 0), 1)
    line_step(("b", 1), 1)
    attend_and_send(1, 1)
    line_step(("h", 0), 3)
    line_step(("h", 1), 3)
    attend_and_send(1, 0)
    gather_side("h")
    mix_whole = pltpu.make_async_remote_copy(
        src_ref=mix_in.at[pl.ds(0, 3)],
        dst_ref=mix_in.at[pl.ds(0, 3)],
        send_sem=mix_send,
        recv_sem=mix_recv,
        device_id=core_dev,
        device_id_type=MESH_ID,
    )
    mix_whole.wait_recv()
    gather_done("o")

    mix[...] = mix_in[...].reshape(WIDTH, ROWS).T
    mats = {m: fulls[m].reshape(WIDTH, WIDTH) for m in "ohb"}

    def middle_step(j, carry):
        cols = tile(j, 256)
        middle[:, cols] = x_ref[:, cols].astype(F32) + dot_nn(mix[...], mats["o"][:, cols])
        return carry

    lax.fori_loop(0, 5, middle_step, 0)

    def rms_inverse(value):
        return lax.rsqrt(jnp.mean(value * value, axis=-1, keepdims=True) + 1e-06)

    def norm_two(step, carry):
        rows = tile(step, 64)
        value = middle[rows, :]
        norm2[rows, :] = (value * rms_inverse(value) * vec_row[4:5, :WIDTH]).astype(BF16)
        return carry

    lax.fori_loop(0, ROWS // 64, norm_two, 0)
    line_step(("b", 0), 2)
    line_step(("b", 1), 2)
    gather_core("h")
    gather_done("h")

    def hidden_step(j, carry):
        cols = tile(j, 256)
        value = dot_nn(norm2[...], mats["h"][:, cols])
        hidden[:, cols] = value
        active[:, cols] = (value * jax.nn.sigmoid(value)).astype(BF16)
        return carry

    lax.fori_loop(0, 5, hidden_step, 0)

    place = s * ROWS + lax.broadcasted_iota(jnp.int32, (ROWS, 1), 0)
    valid = place < len_ref[0]

    def grad_y():
        return jnp.where(valid, cot_ref[...], jnp.zeros((ROWS, WIDTH), BF16))

    parts = {"b": part_b, "h": full_h, "o": full_b}
    outs = {"b": gb_ref, "h": gh_ref, "o": go_ref}
    outs_hbm = {"b": gb_hbm, "h": gh_hbm, "o": go_hbm}
    order = {"b": 0, "h": 1, "o": 2}

    def weight_grad(m, left):
        flat = parts[m].reshape(WIDTH, WIDTH)
        right = {"b": grad_y, "h": lambda: mix[...], "o": lambda: grad_low[...]}[m]()

        def step(j, carry):
            flat[tile(j, 256), :] = left(j, right).astype(BF16)
            return carry

        lax.fori_loop(0, 5, step, 0)

    def sum_piece(stream, zz, far):
        if stream in (0, 1):
            return qkv_part.at[stream, zz, (x + far) % 2]
        m, e = stream
        xx, rows = spot(last_x[m], e, far)
        return parts[m].at[zz, xx, rows, half(c)]

    def sum_in(kind, stream, zz):
        if stream in (0, 1):
            return qkv_near.at[stream, zz] if kind == 2 else qkv_line.at[kind, stream, zz - 1 + kind]
        index = streams.index(stream) - 2
        return far_in.at[index, zz] if kind == 2 else line_in.at[kind, index, zz - 1 + kind]

    def sum_copy(kind, stream, zz):
        if kind == 2:
            device = x_dev if stream in (0, 1) else devs_of(last_x[stream[0]])[1]
        else:
            device = (up_dev, down_dev)[kind]
        index = streams.index(stream)
        return pltpu.make_async_remote_copy(
            src_ref=sum_piece(stream, zz, kind // 2),
            dst_ref=sum_in(kind, stream, zz),
            send_sem=sum_send.at[kind, index],
            recv_sem=far_recv.at[1, index] if kind == 2 else sum_recv.at[kind, index, zz - 1 + kind],
            device_id=device,
            device_id_type=MESH_ID,
        )

    def add_in(kind, stream, zz):
        if kind < 2:
            sum_copy(kind, stream, zz).wait_recv()
        piece = sum_piece(stream, zz, 0)
        piece[...] = (piece[...].astype(F32) + sum_in(kind, stream, zz)[...].astype(F32)).astype(BF16)

    def add_far(stream):
        index = streams.index(stream)
        pieces(stream, 4, sum_send.at[2, index], far_recv.at[1, index]).wait_recv()
        for zz in range(4):
            add_in(2, stream, zz)

    def sum_far(stream):
        for zz in (3, 0, 2, 1):
            sum_copy(2, stream, zz).start()

    def near_copy(zz):
        return pltpu.make_async_remote_copy(
            src_ref=sum_piece(("o", 1), zz, 0),
            dst_ref=line_in.at[zz // 3, 1, zz % 3],
            send_sem=sum_send.at[0, 3],
            recv_sem=sum_recv.at[0, 3, 0],
            device_id=devs_of(last_x["o"])[0],
            device_id_type=MESH_ID,
        )

    def cross():
        add_far(("o", 1))
        for zz in (3, 0, 2, 1):
            near_copy(zz).start()

    def add_near():
        pieces(("o", 1), 4, sum_send.at[0, 3], sum_recv.at[0, 3, 0]).wait_recv()
        for zz in range(4):
            piece = sum_piece(("o", 0), zz, 0)
            piece[...] = (piece[...].astype(F32) + line_in[zz // 3, 1, zz % 3].astype(F32)).astype(BF16)

    def sum_step(stream, step):
        if step == 0:
            add_far(stream)
            if stream == ("o", 0):
                add_near()
        above, below = z + 3 - step, z + step - 3

        @pl.when((z >= 1) & (z <= step))
        def _():
            add_in(0, stream, above)

        @pl.when((z <= 2) & (3 - z <= step))
        def _():
            add_in(1, stream, below)

        if step < 3:

            @pl.when((z <= step) & (z > 0))
            def _():
                sum_copy(0, stream, above).start()

            @pl.when((3 - z <= step) & (z < 3))
            def _():
                sum_copy(1, stream, below).start()

        if step == 0:
            @pl.when(z == 0)
            def _():
                for zz in (3, 2, 1):
                    sum_copy(0, stream, zz).start()

            @pl.when(z == 3)
            def _():
                for zz in (0, 1, 2):
                    sum_copy(1, stream, zz).start()

    direct = (1, ("o", 0),)

    def direct_copy(stream, k):
        index = streams.index(stream)
        return pltpu.make_async_remote_copy(
            src_ref=sum_piece(stream, zs[k], 0),
            dst_ref=sum_in(0, stream, k),
            send_sem=sum_send.at[0, index],
            recv_sem=sum_recv.at[0, index, 0],
            device_id=z_devs[k],
            device_id_type=MESH_ID,
        )

    def direct_start(stream):
        add_far(stream)
        if stream == ("o", 0):
            add_near()
        for k in (2, 1, 3):
            direct_copy(stream, k).start()

    def direct_done(stream):
        total = sum_piece(stream, z, 0)[...].astype(F32)
        index = streams.index(stream)
        pieces(stream, 3, sum_send.at[0, index], sum_recv.at[0, index, 0]).wait_recv()
        for k in (1, 2, 3):
            total += sum_in(0, stream, k)[...].astype(F32)
        sum_piece(stream, z, 0)[...] = total.astype(BF16)

    def sum_sent(stream):
        index = streams.index(stream)
        recvs = far_recv.at[1, index]
        if stream == ("o", 1):
            pieces(stream, 4, sum_send.at[0, index], recvs).wait_send()
        elif stream in direct:
            pieces(stream, 3, sum_send.at[0, index], recvs).wait_send()
        else:
            for zz in range(3):

                @pl.when(z == zz)
                def _():
                    pieces(stream, 3 - zz, sum_send.at[0, index], recvs).wait_send()

                @pl.when(z == zz + 1)
                def _():
                    pieces(stream, zz + 1, sum_send.at[1, index], recvs).wait_send()

        pieces(stream, 4, sum_send.at[2, index], recvs).wait_send()

    def core_piece(m, far, e):
        xx, rows = spot(last_x[m], e, far)
        return parts[m].at[:, xx, rows, half(c)]

    def scatter_core(m):
        for far in (1, 0):
            links.group(("gc", m, far), core_in.at[order[m], far])
            for e in (0, 1):
                xx, rows = spot(last_x_other[m], e, far)
                piece = parts[m].at[:, xx, rows, half(1 - c)]
                send(None, piece, core_in.at[order[m], far, e], core_dev, ("gc", m, far))

    def core_add(m, far, e):
        if e == 0:
            recv(("gc", m, far))
        target, other = core_piece(m, far, e), core_in.at[order[m], far, e]

        def step(zz, carry):
            target[zz] = (target[zz].astype(F32) + other[zz].astype(F32)).astype(BF16)
            return carry

        lax.fori_loop(0, 4, step, 0)

    def scatter_far(m):
        for e in (0, 1):
            core_add(m, 1, e)
        for e in (1, 0) if m == "o" else (0, 1):
            sum_far((m, e))
        for e in (0, 1):
            core_add(m, 0, e)

    def both(m, step):
        sum_step((m, 0), step)
        if m != "o":
            sum_step((m, 1), step)

    def scatter_last(m):
        send(("gl", m), sum_piece((m, 1), z, 0), last_in.at[order[m]], devs_of(last_x[m])[0])

    def scatter_sum(m):
        total = sum_piece((m, 0), z, 0)[...].astype(F32)
        if m != "o":
            recv(("gl", m))
            total += last_in[order[m]].astype(F32)
        outs[m][:, half(c)] = jnp.where(c == 0, total[:SHARE], total[SHARE:])
        give_out[order[m]] = jnp.where(c == 0, total[SHARE:], total[:SHARE])
        send(("give", m), give_out.at[order[m]], give_in.at[order[m]], core_dev)

    def scatter_done(m):
        recv(("give", m))
        outs[m][:, half(1 - c)] = give_in[order[m]]
        results.start(outs[m], outs_hbm[m])

    weight_grad("b", lambda j, right: dot_tn(active[:, tile(j, 256)], right))
    scatter_core("b")
    line_step(("b", 0), 3)
    line_step(("b", 1), 3)
    gather_side("b")
    scatter_far("b")
    gather_core("b")
    gather_done("b")

    def back_step(j, carry):
        cols = tile(j, 256)
        value = hidden[:, cols]
        sigma = jax.nn.sigmoid(value)
        grad = dot_nt(grad_y(), mats["b"][cols, :])
        grad_low[:, cols] = (grad * sigma * (1.0 + value * (1.0 - sigma))).astype(BF16)
        return carry

    lax.fori_loop(0, 5, back_step, 0)
    mix[...] = grad_low[...]

    def normed_step(j, carry):
        hidden[:, tile(j, 256)] = dot_nt(grad_low[...], mats["h"][tile(j, 256), :])
        return carry

    lax.fori_loop(0, 5, normed_step, 0)
    links.sent_of("h")
    line_sent(("h", 0))
    line_sent(("h", 1))
    weight_grad("h", lambda j, right: dot_tn(norm2[:, tile(j, 256)], right))
    scatter_core("h")
    both("b", 0)
    vec_part[...] = jnp.zeros_like(vec_part)

    def middle_back(step, carry):
        rows = tile(step, 64)
        value = middle[rows, :]
        inverse = rms_inverse(value)
        unit = value * inverse
        grad = hidden[rows, :]
        vec_part[4:5, :] += jnp.sum(grad * unit, axis=0, keepdims=True)
        scaled = grad * vec_row[4:5, :WIDTH]
        inside = (s * ROWS + step * 64 + lax.broadcasted_iota(jnp.int32, (64, 1), 0)) < len_ref[0]
        base = jnp.where(inside, cot_ref[rows, :].astype(F32), 0.0)
        total = base + inverse * (scaled - unit * jnp.mean(scaled * unit, axis=-1, keepdims=True))
        ig_ref[rows, :] = total
        grad_low[rows, :] = total.astype(BF16)
        return carry

    lax.fori_loop(0, ROWS // 64, middle_back, 0)

    mix_whole.wait_send()

    def mixed_back(member, carry):
        mix_out[member] = dot_nt(mats["o"][tile(member, MINE), :], grad_low[...]).astype(BF16)
        return carry

    lax.fori_loop(0, 4, mixed_back, 0)
    for p in range(2):
        rows = slice(PAIR * p, PAIR * (p + 1))
        links.group(("gm", p), gmix_in.at[pl.ds(0, 3), rows])
        for k, device in ((2, y_dev), (3, yc_dev), (1, core_dev)):
            send(None, mix_out.at[peers[k], rows], gmix_in.at[s, rows], device, ("gm", p))
    gmix_in[s] = mix_out[s]
    scatter_far("h")

    def out_step(j, carry):
        cols = tile(j, 256)
        value = middle[:, cols] + dot_nn(active[...], mats["b"][:, cols])
        out_ref[:, cols] = jnp.where(valid, value, 0.0).astype(BF16)
        return carry

    lax.fori_loop(0, 5, out_step, 0)
    results.start(out_ref, out_hbm)
    links.sent_of("b")
    line_sent(("b", 0))
    line_sent(("b", 1))
    mixed_flat = mix_in.reshape(WIDTH, ROWS)
    weight_grad("o", lambda j, right: dot_nn(mixed_flat[tile(j, 256), :], right))
    scatter_core("o")

    def attend_back(h):
        rows = slice(HEAD_DIM * h, HEAD_DIM * (h + 1))
        dk_acc[...] = jnp.zeros_like(dk_acc)
        dv_acc[...] = jnp.zeros_like(dv_acc)
        for i in range(4):
            low, high = i * ROWS, (i + 1) * ROWS
            query = queries_t[rows, low:high]
            grad = gmix_in[i, rows, :]
            log_total = lse[h, :, low:high]
            spans = [(0, low), (low, high)] if i else [(low, high)]
            held = []
            inner = jnp.zeros((1, ROWS), F32)
            for first, last in spans:
                scores = dot_nn(keys[h, first:last, :], query)
                if first == low:
                    scores = jnp.where(allowed, scores, masked_score)
                probs = jnp.exp(scores - log_total)
                grad_probs = dot_nn(vals[h, first:last, :], grad)
                inner += jnp.sum(probs * grad_probs, axis=0, keepdims=True)
                held.append((first, last, probs, grad_probs))
            grad_query = jnp.zeros((HEAD_DIM, ROWS), F32)
            for first, last, probs, grad_probs in held:
                grad_scores = (probs * (grad_probs - inner)).astype(BF16)
                grad_query += dot_nn(keys_t[rows, first:last], grad_scores)
                dk_acc[first:last, :] += dot_nt(grad_scores, query)
                dv_acc[first:last, :] += dot_nt(probs.astype(BF16), grad)
            dq_t[HEAD_DIM * (h % 2) : HEAD_DIM * (h % 2 + 1), low:high] = grad_query
        first = PAIR + HEAD_DIM * (h % 2)
        grads[h // 2, :, first : first + HEAD_DIM] = dk_acc[...].astype(BF16)
        grads[h // 2, :, first + PAIR : first + PAIR + HEAD_DIM] = dv_acc[...].astype(BF16)

    def finish_pair(p):
        lanes = slice(PAIR * p, PAIR * (p + 1))
        pair_scale = scale[:, lanes]
        bias_grad = jnp.zeros((1, PAIR), F32)
        scale_grad = jnp.zeros((1, PAIR), F32)
        value_grad = jnp.zeros((1, PAIR), F32)
        grads[p, :, 3 * PAIR :] = jnp.zeros((SLOTS, PACK - 3 * PAIR), BF16)
        for i in range(4):
            rows = slice(i * ROWS, (i + 1) * ROWS)
            grad = dq_t[:, rows].T
            low_grad = (grad * pair_scale).astype(BF16)
            grads[p, rows, 0:PAIR] = low_grad
            bias_grad += jnp.sum(low_grad.astype(F32), axis=0, keepdims=True)
            scale_grad += jnp.sum(grad * queries_n[p, i].astype(F32), axis=0, keepdims=True)
            value_grad += jnp.sum(grads[p, rows, 2 * PAIR : 3 * PAIR].astype(F32), axis=0, keepdims=True)
        scale_grad = scale_grad / pair_scale * jax.nn.sigmoid(query_log[:, lanes]) * factor
        return bias_grad, scale_grad, value_grad

    def qkv_grad_pair(p):
        flat = qkv_part.at[p].reshape(WIDTH, PACK)

        def qkv_grad(j, carry):
            total = jnp.zeros((256, PACK), F32)
            for i in range(4):
                total += dot_tn(tokens[i, :, tile(j, 256)], grads[p, i * ROWS : (i + 1) * ROWS, :])
            flat[tile(j, 256), :] = total.astype(BF16)
            return carry

        lax.fori_loop(0, 5, qkv_grad, 0)
        sum_far(p)

    def qkv_sum_pair(p):
        links.sent(("a2a", p))
        if p in direct:
            direct_done(p)
        total = qkv_part[p, z, x].astype(F32)
        for member in range(4):
            stage[p, member] = total[SHARE * member : SHARE * (member + 1), :].astype(BF16)
        links.group(("ph", p), qkv_home.at[p, pl.ds(0, 3)])
        for k, device in ((2, y_dev), (3, yc_dev), (1, core_dev)):
            send(None, stage.at[p, peers[k]], qkv_home.at[p, s], device, ("ph", p))
        qkv_home[p, s] = stage[p, s]

    both("b", 1)
    recv(("gm", 0))
    attend_back(0)
    scatter_far("o")
    both("b", 2)
    attend_back(1)
    pair_grads = [finish_pair(0)]
    qkv_grad_pair(0)
    both("b", 3)
    scatter_last("b")
    both("h", 0)
    recv(("gm", 1))
    attend_back(2)
    attend_back(3)
    pair_grads.append(finish_pair(1))
    both("h", 1)
    qkv_grad_pair(1)
    both("h", 2)
    for row in range(3):
        value = jnp.concatenate([pair_grads[0][row], pair_grads[1][row]], axis=1)
        vec_part[row + 1 : row + 2, :] = jnp.concatenate(
            [jnp.where(s == member, value, 0.0) for member in range(4)], axis=1
        )

    def unit_rows(member):
        def unit_grad(j, carry):
            cols = tile(j, 256)
            value = dot_nt(grads[0, tile(member, ROWS), :], weights[0][cols, :])
            value += dot_nt(grads[1, tile(member, ROWS), :], weights[1][cols, :])
            tokens[member, :, cols] = value.astype(BF16)
            return carry

        lax.fori_loop(0, 5, unit_grad, 0)

    unit_rows((1 - y) * 2 + (1 - c))
    send(("uc", 1), tokens.at[(1 - y) * 2 + (1 - c)], unit_core.at[1], core_dev)
    far_member = (1 - y) * 2 + c
    sum_step(0, 0)
    unit_rows(far_member)
    recv(("uc", 1))
    tokens[far_member] = (tokens[far_member].astype(F32) + unit_core[1].astype(F32)).astype(BF16)
    send("uy", tokens.at[far_member], unit_far, y_dev)
    both("h", 3)
    scatter_last("h")
    sum_step(0, 1)
    unit_rows(y * 2 + (1 - c))
    send(("uc", 0), tokens.at[y * 2 + (1 - c)], unit_core.at[0], core_dev)
    cross()
    unit_rows(s)
    recv(("uc", 0))
    sum_step(0, 2)
    direct_start(1)
    sum_step(0, 3)
    qkv_sum_pair(0)
    direct_start(("o", 0))
    recv("uy")

    def unpack(p):
        recv(("ph", p))
        for index, ref in enumerate((gq_ref, gk_ref, gv_ref)):
            for member in range(4):
                first = MINE * member + PAIR * p
                ref[:, first : first + PAIR] = qkv_home[
                    p, member, :, PAIR * index : PAIR * (index + 1)
                ].astype(F32)

    def input_back(step, carry):
        rows = tile(step, 64)
        value = x_ref[rows, :].astype(F32)
        inverse = rms_inverse(value)
        unit = value * inverse
        grad = (
            tokens[s, rows, :].astype(F32) + unit_core[0, rows, :].astype(F32) + unit_far[rows, :].astype(F32)
        )
        vec_part[0:1, :] += jnp.sum(grad * unit, axis=0, keepdims=True)
        scaled = grad * vec_row[0:1, :WIDTH]
        ig_ref[rows, :] += inverse * (scaled - unit * jnp.mean(scaled * unit, axis=-1, keepdims=True))
        return carry

    lax.fori_loop(0, ROWS // 64, input_back, 0)
    results.start(ig_ref, ig_hbm)
    links.group("sg", vec_in.at[pl.ds(0, 3)])
    for k, device in ((2, y_dev), (3, yc_dev), (1, core_dev)):
        send(None, vec_part, vec_in.at[k - 1], device, "sg")
    scatter_sum("b")
    scatter_sum("h")
    recv("sg")
    links.sent("sg")
    vec_part[...] += vec_in[0] + vec_in[1] + vec_in[2]
    send("sx", vec_part, vec_in.at[3], x_dev)
    recv("sx")
    links.sent("sx")
    vec_part[...] += vec_in[3]
    links.group("sz", vec_in.at[pl.ds(4, 3)])
    for k in (1, 2, 3):
        send(None, vec_part, vec_in.at[3 + k], z_devs[k], "sz")
    scatter_done("b")
    scatter_done("h")
    qkv_sum_pair(1)
    direct_done(("o", 0))
    scatter_sum("o")
    unpack(0)
    recv("sz")
    total = vec_part[...] + vec_in[4] + vec_in[5] + vec_in[6]
    gvec_ref[...] = pltpu.roll(total, WIDTH - (d * 4 + s) * SHARE, 1)[:, :128]
    results.start(gvec_ref, gvec_hbm)
    scatter_done("o")
    unpack(1)
    for held, target in ((gq_ref, gq_hbm), (gk_ref, gk_hbm), (gv_ref, gv_hbm)):
        results.start(held, target)
    results.wait()
    links.sent_all()
    line_sent(("o", 0))
    line_sent(("o", 1))
    for stream in streams:
        sum_sent(stream)
    line_sent(0)
    line_sent(1)


def finish_kernel(*refs):
    sources, gvec, targets, held = refs[:8], refs[8], refs[9:22], refs[22:30]
    vectors, sems = refs[30:35], refs[35]
    places = (1, 0, 3, 6, 7, 9, 11, 12)
    rows = (2, 4, 5, 8, 10)
    loads = [pltpu.make_async_copy(sources[i], held[i], sems.at[0, i]) for i in range(8)]
    stores = [pltpu.make_async_copy(held[i], targets[places[i]], sems.at[1, i]) for i in range(8)]
    small = [pltpu.make_async_copy(vectors[i], targets[rows[i]], sems.at[1, 8 + i]) for i in range(5)]
    for copy in loads:
        copy.start()
    for row in range(5):
        vectors[row][...] = gvec[row, :SHARE]
        small[row].start()
    for load, store in zip(loads, stores):
        load.wait()
        store.start()
    for copy in stores + small:
        copy.wait()


def fused_shards(
    inputs,
    lengths,
    cotangent,
    gain_attn,
    w_query,
    bias_query,
    query_scale,
    w_key,
    w_value,
    bias_value,
    w_out,
    gain_mlp,
    w_hidden,
    w_back,
):
    vectors = [v.reshape(1, SHARE) for v in (gain_attn, bias_query, query_scale, bias_value, gain_mlp)]
    vmem = pl.BlockSpec(memory_space=pltpu.VMEM)
    whole = (4, 2, 4 * SHARE, WIDTH)
    buffers = [
        ((ROWS, WIDTH), BF16),
        ((ROWS, WIDTH), F32),
        ((8, 128), F32),
        ((8, 128), F32),
    ]
    buffers += [((SHARE, WIDTH), F32)] * 6
    buffers += [
        (whole, BF16),
        (whole, BF16),
        (whole, BF16),
        (whole, BF16),
        ((3, 2, 2, 4, 2 * SHARE, WIDTH // 2), BF16),
        ((6, 4, 2 * SHARE, WIDTH // 2), BF16),
        ((2, 6, 3, 2 * SHARE, WIDTH // 2), BF16),
        ((3, 2 * SHARE, WIDTH // 2), BF16),
        ((2, 8, 4 * SHARE, PACK), BF16),
        ((2, 4, SHARE, PACK), BF16),
        ((4, ROWS, WIDTH), BF16),
        ((4, SLOTS, HEAD_DIM), BF16),
        ((4, SLOTS, HEAD_DIM), BF16),
        ((MINE, SLOTS), BF16),
        ((MINE, SLOTS), BF16),
        ((MINE, SLOTS), BF16),
        ((2, 4, ROWS, PAIR), BF16),
        ((4, 1, SLOTS), F32),
        ((4, MINE, ROWS), BF16),
        ((4, MINE, ROWS), BF16),
        ((ROWS, WIDTH), BF16),
        ((ROWS, WIDTH), F32),
        ((ROWS, WIDTH), F32),
        ((ROWS, WIDTH), BF16),
        ((ROWS, WIDTH), BF16),
        ((4, MINE, ROWS), BF16),
        ((ROWS, WIDTH), BF16),
        ((SLOTS, HEAD_DIM), F32),
        ((SLOTS, HEAD_DIM), F32),
        ((PAIR, SLOTS), F32),
        ((2, SLOTS, PACK), BF16),
        ((2, ROWS, WIDTH), BF16),
        ((ROWS, WIDTH), BF16),
        ((2, 4, 2, 4 * SHARE, PACK), BF16),
        ((2, 4, 4 * SHARE, PACK), BF16),
        ((2, 2, 3, 4 * SHARE, PACK), BF16),
        ((2, 4, SHARE, PACK), BF16),
        ((2, 2, 4, 2, 8, 128), F32),
        ((8, WIDTH + 128), F32),
        ((8, WIDTH), F32),
        ((7, 8, WIDTH), F32),
        ((2, 4, SHARE, PACK), BF16),
        ((3, 2, SHARE, WIDTH // 2), BF16),
        ((3, SHARE, WIDTH // 2), F32),
        ((3, SHARE, WIDTH // 2), F32),
    ]
    scratch = [pltpu.VMEM(shape, kind) for shape, kind in buffers]
    scratch += [pltpu.SemaphoreType.DMA((9,))]
    dma = pltpu.SemaphoreType.DMA
    scratch += [dma, dma] + [dma((3, 8)), dma((2, 8, 3))] * 2 + [dma((2, 8))]
    scratch += [dma((COPIES,))] * 2
    square = jax.ShapeDtypeStruct((SHARE, WIDTH), F32)
    results = pl.pallas_call(
        layer_kernel,
        out_shape=(
            jax.ShapeDtypeStruct((ROWS, WIDTH), BF16),
            jax.ShapeDtypeStruct((ROWS, WIDTH), F32),
            jax.ShapeDtypeStruct((8, 128), F32),
            square,
            square,
            square,
            square,
            square,
            square,
        ),
        in_specs=[vmem, pl.BlockSpec(memory_space=pltpu.SMEM)] + [vmem] * 12,
        out_specs=tuple([pl.BlockSpec(memory_space=pl.ANY)] * 9),
        scratch_shapes=scratch,
        compiler_params=pltpu.CompilerParams(
            collective_id=0, has_side_effects=True, vmem_limit_bytes=66 * 1000 * 1000
        ),
        cost_estimate=pl.CostEstimate(flops=25_000_000_000, bytes_accessed=10_000_000, transcendentals=10_000_000),
    )(
        inputs.reshape(ROWS, WIDTH),
        lengths,
        cotangent.reshape(ROWS, WIDTH),
        *vectors,
        w_query,
        w_key,
        w_value,
        w_out,
        w_hidden,
        w_back,
    )
    out, input_grad, gvec, gq, gk, gv, go, gh, gb = results
    moved = (input_grad, out, gq, gk, gv, go, gh, gb)
    anywhere = pl.BlockSpec(memory_space=pl.ANY)
    vector = jax.ShapeDtypeStruct((SHARE,), F32)
    shapes = [jax.ShapeDtypeStruct((ROWS, WIDTH), BF16), jax.ShapeDtypeStruct((ROWS, WIDTH), F32), vector, square]
    shapes += [vector, vector, square, square, vector, square, vector, square, square]
    done = pl.pallas_call(
        finish_kernel,
        out_shape=tuple(shapes),
        in_specs=[anywhere] * 8 + [vmem],
        out_specs=tuple([anywhere] * 13),
        scratch_shapes=[pltpu.VMEM(array.shape, array.dtype) for array in moved]
        + [pltpu.VMEM((SHARE,), F32)] * 5
        + [pltpu.SemaphoreType.DMA((2, 13))],
        compiler_params=pltpu.CompilerParams(vmem_limit_bytes=66 * 1000 * 1000),
    )(*moved, gvec)
    return (done[0].reshape(inputs.shape), done[1].reshape(inputs.shape), *done[2:])


def solution(mesh):
    placed = (
        P("dp", "seq", None),
        P("dp"),
        P("dp", "seq", None),
        P(("dp", "seq")),
        P(("dp", "seq"), None),
        P(("dp", "seq")),
        P(("dp", "seq")),
        P(("dp", "seq"), None),
        P(("dp", "seq"), None),
        P(("dp", "seq")),
        P(("dp", "seq"), None),
        P(("dp", "seq")),
        P(("dp", "seq"), None),
        P(("dp", "seq"), None),
    )
    return jax.shard_map(
        fused_shards if fits(mesh) else shards,
        mesh=mesh,
        in_specs=placed,
        out_specs=(
            P("dp", "seq", None),
            P("dp", "seq", None),
            P(("dp", "seq")),
            P(("dp", "seq"), None),
            P(("dp", "seq")),
            P(("dp", "seq")),
            P(("dp", "seq"), None),
            P(("dp", "seq"), None),
            P(("dp", "seq")),
            P(("dp", "seq"), None),
            P(("dp", "seq")),
            P(("dp", "seq"), None),
            P(("dp", "seq"), None),
        ),
        check_vma=False,
    )
```
